32 devices in a mesh: rep: 8 (over z, y), tp: 4 (over x, core).
Axes of the slice: x: 2, y: 2, z: 4, core: 2. Of those that a mesh axis runs over, the one named last changes fastest.
Arguments:
- grads: bfloat16 [8, 12, 768, 2048], P('rep', None, None, 'tp'), may hold values from -6 to 6
- error: float32 [8, 12, 768, 2048], P('rep', None, None, 'tp'), may hold values from -2 to 2
- query: float32 [12, 32, 2048], P(None, None, 'tp'), may hold values from -6 to 6
- momentum: float32 [9216, 2048], P(('rep', 'tp')), may hold values from -0.8 to 0.8
- master: float32 [9216, 2048], P(('rep', 'tp')), may hold values from -0.8 to 0.8
Outputs:
- new_error: float32 [8, 12, 768, 2048], P('rep', None, None, 'tp')
- new_query: float32 [12, 32, 2048], P(None, None, 'tp')
- new_momentum: float32 [9216, 2048], P(('rep', 'tp'))
- new_master: float32 [9216, 2048], P(('rep', 'tp'))
- weights: bfloat16 [12, 768, 2048], P(None, None, 'tp')
The draws below stay inside these ranges and needn't reach their ends.
All inputs are finite; a program needn't handle non-finite values.
Results may differ from the reference program's by a relative error of at most 0.0004.
Values may be sent and summed in bfloat16 or wider, within the bound.
No kernel may reach another device: no remote copies, remote signals or barrier semaphores. Data moves between devices by JAX's collectives and lax.ppermute only.
A program may use at most 128 MiB of HBM per device.

```python
import jax
import jax.numpy as jnp
from jax import lax

D = 768
FF = 2048
RANK = 32
ROUNDS = 2
NS_STEPS = 5
MATS = 12
REPLICAS = 8
N_REP = 8


def block_levels(rng, dims, shards, low, top_value):
    factor_of, own = 1.0, jax.random.fold_in(rng, 6)
    for dim, blocks in shards:
        heights = jnp.exp(jax.random.uniform(jax.random.fold_in(own, dim), (blocks,), jnp.float32, low / len(shards), top_value / len(shards)))
        factor_of = factor_of * jnp.repeat(heights, dims[dim] // blocks).reshape([-1 if axis == dim else 1 for axis in range(len(dims))])
    return factor_of


def noise(stream_key, shape, deviation, reach, pieces=(), dtype=jnp.bfloat16):
    values = deviation * jax.random.normal(stream_key, shape, jnp.float32)
    if pieces:
        values = values * block_levels(stream_key, shape, pieces, -0.22, 0.18)
    return jnp.clip(values, -reach, reach).astype(dtype)


def setup_inputs(seed: int = 0) -> dict:
    streams_of = jax.random.split(jax.random.key(seed), 6)
    return {
        "grads": noise(streams_of[0], (REPLICAS, MATS, D, FF), 1.0, 6.0, ((0, 8), (3, 4))),
        "error": noise(streams_of[1], (REPLICAS, MATS, D, FF), 0.3, 2.0, ((0, 8), (3, 4)), jnp.float32),
        "query": noise(streams_of[2], (MATS, RANK, FF), 1.0, 6.0, ((2, 4),), jnp.float32),
        "momentum": noise(streams_of[3], (MATS * D, FF), 0.2, 0.8, ((0, 32),), jnp.float32),
        "master": noise(streams_of[4], (MATS * D, FF), 0.2, 0.8, ((0, 32),), jnp.float32),
    }


NORM_EPSILON = 1e-06
MOMENTUM_DECAY = 0.9
LEARNING_RATE = 0.5

def gram_matrix(factor):
    return jnp.einsum('krd,ksd->krs', factor, factor, precision=lax.Precision.HIGHEST)

def orthonormal(factor):
    gram_now = gram_matrix(factor)
    sum_squares = jnp.trace(gram_now, axis1=1, axis2=2)[:, None, None]
    factor_scale = lax.rsqrt(sum_squares + NORM_EPSILON)
    ortho_basis = factor * factor_scale
    gram_now = gram_now * (factor_scale * factor_scale)
    for iteration in range(NS_STEPS):
        if iteration > 0:
            gram_now = gram_matrix(ortho_basis)
        ortho_basis = 1.5 * ortho_basis - 0.5 * jnp.einsum('krs,ksd->krd', gram_now, ortho_basis, precision=lax.Precision.HIGHEST)
    return ortho_basis

def reference(grads, error, query, momentum, master):
    corrected = grads.astype(jnp.float32) + error
    current = query
    for power_pass in range(ROUNDS):
        summed = jnp.einsum('nkdf,krf->krd', corrected, current, precision=lax.Precision.HIGHEST)
        ortho_basis = orthonormal(summed)
        current = jnp.einsum('nkdf,krd->krf', corrected, ortho_basis, precision=lax.Precision.HIGHEST) / N_REP
    approx = jnp.einsum('krd,krf->kdf', ortho_basis, current, precision=lax.Precision.HIGHEST)
    new_error = corrected - approx[None]
    flat_approx = approx.reshape(MATS * D, FF)
    new_momentum = MOMENTUM_DECAY * momentum + flat_approx
    new_master = master - LEARNING_RATE * new_momentum
    weights = new_master.astype(jnp.bfloat16).reshape(MATS, D, FF)
    return (new_error, current, new_momentum, new_master, weights)
```

```python
import math

import jax
import jax.numpy as jnp
from jax import lax
from jax.sharding import PartitionSpec as P

ROUNDS = 2
NS_STEPS = 5


NORM_EPSILON = 1e-06
MOMENTUM_DECAY = 0.9
LEARNING_RATE = 0.5
HIGHEST = lax.Precision.HIGHEST


def share(block, axes, count):
    spread = jnp.broadcast_to(block[None], (count, *block.shape))
    return lax.all_to_all(spread, axes, split_axis=0, concat_axis=0, tiled=True)


def total(parts, axes, count):
    mine = lax.all_to_all(parts, axes, split_axis=0, concat_axis=0, tiled=True)
    return share(jnp.sum(mine, axis=0), axes, count)


def orthonormal(factor):
    gram_now = jnp.einsum("krd,ksd->krs", factor, factor, precision=HIGHEST)
    sum_squares = jnp.trace(gram_now, axis1=1, axis2=2)[:, None, None]
    scale = lax.rsqrt(sum_squares + NORM_EPSILON)
    gram_now = gram_now * (scale * scale)
    eye = jnp.eye(factor.shape[1], dtype=jnp.float32)
    mixed = scale * eye
    for iteration in range(NS_STEPS):
        step = 1.5 * eye - 0.5 * gram_now
        mixed = jnp.einsum("krs,kst->krt", step, mixed, precision=HIGHEST)
        if iteration + 1 < NS_STEPS:
            half = jnp.einsum("krs,kst->krt", step, gram_now, precision=HIGHEST)
            gram_now = jnp.einsum("krs,kst->krt", half, step, precision=HIGHEST)
    return jnp.einsum("krs,ksd->krd", mixed, factor, precision=HIGHEST)


def local(grads, error, query, momentum, master):
    replicas, tps = lax.axis_size("rep"), lax.axis_size("tp")
    rep, tp = lax.axis_index("rep"), lax.axis_index("tp")
    corrected = grads[0].astype(jnp.float32) + error[0]
    matrices, width, shard_cols = corrected.shape
    rank = query.shape[1]
    devices = replicas * tps
    lanes = 128
    current = query
    for power_pass in range(ROUNDS):
        partial_factor = jnp.einsum("kdf,krf->krd", corrected, current, precision=HIGHEST)
        parts = partial_factor.reshape(matrices * rank, width // lanes, lanes)
        parts = parts.transpose(1, 0, 2).reshape(devices, -1, lanes)
        summed = total(parts, ("rep", "tp"), devices)
        summed = summed.reshape(width // lanes, matrices * rank, lanes).transpose(1, 0, 2)
        ortho_basis = orthonormal(summed.reshape(matrices, rank, width))
        partial_query = jnp.einsum("kdf,krd->krf", corrected, ortho_basis, precision=HIGHEST)
        summed = total(partial_query.reshape(replicas, -1, shard_cols), "rep", replicas)
        current = summed.reshape(matrices, rank, shard_cols) / replicas
    approx = jnp.einsum("krd,krf->kdf", ortho_basis, current, precision=HIGHEST)
    new_error = (corrected - approx)[None]
    rep_rows = matrices * width // replicas
    own_rows = rep_rows // tps
    spans = -(-(width - math.gcd(width, rep_rows) + rep_rows) // width)
    first = jnp.minimum(rep * rep_rows // width, matrices - spans)
    near = lax.dynamic_slice_in_dim(current, first, spans, 0)
    near = share(near, "tp", tps).transpose(1, 2, 0, 3).reshape(spans * rank, -1)
    near_basis = lax.dynamic_slice_in_dim(ortho_basis, first, spans, 0)
    row_factors = near_basis.transpose(0, 2, 1)[:, :, None, :] * jnp.eye(spans, dtype=jnp.float32)[:, None, :, None]
    row_factors = row_factors.reshape(spans * width, spans * rank)
    start = rep * rep_rows + tp * own_rows - first * width
    row_factors = lax.dynamic_slice_in_dim(row_factors, start, own_rows, 0)
    flat_approx = jnp.dot(row_factors, near, precision=HIGHEST)
    new_momentum = MOMENTUM_DECAY * momentum + flat_approx
    new_master = master - LEARNING_RATE * new_momentum
    working = new_master.astype(jnp.bfloat16)
    by_columns = lax.all_to_all(working, "tp", split_axis=1, concat_axis=0, tiled=True)
    weight_rows = lax.all_gather(by_columns, "rep", axis=0, tiled=True)
    weights = weight_rows.reshape(matrices, width, shard_cols)
    return (new_error, current, new_momentum, new_master, weights)


def solution(mesh):
    placed = (
        P("rep", None, None, "tp"),
        P("rep", None, None, "tp"),
        P(None, None, "tp"),
        P(("rep", "tp"), None),
        P(("rep", "tp"), None),
    )
    return jax.shard_map(
        local,
        mesh=mesh,
        in_specs=placed,
        out_specs=(
            P("rep", None, None, "tp"),
            P(None, None, "tp"),
            P(("rep", "tp"), None),
            P(("rep", "tp"), None),
            P(None, None, "tp"),
        ),
        check_vma=False,
    )
```

```python
import functools
import math

import jax
import jax.numpy as jnp
from jax import lax
from jax.experimental import pallas as pl
from jax.experimental.pallas import tpu as pltpu
from jax.sharding import PartitionSpec as P

ROUNDS = 2
NS_STEPS = 5


NORM_EPSILON = 1e-06
MOMENTUM_DECAY = 0.9
LEARNING_RATE = 0.5
HIGHEST = lax.Precision.HIGHEST
LANES = 128
GROUPS = 3
F32, BF16 = jnp.float32, jnp.bfloat16
PARAMS = pltpu.CompilerParams(vmem_limit_bytes=40 * 2**20)


def two_terms(x):
    high = x.astype(BF16)
    return high, (x - high.astype(F32)).astype(BF16)


def dot(a, b, transposed=False):
    dims = (((1,), (1 if transposed else 0,)), ((), ()))
    return lax.dot_general(a, b, dims, preferred_element_type=F32)


def small_by_large(small, high, low, transposed):
    rows = small.shape[0]
    small_high, small_low = two_terms(small)
    both = dot(jnp.concatenate([small_high, small_low], axis=0), high, transposed)
    return both[:rows] + both[rows:] + dot(small_high, low, transposed)


def dot3(a, b):
    a_high, a_low = two_terms(a)
    b_high, b_low = two_terms(b)
    return dot(
        jnp.concatenate([a_high, a_low, a_high], axis=1),
        jnp.concatenate([b_high, b_high, b_low], axis=0),
    )


def put_left(left_ref, left):
    for block in range(left_ref.shape[0]):
        left_ref[block] = left[:, block * LANES : (block + 1) * LANES]


def first_left_kernel(grads_ref, error_ref, query_ref, high_ref, low_ref, left_ref):
    high, low = two_terms(grads_ref[0, 0].astype(F32) + error_ref[0, 0])
    high_ref[0] = high
    low_ref[0] = low
    put_left(left_ref, small_by_large(query_ref[0], high, low, True))


def left_kernel(high_ref, low_ref, current_ref, left_ref):
    put_left(left_ref, small_by_large(current_ref[...], high_ref[0], low_ref[0], True))


def mixing(left, rank):
    rows = left.shape[0]
    row_id = lax.broadcasted_iota(jnp.int32, (rows, rows), 0)
    col_id = lax.broadcasted_iota(jnp.int32, (rows, rows), 1)
    same = (row_id // rank) == (col_id // rank)
    eye = (row_id == col_id).astype(F32)
    left_high, left_low = two_terms(left)
    cross = dot(left_high, left_low, True)
    gram = jnp.where(same, dot(left_high, left_high, True) + cross + cross.T, 0.0)
    diagonal = jnp.sum(gram * eye, axis=0, keepdims=True)
    trace = jnp.sum(jnp.where(same, diagonal, 0.0), axis=1, keepdims=True) + NORM_EPSILON
    scale = lax.rsqrt(trace)
    scale = scale * (1.5 - 0.5 * trace * scale * scale)
    gram = gram * (scale * scale)
    step = 1.5 * eye - 0.5 * gram
    mixed = step * scale
    for _ in range(NS_STEPS - 1):
        gram = dot3(dot3(step, gram), step)
        step = 1.5 * eye - 0.5 * gram
        mixed = dot3(step, mixed)
    return mixed


def right_kernel(rank, last, left_ref, high_ref, low_ref, right_ref, *rest):
    basis = rest[-1]
    matrix = pl.program_id(0)

    @pl.when(matrix == 0)
    def _():
        left = jnp.concatenate([left_ref[block] for block in range(left_ref.shape[0])], axis=1)
        basis[...] = dot3(mixing(left, rank), left)

    own = basis[pl.ds(pl.multiple_of(matrix * rank, rank), rank), :]
    right_ref[...] = small_by_large(own, high_ref[0], low_ref[0], False)
    if last:
        own_high, own_low = two_terms(own.T)
        rest[0][...] = jnp.concatenate([own_high, own_low, own_high], axis=1)


def sum_kernel(scale, parts_ref, out_ref):
    summed = parts_ref[0]
    for part in range(1, parts_ref.shape[0]):
        summed = summed + parts_ref[part]
    if scale != 1.0:
        summed = summed * scale
    for part in range(parts_ref.shape[0]):
        out_ref[part] = summed


def total(parts, axes, scale=1.0):
    mine = lax.all_to_all(parts, axes, split_axis=0, concat_axis=0, tiled=True)
    spread = pl.pallas_call(
        functools.partial(sum_kernel, scale),
        out_shape=jax.ShapeDtypeStruct(parts.shape, parts.dtype),
        compiler_params=PARAMS,
        name="sum_parts",
        cost_estimate=pl.CostEstimate(flops=parts.size, bytes_accessed=8 * parts.size, transcendentals=0),
    )(mine)
    return lax.all_to_all(spread, axes, split_axis=0, concat_axis=0, tiled=True)


def stacked(right):
    right_high, right_low = two_terms(right)
    return jnp.concatenate([right_high, right_high, right_low], axis=0)


def weight_kernel(_, factors_ref, right_ref, base_ref, weights_ref):
    approx = dot(factors_ref[...], stacked(right_ref[...]))
    weights_ref[...] = (base_ref[...] - LEARNING_RATE * approx).astype(BF16)


def error_kernel(groups, per_group, *refs):
    new_error_ref = refs[-1]
    matrix = pl.program_id(0)
    for group in range(groups):
        high_ref, low_ref, factors_ref, right_ref = refs[4 * group : 4 * group + 4]

        @pl.when(matrix // per_group == group)
        def _():
            approx = dot(factors_ref[...], stacked(right_ref[...]))
            new_error_ref[0, 0] = high_ref[0].astype(F32) + low_ref[0].astype(F32) - approx


def gather_blocks(block, replicas):
    ring = [(rep, (rep + 2) % replicas) for rep in range(replicas)]
    pair = [(rep, rep ^ 1) for rep in range(replicas)]
    rep = lax.axis_index("rep")
    held = [(block, rep)]
    for step in range(1, replicas // 2):
        block = lax.ppermute(block, "rep", ring)
        held.append((block, (rep - 2 * step) % replicas))
    crossed = [(lax.ppermute(one, "rep", pair), owner ^ 1) for one, owner in held]
    return held + crossed


def local(grads, error, query, momentum, master):
    replicas, tps = lax.axis_size("rep"), lax.axis_size("tp")
    rep, tp = lax.axis_index("rep"), lax.axis_index("tp")
    _, matrices, width, cols = grads.shape
    rank = query.shape[1]
    devices = replicas * tps
    per_group = matrices // GROUPS
    group_rows = per_group * rank
    blocks = width // LANES
    flops = 2 * 3 * per_group * rank * width * cols
    elements = per_group * width * cols

    one_matrix = pl.BlockSpec((1, width, cols), lambda k: (k, 0, 0))
    left_spec = pl.BlockSpec((blocks, rank, LANES), lambda k: (0, k, 0))
    right_spec = pl.BlockSpec((rank, cols), lambda k: (k, 0))
    left_shape = jax.ShapeDtypeStruct((blocks, group_rows, LANES), F32)
    right_shape = jax.ShapeDtypeStruct((group_rows, cols), F32)
    term_shape = jax.ShapeDtypeStruct((per_group, width, cols), BF16)

    def total_left(left):
        return total(left.reshape(devices, -1, LANES), ("rep", "tp")).reshape(blocks, group_rows, LANES)

    def total_right(right):
        return total(right.reshape(replicas, -1, cols), "rep", 1.0 / replicas).reshape(group_rows, cols)

    own_rows = momentum.shape[0]
    base = master - (LEARNING_RATE * MOMENTUM_DECAY) * momentum
    base = lax.all_to_all(base.reshape(own_rows, tps, cols).transpose(1, 0, 2), "tp", split_axis=0, concat_axis=0, tiled=True)
    rep_rows = tps * own_rows
    base = base.reshape(rep_rows, cols)

    terms, lefts = [], []
    for group in range(GROUPS):
        picked = functools.partial(lambda group, k: (0, group * per_group + k, 0, 0), group)
        high, low, left = pl.pallas_call(
            first_left_kernel,
            grid=(per_group,),
            in_specs=[
                pl.BlockSpec((1, 1, width, cols), picked),
                pl.BlockSpec((1, 1, width, cols), picked),
                pl.BlockSpec((1, rank, cols), functools.partial(lambda group, k: (group * per_group + k, 0, 0), group)),
            ],
            out_specs=[one_matrix, one_matrix, left_spec],
            out_shape=[term_shape, term_shape, left_shape],
            compiler_params=PARAMS,
            name="first_left",
            cost_estimate=pl.CostEstimate(flops=flops, bytes_accessed=10 * elements, transcendentals=0),
        )(grads, error, query)
        terms.append((high, low))
        lefts.append(left)

    factors = [None] * GROUPS
    for power_pass in range(ROUNDS):
        last = power_pass == ROUNDS - 1
        lefts = [total_left(left) for left in lefts]
        rights = []
        for group in range(GROUPS):
            out_shape, out_specs = [right_shape], [right_spec]
            if last:
                out_shape.append(jax.ShapeDtypeStruct((per_group * width, 3 * rank), BF16))
                out_specs.append(pl.BlockSpec((width, 3 * rank), lambda k: (k, 0)))
            outs = pl.pallas_call(
                functools.partial(right_kernel, rank, last),
                grid=(per_group,),
                in_specs=[pl.BlockSpec((blocks, group_rows, LANES), lambda k: (0, 0, 0)), one_matrix, one_matrix],
                out_specs=out_specs,
                out_shape=out_shape,
                scratch_shapes=[pltpu.VMEM((group_rows, width), F32)],
                compiler_params=PARAMS,
                name="right",
                cost_estimate=pl.CostEstimate(flops=flops, bytes_accessed=4 * elements, transcendentals=0),
            )(lefts[group], *terms[group])
            rights.append(outs[0])
            if last:
                factors[group] = outs[1]
        rights = [total_right(right) for right in rights]
        if not last:
            lefts = [
                pl.pallas_call(
                    left_kernel,
                    grid=(per_group,),
                    in_specs=[one_matrix, one_matrix, right_spec],
                    out_specs=left_spec,
                    out_shape=left_shape,
                    compiler_params=PARAMS,
                    name="left",
                    cost_estimate=pl.CostEstimate(flops=flops, bytes_accessed=4 * elements, transcendentals=0),
                )(*terms[group], rights[group])
                for group in range(GROUPS)
            ]
    all_right = jnp.concatenate(rights, axis=0)
    all_factors = jnp.concatenate(factors, axis=0)
    current = all_right.reshape(matrices, rank, cols)

    chunk = math.gcd(rep_rows, width)
    chunks = rep_rows // chunk
    block = pl.pallas_call(
        weight_kernel,
        grid_spec=pltpu.PrefetchScalarGridSpec(
            num_scalar_prefetch=1,
            grid=(chunks,),
            in_specs=[
                pl.BlockSpec((chunk, 3 * rank), lambda b, at: (at[0] * chunks + b, 0)),
                pl.BlockSpec((rank, cols), lambda b, at: ((at[0] * chunks + b) * chunk // width, 0)),
                pl.BlockSpec((chunk, cols), lambda b, at: (b, 0)),
            ],
            out_specs=pl.BlockSpec((chunk, cols), lambda b, at: (b, 0)),
        ),
        out_shape=jax.ShapeDtypeStruct((rep_rows, cols), BF16),
        compiler_params=PARAMS,
        name="weight_block",
    )(rep[None], all_factors, all_right, base)
    weights = jnp.zeros((replicas, rep_rows, cols), BF16)
    for one, owner in gather_blocks(block, replicas):
        weights = lax.dynamic_update_slice(weights, one[None], (owner, 0, 0))
    weights = weights.reshape(matrices, width, cols)

    operands, specs = [], []
    for group in range(GROUPS):
        picked = functools.partial(lambda group, k: jnp.clip(k - group * per_group, 0, per_group - 1), group)
        operands += [*terms[group], factors[group], rights[group]]
        specs += [
            pl.BlockSpec((1, width, cols), functools.partial(lambda at, k: (at(k), 0, 0), picked)),
            pl.BlockSpec((1, width, cols), functools.partial(lambda at, k: (at(k), 0, 0), picked)),
            pl.BlockSpec((width, 3 * rank), functools.partial(lambda at, k: (at(k), 0), picked)),
            pl.BlockSpec((rank, cols), functools.partial(lambda at, k: (at(k), 0), picked)),
        ]
    new_error = pl.pallas_call(
        functools.partial(error_kernel, GROUPS, per_group),
        grid=(matrices,),
        in_specs=specs,
        out_specs=pl.BlockSpec((1, 1, width, cols), lambda k: (0, k, 0, 0)),
        out_shape=jax.ShapeDtypeStruct(error.shape, F32),
        compiler_params=PARAMS,
        name="new_error",
        cost_estimate=pl.CostEstimate(flops=2 * 3 * rank * error.size, bytes_accessed=8 * error.size, transcendentals=0),
    )(*operands)

    spans = -(-(width - chunk + rep_rows) // width)
    first = jnp.minimum(rep * rep_rows // width, matrices - spans)
    near = lax.dynamic_slice_in_dim(current, first, spans, 0)
    near = jnp.broadcast_to(near[None], (tps, *near.shape))
    near = lax.all_to_all(near, "tp", split_axis=0, concat_axis=0, tiled=True)
    near = near.transpose(1, 2, 0, 3).reshape(spans * rank, -1)
    start = rep * rep_rows + tp * own_rows
    own_factors = lax.dynamic_slice_in_dim(all_factors, start, own_rows, 0).astype(F32)
    own_factors = own_factors[:, :rank] + own_factors[:, rank : 2 * rank]
    span_of = (start + jnp.arange(own_rows)) // width - first
    chosen = (span_of[:, None] == jnp.arange(spans)[None]).astype(F32)
    own_factors = (chosen[:, :, None] * own_factors[:, None, :]).reshape(own_rows, spans * rank)
    flat_approx = jnp.dot(own_factors, near, precision=HIGHEST)
    new_momentum = MOMENTUM_DECAY * momentum + flat_approx
    new_master = master - LEARNING_RATE * new_momentum
    return (new_error, current, new_momentum, new_master, weights)


def solution(mesh):
    placed = (
        P("rep", None, None, "tp"),
        P("rep", None, None, "tp"),
        P(None, None, "tp"),
        P(("rep", "tp"), None),
        P(("rep", "tp"), None),
    )
    return jax.shard_map(
        local,
        mesh=mesh,
        in_specs=placed,
        out_specs=(
            P("rep", None, None, "tp"),
            P(None, None, "tp"),
            P(("rep", "tp"), None),
            P(("rep", "tp"), None),
            P(None, None, "tp"),
        ),
        check_vma=False,
    )
```

```python
import functools
import math

import jax
import jax.numpy as jnp
from jax import lax
from jax.experimental import pallas as pl
from jax.experimental.pallas import tpu as pltpu
from jax.sharding import PartitionSpec as P

ROUNDS = 2
NS_STEPS = 5


NORM_EPSILON = 1e-06
MOMENTUM_DECAY = 0.9
LEARNING_RATE = 0.5
HIGHEST = lax.Precision.HIGHEST
LANES = 128
EARLY = 2
F32, BF16 = jnp.float32, jnp.bfloat16
PARAMS = pltpu.CompilerParams(vmem_limit_bytes=60 * 2**20)
SCALARS = pl.BlockSpec(memory_space=pltpu.SMEM)


def two_terms(x):
    high = x.astype(BF16)
    return high, (x - high.astype(F32)).astype(BF16)


def dot(a, b, transposed=False):
    dims = (((1,), (1 if transposed else 0,)), ((), ()))
    return lax.dot_general(a, b, dims, preferred_element_type=F32)


def small_by_large(small, high, low, transposed):
    rows = small.shape[0]
    small_high, small_low = two_terms(small)
    both = dot(jnp.concatenate([small_high, small_low], axis=0), high, transposed)
    return both[:rows] + both[rows:] + dot(small_high, low, transposed)


def dot3(a, b):
    a_high, a_low = two_terms(a)
    b_high, b_low = two_terms(b)
    return dot(
        jnp.concatenate([a_high, a_low, a_high], axis=1),
        jnp.concatenate([b_high, b_high, b_low], axis=0),
    )


def stacked(right):
    right_high, right_low = two_terms(right)
    return jnp.concatenate([right_high, right_high, right_low], axis=0)


def lay_lanes(scratch, value):
    rows = value.shape[0]
    for block in range(value.shape[1] // LANES):
        scratch[block * rows : (block + 1) * rows] = value[:, block * LANES : (block + 1) * LANES]


def read_lanes(scratch, rows):
    blocks = scratch.shape[0] // rows
    return jnp.concatenate([scratch[block * rows : (block + 1) * rows] for block in range(blocks)], axis=1)


def part_at(index, rows):
    return pl.ds(pl.multiple_of(index * rows, 8), rows)


def split_parts(scratch, me, part_refs):
    rows = part_refs[0].shape[0]
    for offset, part_ref in enumerate(part_refs):
        part_ref[...] = scratch[part_at(me ^ offset, rows), :]


def join_parts(scratch, me, part_refs):
    rows = part_refs[0].shape[0]
    for offset, part_ref in enumerate(part_refs):
        scratch[part_at(me ^ offset, rows), :] = part_ref[...]


def sum_of(refs):
    values = [ref[...] for ref in refs]
    while len(values) > 1:
        values = [sum(values[at : at + 2][1:], values[at]) for at in range(0, len(values), 2)]
    return values[0]


def put_left(left, step, left_refs, per_tp):
    for which, left_ref in enumerate(left_refs):

        @pl.when(step // per_tp == which)
        def _():
            left_ref[...] = left


def first_left_kernel(per_tp, ids_ref, grads_ref, error_ref, query_ref, high_ref, low_ref, *left_refs):
    high, low = two_terms(grads_ref[0, 0].astype(F32) + error_ref[0, 0])
    high_ref[0] = high
    low_ref[0] = low
    put_left(small_by_large(query_ref[0], high, low, True), pl.program_id(0), left_refs, per_tp)


def left_kernel(per_tp, ids_ref, high_ref, low_ref, *refs):
    parts, left_refs, (scratch, current) = refs[:-4], refs[-4:-2], refs[-2:]
    step = pl.program_id(0)
    rank = left_refs[0].shape[0]

    @pl.when(step == 0)
    def _():
        join_parts(scratch, ids_ref[0], parts)
        current[...] = read_lanes(scratch, current.shape[0])

    own = current[part_at(step, rank), :]
    put_left(small_by_large(own, high_ref[0], low_ref[0], True), step, left_refs, per_tp)


def split_kernel(tps, ids_ref, *refs):
    scratch = refs[-1]
    lay_lanes(scratch, sum_of(refs[:tps]))
    split_parts(scratch, ids_ref[0], refs[tps:-1])


def sum_kernel(scale, *refs):
    summed = sum_of(refs[:-1])
    refs[-1][...] = summed if scale == 1.0 else summed * scale


def mixing(left, rank):
    rows = left.shape[0]
    row_id = lax.broadcasted_iota(jnp.int32, (rows, rows), 0)
    col_id = lax.broadcasted_iota(jnp.int32, (rows, rows), 1)
    same = (row_id // rank) == (col_id // rank)
    eye = (row_id == col_id).astype(F32)
    left_high, left_low = two_terms(left)
    cross = dot(left_high, left_low, True)
    gram = jnp.where(same, dot(left_high, left_high, True) + cross + cross.T, 0.0)
    diagonal = jnp.sum(gram * eye, axis=0, keepdims=True)
    trace = jnp.sum(jnp.where(same, diagonal, 0.0), axis=1, keepdims=True) + NORM_EPSILON
    scale = lax.rsqrt(trace)
    scale = scale * (1.5 - 0.5 * trace * scale * scale)
    gram = gram * (scale * scale)
    step = 1.5 * eye - 0.5 * gram
    mixed = step * scale
    for _ in range(NS_STEPS - 1):
        gram = dot3(dot3(step, gram), step)
        step = 1.5 * eye - 0.5 * gram
        mixed = dot3(step, mixed)
    return mixed


def basis_kernel(rank, ids_ref, *refs):
    basis_ref, scratch = refs[-2:]
    join_parts(scratch, ids_ref[0], refs[:-2])
    rows = basis_ref.shape[0]
    left = read_lanes(scratch, rows)
    padded = jnp.concatenate([left, jnp.zeros((-rows % LANES, left.shape[1]), F32)], axis=0)
    basis_ref[...] = dot3(mixing(padded, rank), padded)[:rows]


def right_kernel(per_tp, ids_ref, first_ref, second_ref, high_ref, low_ref, *refs):
    part_refs, (scratch, right) = refs[:-2], refs[-2:]
    step = pl.program_id(0)
    rank = first_ref.shape[0] // per_tp
    at = part_at(step % per_tp, rank)
    own = jnp.where(step // per_tp == 0, first_ref[at, :], second_ref[at, :])
    right[part_at(step, rank), :] = small_by_large(own, high_ref[0], low_ref[0], False)

    @pl.when(step == pl.num_programs(0) - 1)
    def _():
        lay_lanes(scratch, right[...])
        split_parts(scratch, ids_ref[0], part_refs)


def factor_kernel(ids_ref, basis_ref, factors_ref):
    high, low = two_terms(basis_ref[0].T)
    factors_ref[...] = jnp.concatenate([high, low, high], axis=1)


def query_kernel(tps, ids_ref, *refs):
    query_ref, scratch = refs[-2:]
    halves = tps // 2
    per_half = (len(refs) - 2) // halves
    rows = query_ref.shape[0] // halves
    for half in range(halves):
        join_parts(scratch, ids_ref[0], refs[half * per_half : (half + 1) * per_half])
        value = read_lanes(scratch, rows)
        for which in range(2):
            owner = ids_ref[1] ^ (2 * half + which)
            query_ref[part_at(owner, rows // 2), :] = value[which * (rows // 2) : (which + 1) * (rows // 2)]


def weight_kernel(ids_ref, factors_ref, right_ref, base_ref, weights_ref):
    approx = dot(factors_ref[...], stacked(right_ref[...]))
    weights = (base_ref[...].reshape(approx.shape) - LEARNING_RATE * approx).astype(BF16)
    weights_ref[...] = weights.reshape(weights_ref.shape)


def place_kernel(ids_ref, part_ref, _, weights_ref):
    weights_ref[...] = part_ref[...].reshape(weights_ref.shape)


def error_kernel(per_half, ids_ref, factors_ref, right_ref, *refs):
    new_error_ref = refs[-1]
    approx = dot(factors_ref[...], stacked(right_ref[...]))
    for half in range(len(refs) // 2):
        high_ref, low_ref = refs[2 * half : 2 * half + 2]

        @pl.when(pl.program_id(0) // per_half == half)
        def _():
            new_error_ref[0, 0] = high_ref[0].astype(F32) + low_ref[0].astype(F32) - approx


def flat_kernel(ids_ref, factors_ref, right_ref, momentum_ref, master_ref, new_momentum_ref, new_master_ref):
    approx = dot(factors_ref[...], stacked(right_ref[...].reshape(right_ref.shape[-2:])))
    new_momentum = MOMENTUM_DECAY * momentum_ref[...] + approx
    new_momentum_ref[...] = new_momentum
    new_master_ref[...] = master_ref[...] - LEARNING_RATE * new_momentum


def shape(*dims, dtype=F32):
    return jax.ShapeDtypeStruct(dims, dtype)


def whole_call(kernel, name, out_shape, operands, ids=None, scratch=()):
    specs = [pl.BlockSpec(memory_space=pltpu.VMEM)] * len(operands)
    many = isinstance(out_shape, (list, tuple))
    out_spec = pl.BlockSpec(memory_space=pltpu.VMEM)
    moved = sum(4 * x.size for x in operands)
    if ids is not None:
        operands, specs = [ids, *operands], [SCALARS, *specs]
    return pl.pallas_call(
        kernel,
        in_specs=specs,
        out_specs=[out_spec] * len(out_shape) if many else out_spec,
        out_shape=out_shape,
        scratch_shapes=list(scratch),
        compiler_params=PARAMS,
        name=name,
        cost_estimate=pl.CostEstimate(flops=moved, bytes_accessed=2 * moved, transcendentals=0),
    )(*operands)


def grid_call(kernel, name, ids, grid, in_specs, out_specs, out_shape, operands, scratch=(), aliases=None, flops=0, moved=0):
    return pl.pallas_call(
        kernel,
        grid_spec=pltpu.PrefetchScalarGridSpec(
            num_scalar_prefetch=1,
            grid=grid,
            in_specs=in_specs,
            out_specs=out_specs,
            scratch_shapes=list(scratch),
        ),
        out_shape=out_shape,
        input_output_aliases=aliases or {},
        compiler_params=PARAMS,
        name=name,
        cost_estimate=pl.CostEstimate(flops=flops, bytes_accessed=moved, transcendentals=0),
    )(ids, *operands)


def swap(x, axis, size, offset):
    return lax.ppermute(x, axis, [(index, index ^ offset) for index in range(size)])


def scattered(parts, replicas):
    return [parts[0]] + [swap(parts[offset], "rep", replicas, offset) for offset in range(1, replicas)]


def spread(part, axis, size):
    return [part] + [swap(part, axis, size, offset) for offset in range(1, size)]


def local(grads, error, query, momentum, master):
    replicas, tps = lax.axis_size("rep"), lax.axis_size("tp")
    rep, tp = lax.axis_index("rep"), lax.axis_index("tp")
    ids = jnp.stack([rep, tp]).astype(jnp.int32)
    _, matrices, width, cols = grads.shape
    rank = query.shape[1]
    per_tp = matrices // tps
    per_half = 2 * per_tp
    halves = tps // 2
    tp_rows = per_tp * rank
    left_part = tp_rows * width // LANES // replicas
    right_part = 2 * tp_rows * cols // LANES // replicas
    own_rows = momentum.shape[0]
    flops = 2 * 3 * per_half * rank * width * cols
    elements = per_half * width * cols

    def matrix_of(half, k, at):
        return (at[1] ^ (2 * half + k // per_tp)) * per_tp + k % per_tp

    term_spec = pl.BlockSpec((1, width, cols), lambda k, at: (k, 0, 0))
    term_shape = shape(per_half, width, cols, dtype=BF16)
    left_specs = [
        pl.BlockSpec((rank, width), lambda k, at, which=which: (jnp.clip(k - which * per_tp, 0, per_tp - 1), 0))
        for which in range(2)
    ]
    left_shapes = [shape(tp_rows, width)] * 2

    def whole_spec(*dims):
        return pl.BlockSpec(dims, lambda k, at: (0,) * len(dims))

    terms, lefts = [None] * halves, [None] * tps
    for half in reversed(range(halves)):
        picked = functools.partial(matrix_of, half)
        high, low, *out = grid_call(
            functools.partial(first_left_kernel, per_tp),
            "first_left",
            ids,
            (per_half,),
            [
                pl.BlockSpec((1, 1, width, cols), lambda k, at, picked=picked: (0, picked(k, at), 0, 0)),
                pl.BlockSpec((1, 1, width, cols), lambda k, at, picked=picked: (0, picked(k, at), 0, 0)),
                pl.BlockSpec((1, rank, cols), lambda k, at, picked=picked: (picked(k, at), 0, 0)),
            ],
            [term_spec, term_spec, *left_specs],
            [term_shape, term_shape, *left_shapes],
            (grads, error, query),
            flops=flops,
            moved=10 * elements,
        )
        terms[half] = (high, low)
        lefts[2 * half : 2 * half + 2] = out

    gathered = []
    for power_pass in range(ROUNDS):
        met = [lefts[0]] + [swap(lefts[offset], "tp", tps, offset) for offset in range(1, tps)]
        parts = whole_call(
            functools.partial(split_kernel, tps),
            "left_split",
            [shape(left_part, LANES)] * replicas,
            met,
            ids,
            [pltpu.VMEM((left_part * replicas, LANES), F32)],
        )
        if power_pass == 0:
            base = []
            tied = lax.optimization_barrier((master, momentum, *parts))
            parts = list(tied[2:])
            for offset in range(tps):
                column = (tp ^ offset) * cols
                piece = lax.dynamic_slice_in_dim(tied[0], column, cols, 1)
                piece = piece - (LEARNING_RATE * MOMENTUM_DECAY) * lax.dynamic_slice_in_dim(tied[1], column, cols, 1)
                base.append(piece if offset == 0 else swap(piece, "tp", tps, offset))
            gathered = [lax.all_gather(base[offset], "rep") for offset in range(EARLY)]
        met = scattered(parts, replicas)
        part = whole_call(functools.partial(sum_kernel, 1.0), "left_sum", shape(left_part, LANES), met)
        basis = whole_call(
            functools.partial(basis_kernel, rank),
            "basis",
            shape(tp_rows, width),
            spread(part, "rep", replicas),
            ids,
            [pltpu.VMEM((left_part * replicas, LANES), F32)],
        )
        bases = spread(basis, "tp", tps)
        rights = []
        for half in range(halves):
            parts = grid_call(
                functools.partial(right_kernel, per_tp),
                "right",
                ids,
                (per_half,),
                [whole_spec(tp_rows, width), whole_spec(tp_rows, width), term_spec, term_spec],
                [whole_spec(right_part, LANES)] * replicas,
                [shape(right_part, LANES)] * replicas,
                (*bases[2 * half : 2 * half + 2], *terms[half]),
                [pltpu.VMEM((right_part * replicas, LANES), F32), pltpu.VMEM((2 * tp_rows, cols), F32)],
                flops=flops,
                moved=4 * elements,
            )
            met = scattered(parts, replicas)
            part = whole_call(functools.partial(sum_kernel, 1.0 / replicas), "right_sum", shape(right_part, LANES), met)
            rights.append(spread(part, "rep", replicas))
        if power_pass < ROUNDS - 1:
            for half in range(halves):
                lefts[2 * half : 2 * half + 2] = grid_call(
                    functools.partial(left_kernel, per_tp),
                    "left",
                    ids,
                    (per_half,),
                    [term_spec, term_spec] + [whole_spec(right_part, LANES)] * replicas,
                    left_specs,
                    left_shapes,
                    (*terms[half], *rights[half]),
                    [pltpu.VMEM((right_part * replicas, LANES), F32), pltpu.VMEM((2 * tp_rows, cols), F32)],
                    flops=flops,
                    moved=4 * elements,
                )

    factors = grid_call(
        factor_kernel,
        "factors",
        ids,
        (matrices,),
        [pl.BlockSpec((1, rank, width), lambda k, at: ((at[1] ^ (k // per_tp)) * per_tp + k % per_tp, 0, 0))],
        pl.BlockSpec((width, 3 * rank), lambda k, at: (k, 0)),
        shape(matrices * width, 3 * rank, dtype=BF16),
        (jnp.concatenate(bases, axis=0).reshape(matrices, rank, width),),
    )
    right = whole_call(
        functools.partial(query_kernel, tps),
        "new_query",
        shape(matrices * rank, cols),
        [part for parts in rights for part in parts],
        ids,
        [pltpu.VMEM((right_part * replicas, LANES), F32)],
    )

    chunk = math.gcd(own_rows, width)
    chunks = own_rows // chunk

    def chunk_at(replica, owner, b):
        return (replica * tps + owner) * chunks + b

    late = tps - EARLY
    block = grid_call(
        weight_kernel,
        "late_weights",
        ids,
        (late, chunks),
        [
            pl.BlockSpec((chunk, 3 * rank), lambda s, b, at: (chunk_at(at[0], at[1] ^ (EARLY + s), b), 0)),
            pl.BlockSpec((rank, cols), lambda s, b, at: (chunk_at(at[0], at[1] ^ (EARLY + s), b) * chunk // width, 0)),
            pl.BlockSpec((1, chunk, cols), lambda s, b, at: (s, b, 0)),
        ],
        pl.BlockSpec((1, chunk, cols), lambda s, b, at: (s, b, 0)),
        shape(late, own_rows, cols, dtype=BF16),
        (factors, right, jnp.stack(base[EARLY:])),
    )
    late_rows = lax.all_gather(block, "rep")

    weights_shape = shape(replicas, tps, own_rows, cols, dtype=BF16)
    weights = None
    for offset in range(EARLY):
        kernel = weight_kernel if weights is None else lambda ids_ref, a, b, c, _, out: weight_kernel(ids_ref, a, b, c, out)
        weights = grid_call(
            kernel,
            "early_weights",
            ids,
            (replicas, chunks),
            [
                pl.BlockSpec((chunk, 3 * rank), lambda q, b, at, offset=offset: (chunk_at(q, at[1] ^ offset, b), 0)),
                pl.BlockSpec((rank, cols), lambda q, b, at, offset=offset: (chunk_at(q, at[1] ^ offset, b) * chunk // width, 0)),
                pl.BlockSpec((1, chunk, cols), lambda q, b, at: (q, b, 0)),
            ]
            + ([] if weights is None else [pl.BlockSpec(memory_space=pl.ANY)]),
            pl.BlockSpec((1, 1, chunk, cols), lambda q, b, at, offset=offset: (q, at[1] ^ offset, b, 0)),
            weights_shape,
            (factors, right, gathered[offset]) + (() if weights is None else (weights,)),
            aliases=None if weights is None else {4: 0},
            flops=2 * 3 * rank * replicas * own_rows * cols,
            moved=6 * replicas * own_rows * cols,
        )
    weights = grid_call(
        place_kernel,
        "place_late",
        ids,
        (replicas, late),
        [
            pl.BlockSpec((1, 1, own_rows, cols), lambda q, s, at: (q, s, 0, 0)),
            pl.BlockSpec(memory_space=pl.ANY),
        ],
        pl.BlockSpec((1, 1, own_rows, cols), lambda q, s, at: (q, at[1] ^ (EARLY + s), 0, 0)),
        weights_shape,
        (late_rows, weights),
        aliases={2: 0},
    )
    weights = weights.reshape(matrices, width, cols)

    def picked(k, at):
        return matrix_of(k // per_half, k % per_half, at)

    new_error = grid_call(
        functools.partial(error_kernel, per_half),
        "new_error",
        ids,
        (matrices,),
        [
            pl.BlockSpec((width, 3 * rank), lambda k, at: (picked(k, at), 0)),
            pl.BlockSpec((rank, cols), lambda k, at: (picked(k, at), 0)),
        ]
        + [
            pl.BlockSpec((1, width, cols), lambda k, at, half=half: (jnp.clip(k - half * per_half, 0, per_half - 1), 0, 0))
            for half in range(halves)
            for _ in range(2)
        ],
        pl.BlockSpec((1, 1, width, cols), lambda k, at: (0, picked(k, at), 0, 0)),
        shape(*error.shape),
        (factors, right, *[term for pair in terms for term in pair]),
        flops=2 * 3 * rank * error.size,
        moved=8 * error.size,
    )

    rep_rows = tps * own_rows
    spans = -(-(width - math.gcd(rep_rows, width) + rep_rows) // width)

    def first_near(at):
        return jnp.minimum(at[0] * rep_rows // width, matrices - spans)

    near = lax.dynamic_slice_in_dim(right.reshape(matrices, rank, cols), first_near(ids), spans, 0)
    near = jnp.stack(spread(near, "tp", tps))
    wide = pl.BlockSpec((chunk, cols), lambda b, s, at: (b, at[1] ^ s))
    new_momentum, new_master = grid_call(
        flat_kernel,
        "flat_rows",
        ids,
        (chunks, tps),
        [
            pl.BlockSpec((chunk, 3 * rank), lambda b, s, at: (chunk_at(at[0], at[1], b), 0)),
            pl.BlockSpec(
                (1, 1, rank, cols),
                lambda b, s, at: (s, chunk_at(at[0], at[1], b) * chunk // width - first_near(at), 0, 0),
            ),
            wide,
            wide,
        ],
        [wide, wide],
        [shape(*momentum.shape), shape(*master.shape)],
        (factors, near, momentum, master),
        flops=2 * 3 * rank * momentum.size,
        moved=16 * momentum.size,
    )
    return (new_error, right.reshape(matrices, rank, cols), new_momentum, new_master, weights)


def plain_orthonormal(factor):
    def gram_of(x):
        return jnp.einsum("krd,ksd->krs", x, x, precision=HIGHEST)

    gram_now = gram_of(factor)
    factor_scale = lax.rsqrt(jnp.trace(gram_now, axis1=1, axis2=2)[:, None, None] + NORM_EPSILON)
    ortho_basis = factor * factor_scale
    gram_now = gram_now * (factor_scale * factor_scale)
    for iteration in range(NS_STEPS):
        if iteration > 0:
            gram_now = gram_of(ortho_basis)
        ortho_basis = 1.5 * ortho_basis - 0.5 * jnp.einsum("krs,ksd->krd", gram_now, ortho_basis, precision=HIGHEST)
    return ortho_basis


def plain_local(grads, error, query, momentum, master):
    corrected = grads[0].astype(F32) + error[0]
    current = query
    replicas = lax.axis_size("rep")
    for _ in range(ROUNDS):
        partial_factor = jnp.einsum("kdf,krf->krd", corrected, current, precision=HIGHEST)
        ortho_basis = plain_orthonormal(lax.psum(partial_factor, ("rep", "tp")))
        partial_query = jnp.einsum("kdf,krd->krf", corrected, ortho_basis, precision=HIGHEST)
        current = lax.psum(partial_query, "rep") / replicas
    approx = jnp.einsum("krd,krf->kdf", ortho_basis, current, precision=HIGHEST)
    new_error = (corrected - approx)[None]
    matrices, width, cols = approx.shape
    block_rows = matrices * width // replicas
    own_block = lax.dynamic_slice_in_dim(
        approx.reshape(matrices * width, cols), lax.axis_index("rep") * block_rows, block_rows, 0
    )
    flat_approx = lax.all_to_all(own_block, "tp", split_axis=0, concat_axis=1, tiled=True)
    new_momentum = MOMENTUM_DECAY * momentum + flat_approx
    new_master = master - LEARNING_RATE * new_momentum
    by_columns = lax.all_to_all(new_master.astype(BF16), "tp", split_axis=1, concat_axis=0, tiled=True)
    weights = lax.all_gather(by_columns, "rep", axis=0, tiled=True).reshape(matrices, width, cols)
    return (new_error, current, new_momentum, new_master, weights)


def divides(mesh, matrices, rank, width, cols):
    replicas, tps = mesh.shape["rep"], mesh.shape["tp"]
    if replicas & (replicas - 1) or tps & (tps - 1) or tps < 4 or matrices % tps or cols % (tps * LANES) or width % LANES:
        return False
    tp_rows = matrices // tps * rank
    tiles = 8 * LANES * replicas
    return tp_rows * width % tiles == 0 and 2 * tp_rows * (cols // tps) % tiles == 0


def solution(mesh):
    placed = (
        P("rep", None, None, "tp"),
        P("rep", None, None, "tp"),
        P(None, None, "tp"),
        P(("rep", "tp"), None),
        P(("rep", "tp"), None),
    )

    def step(grads, error, query, momentum, master):
        fits = divides(mesh, grads.shape[1], query.shape[1], grads.shape[2], grads.shape[3])
        return jax.shard_map(
            local if fits else plain_local,
            mesh=mesh,
            in_specs=placed,
            out_specs=(
                P("rep", None, None, "tp"),
                P(None, None, "tp"),
                P(("rep", "tp"), None),
                P(("rep", "tp"), None),
                P(None, None, "tp"),
            ),
            check_vma=False,
        )(grads, error, query, momentum, master)

    return step
```

```python
import functools
import math

import jax
import jax.numpy as jnp
from jax import lax
from jax.experimental import pallas as pl
from jax.experimental.pallas import tpu as pltpu
from jax.sharding import PartitionSpec as P

ROUNDS = 2
NS_STEPS = 5


NORM_EPSILON = 1e-06
MOMENTUM_DECAY = 0.9
LEARNING_RATE = 0.5
HIGHEST = lax.Precision.HIGHEST
LANES = 128
EARLY = 2
F32, BF16 = jnp.float32, jnp.bfloat16
SCALARS = pl.BlockSpec(memory_space=pltpu.SMEM)


def two_terms(x):
    high = x.astype(BF16)
    return high, (x - high.astype(F32)).astype(BF16)


def dot(a, b, transposed=False):
    dims = (((1,), (1 if transposed else 0,)), ((), ()))
    return lax.dot_general(a, b, dims, preferred_element_type=F32)


def small_by_large(small, high, low, transposed):
    rows = small.shape[0]
    small_high, small_low = two_terms(small)
    both = dot(jnp.concatenate([small_high, small_low], axis=0), high, transposed)
    return both[:rows] + both[rows:] + dot(small_high, low, transposed)


def dot3(a, b):
    a_high, a_low = two_terms(a)
    b_high, b_low = two_terms(b)
    return dot(
        jnp.concatenate([a_high, a_low, a_high], axis=1),
        jnp.concatenate([b_high, b_high, b_low], axis=0),
    )


def stacked(right):
    right_high, right_low = two_terms(right)
    return jnp.concatenate([right_high, right_high, right_low], axis=0)


def lay_lanes(scratch, value):
    rows = value.shape[0]
    for block in range(value.shape[1] // LANES):
        scratch[block * rows : (block + 1) * rows] = value[:, block * LANES : (block + 1) * LANES]


def read_lanes(scratch, rows):
    blocks = scratch.shape[0] // rows
    return jnp.concatenate([scratch[block * rows : (block + 1) * rows] for block in range(blocks)], axis=1)


def part_at(index, rows):
    return pl.ds(pl.multiple_of(index * rows, 8), rows)


def split_parts(scratch, me, part_refs):
    rows = part_refs[0].shape[0]
    for offset, part_ref in enumerate(part_refs):
        part_ref[...] = scratch[part_at(me ^ offset, rows), :]


def join_parts(scratch, me, part_refs):
    rows = part_refs[0].shape[0]
    for offset, part_ref in enumerate(part_refs):
        scratch[part_at(me ^ offset, rows), :] = part_ref[...]


def sum_of(refs):
    values = [ref[...] for ref in refs]
    while len(values) > 1:
        values = [sum(values[at : at + 2][1:], values[at]) for at in range(0, len(values), 2)]
    return values[0]


def put_left(left, step, left_refs, per_tp):
    for which, left_ref in enumerate(left_refs):

        @pl.when(step // per_tp == which)
        def _():
            left_ref[...] = left


def first_left_kernel(per_tp, ids_ref, grads_ref, error_ref, query_ref, high_ref, low_ref, *left_refs):
    high, low = two_terms(grads_ref[0, 0].astype(F32) + error_ref[0, 0])
    high_ref[0] = high
    low_ref[0] = low
    put_left(small_by_large(query_ref[0], high, low, True), pl.program_id(0), left_refs, per_tp)


def left_kernel(per_tp, ids_ref, high_ref, low_ref, *refs):
    parts, left_refs, (scratch, current) = refs[:-4], refs[-4:-2], refs[-2:]
    step = pl.program_id(0)
    rank = left_refs[0].shape[0]

    @pl.when(step == 0)
    def _():
        join_parts(scratch, ids_ref[0], parts)
        current[...] = read_lanes(scratch, current.shape[0])

    own = current[part_at(step, rank), :]
    put_left(small_by_large(own, high_ref[0], low_ref[0], True), step, left_refs, per_tp)


def split_kernel(tps, *refs):
    lay_lanes(refs[-1], sum_of(refs[:tps]))


def total_kernel(parts_ref, out_ref):
    summed = sum_of([parts_ref.at[part] for part in range(parts_ref.shape[0])])
    for part in range(parts_ref.shape[0]):
        out_ref[part] = summed


def sum_kernel(scale, *refs):
    summed = sum_of(refs[:-1])
    refs[-1][...] = summed if scale == 1.0 else summed * scale


def mixing(left, rank):
    rows = left.shape[0]
    row_id = lax.broadcasted_iota(jnp.int32, (rows, rows), 0)
    col_id = lax.broadcasted_iota(jnp.int32, (rows, rows), 1)
    same = (row_id // rank) == (col_id // rank)
    eye = (row_id == col_id).astype(F32)
    left_high, left_low = two_terms(left)
    cross = dot(left_high, left_low, True)
    gram = jnp.where(same, dot(left_high, left_high, True) + cross + cross.T, 0.0)
    diagonal = jnp.sum(gram * eye, axis=0, keepdims=True)
    trace = jnp.sum(jnp.where(same, diagonal, 0.0), axis=1, keepdims=True) + NORM_EPSILON
    scale = lax.rsqrt(trace)
    scale = scale * (1.5 - 0.5 * trace * scale * scale)
    gram = gram * (scale * scale)
    step = 1.5 * eye - 0.5 * gram
    mixed = step * scale
    for _ in range(NS_STEPS - 1):
        gram = dot3(dot3(step, gram), step)
        step = 1.5 * eye - 0.5 * gram
        mixed = dot3(step, mixed)
    return mixed


def basis_kernel(rank, left_ref, basis_ref):
    rows = basis_ref.shape[0]
    left = read_lanes(left_ref, rows)
    padded = jnp.concatenate([left, jnp.zeros((-rows % LANES, left.shape[1]), F32)], axis=0)
    basis_ref[...] = dot3(mixing(padded, rank), padded)[:rows]


def right_kernel(per_tp, ids_ref, first_ref, second_ref, high_ref, low_ref, *refs):
    part_refs, (scratch, right) = refs[:-2], refs[-2:]
    step = pl.program_id(0)
    rank = first_ref.shape[0] // per_tp
    at = part_at(step % per_tp, rank)
    own = jnp.where(step // per_tp == 0, first_ref[at, :], second_ref[at, :])
    right[part_at(step, rank), :] = small_by_large(own, high_ref[0], low_ref[0], False)

    @pl.when(step == pl.num_programs(0) - 1)
    def _():
        lay_lanes(scratch, right[...])
        split_parts(scratch, ids_ref[0], part_refs)


def rows_of_update(basis_ref, right_ref, scratch, first_unit, unit, per_tp, rank, tp, first_matrix):
    per_matrix = basis_ref.shape[1] // unit
    for u in range(scratch.shape[0] // unit):
        at = first_unit + u
        matrix = at // per_matrix
        slot = ((matrix // per_tp) ^ tp) * per_tp + matrix % per_tp
        lanes = pl.ds(pl.multiple_of((at % per_matrix) * unit, LANES), unit)
        factor = basis_ref[part_at(slot, rank), lanes]
        right = right_ref[part_at(matrix - first_matrix, rank), :]
        scratch[u * unit : (u + 1) * unit] = product(factor, right)


def product(factor, right):
    high, low = two_terms(factor.T)
    return dot(jnp.concatenate([high, low, high], axis=1), stacked(right))


def late_kernel(tps, early, unit, per_tp, rank, ids_ref, basis_ref, *refs):
    late = tps - early
    lanes, approx = refs[-2:]
    query_ref, weight_refs = refs[-3 - late], refs[-2 - late : -2]
    base_refs = refs[-3 - 2 * late : -3 - late]
    part_refs = refs[: -3 - 2 * late]
    halves = tps // 2
    per_half = len(part_refs) // halves
    rows = query_ref.shape[0] // halves
    tp = ids_ref[1]
    for half in range(halves):
        join_parts(lanes, ids_ref[0], part_refs[half * per_half : (half + 1) * per_half])
        value = read_lanes(lanes, rows)
        for which in range(2):
            owner = tp ^ (2 * half + which)
            query_ref[part_at(owner, rows // 2), :] = value[which * (rows // 2) : (which + 1) * (rows // 2)]
    units = approx.shape[0] // unit
    rows_of_update(basis_ref, query_ref, approx, ids_ref[0] * units, unit, per_tp, rank, tp, 0)
    for which in range(late):
        base = base_refs[which][...]
        own = approx[part_at(tp ^ (early + which), base.shape[0]), :]
        weight_refs[which][...] = (base - LEARNING_RATE * own).astype(BF16)


def place_kernel(ids_ref, part_ref, _, weights_ref):
    weights_ref[...] = part_ref[...].reshape(weights_ref.shape)


def update_kernel(early, per_tp, rank, ids_ref, basis_ref, right_ref, *refs):
    new_error_ref, weights_ref, approx = refs[-3:]
    base_refs, term_refs = refs[:early], refs[early:-3]
    slot, matrix = pl.program_id(0), pl.program_id(1)
    at = part_at(matrix, rank)
    own = product(basis_ref[at, :], right_ref[at, :])
    width = own.shape[0]
    approx[part_at(matrix, width), :] = own
    for half in range(len(term_refs) // 2):

        @pl.when(slot // 2 == half)
        def _():
            high, low = (ref[0].astype(F32) for ref in term_refs[2 * half : 2 * half + 2])
            new_error_ref[0, 0] = high + low - own

    @pl.when(matrix == per_tp - 1)
    def _():
        replicas, tps, own_rows, _ = weights_ref.shape
        for replica in range(replicas):
            for offset, base_ref in enumerate(base_refs):
                owner = ids_ref[1] ^ offset
                rows = approx[part_at(replica * tps + owner, own_rows), :]
                weights_ref[replica, owner] = (base_ref[replica] - LEARNING_RATE * rows).astype(BF16)


def flat_kernel(unit, per_tp, rank, matrices, ids_ref, basis_ref, near_ref, momentum_ref, master_ref, new_momentum_ref, new_master_ref, approx):
    units = approx.shape[0] // unit
    spans = near_ref.shape[1] // rank
    first_unit = ids_ref[0] * units
    first = jnp.minimum(first_unit // (basis_ref.shape[1] // unit), matrices - spans)
    rows_of_update(basis_ref, near_ref.at[0], approx, first_unit, unit, per_tp, rank, ids_ref[1], first)
    own = approx[part_at(ids_ref[1], momentum_ref.shape[0]), :]
    new_momentum = MOMENTUM_DECAY * momentum_ref[...] + own
    new_momentum_ref[...] = new_momentum
    new_master_ref[...] = master_ref[...] - LEARNING_RATE * new_momentum


def shape(*dims, dtype=F32):
    return jax.ShapeDtypeStruct(dims, dtype)


def grant(mib):
    return pltpu.CompilerParams(vmem_limit_bytes=mib * 2**20)


def whole_call(kernel, name, out_shape, operands, ids=None, scratch=()):
    specs = [pl.BlockSpec(memory_space=pltpu.VMEM)] * len(operands)
    many = isinstance(out_shape, (list, tuple))
    out_spec = pl.BlockSpec(memory_space=pltpu.VMEM)
    moved = sum(4 * x.size for x in operands)
    if ids is not None:
        operands, specs = [ids, *operands], [SCALARS, *specs]
    return pl.pallas_call(
        kernel,
        in_specs=specs,
        out_specs=[out_spec] * len(out_shape) if many else out_spec,
        out_shape=out_shape,
        scratch_shapes=list(scratch),
        compiler_params=grant(12),
        name=name,
        cost_estimate=pl.CostEstimate(flops=moved, bytes_accessed=2 * moved, transcendentals=0),
    )(*operands)


def grid_call(kernel, name, ids, grid, in_specs, out_specs, out_shape, operands, scratch=(), aliases=None, flops=0, moved=0, mib=20):
    return pl.pallas_call(
        kernel,
        grid_spec=pltpu.PrefetchScalarGridSpec(
            num_scalar_prefetch=1,
            grid=grid,
            in_specs=in_specs,
            out_specs=out_specs,
            scratch_shapes=list(scratch),
        ),
        out_shape=out_shape,
        input_output_aliases=aliases or {},
        compiler_params=grant(mib),
        name=name,
        cost_estimate=pl.CostEstimate(flops=flops, bytes_accessed=moved, transcendentals=0),
    )(ids, *operands)


def swap(x, axis, size, offset):
    return lax.ppermute(x, axis, [(index, index ^ offset) for index in range(size)])


def scattered(parts, replicas):
    return [parts[0]] + [swap(parts[offset], "rep", replicas, offset) for offset in range(1, replicas)]


def spread(part, axis, size):
    return [part] + [swap(part, axis, size, offset) for offset in range(1, size)]


def local(grads, error, query, momentum, master):
    replicas, tps = lax.axis_size("rep"), lax.axis_size("tp")
    rep, tp = lax.axis_index("rep"), lax.axis_index("tp")
    ids = jnp.stack([rep, tp]).astype(jnp.int32)
    _, matrices, width, cols = grads.shape
    rank = query.shape[1]
    per_tp = matrices // tps
    per_half = 2 * per_tp
    halves = tps // 2
    tp_rows = per_tp * rank
    left_part = tp_rows * width // LANES // replicas
    right_part = 2 * tp_rows * cols // LANES // replicas
    own_rows = momentum.shape[0]
    flops = 2 * 3 * per_half * rank * width * cols
    elements = per_half * width * cols

    def matrix_of(half, k, at):
        return (at[1] ^ (2 * half + k // per_tp)) * per_tp + k % per_tp

    term_spec = pl.BlockSpec((1, width, cols), lambda k, at: (k, 0, 0))
    term_shape = shape(per_half, width, cols, dtype=BF16)
    left_specs = [
        pl.BlockSpec((rank, width), lambda k, at, which=which: (jnp.clip(k - which * per_tp, 0, per_tp - 1), 0))
        for which in range(2)
    ]
    left_shapes = [shape(tp_rows, width)] * 2

    def whole_spec(*dims):
        return pl.BlockSpec(dims, lambda k, at: (0,) * len(dims))

    terms, lefts = [None] * halves, [None] * tps
    for half in reversed(range(halves)):
        picked = functools.partial(matrix_of, half)
        high, low, *out = grid_call(
            functools.partial(first_left_kernel, per_tp),
            "first_left",
            ids,
            (per_half,),
            [
                pl.BlockSpec((1, 1, width, cols), lambda k, at, picked=picked: (0, picked(k, at), 0, 0)),
                pl.BlockSpec((1, 1, width, cols), lambda k, at, picked=picked: (0, picked(k, at), 0, 0)),
                pl.BlockSpec((1, rank, cols), lambda k, at, picked=picked: (picked(k, at), 0, 0)),
            ],
            [term_spec, term_spec, *left_specs],
            [term_shape, term_shape, *left_shapes],
            (grads, error, query),
            flops=flops,
            moved=10 * elements,
        )
        terms[half] = (high, low)
        lefts[2 * half : 2 * half + 2] = out

    def base_at(offset, new_values, old_values):
        column = (tp ^ offset) * cols
        piece = lax.dynamic_slice_in_dim(new_values, column, cols, 1)
        piece = piece - (LEARNING_RATE * MOMENTUM_DECAY) * lax.dynamic_slice_in_dim(old_values, column, cols, 1)
        return piece if offset == 0 else swap(piece, "tp", tps, offset)

    base = [base_at(0, master, momentum)]
    gathered = [lax.all_gather(base[0], "rep")]
    for power_pass in range(ROUNDS):
        met = [lefts[0]] + [swap(lefts[offset], "tp", tps, offset) for offset in range(1, tps)]
        parts = whole_call(
            functools.partial(split_kernel, tps), "left_split", shape(left_part * replicas, LANES), met
        )
        if power_pass == 0:
            parts, new_values, old_values = lax.optimization_barrier((parts, master, momentum))
            base += [base_at(offset, new_values, old_values) for offset in range(1, tps)]
            gathered += [lax.all_gather(base[offset], "rep") for offset in range(1, EARLY)]
        parts = parts.reshape(replicas, left_part, LANES)
        parts = lax.all_to_all(parts, "rep", split_axis=0, concat_axis=0, tiled=True)
        parts = whole_call(total_kernel, "left_sum", shape(*parts.shape), [parts])
        parts = lax.all_to_all(parts, "rep", split_axis=0, concat_axis=0, tiled=True)
        basis = whole_call(
            functools.partial(basis_kernel, rank), "basis", shape(tp_rows, width), [parts.reshape(-1, LANES)]
        )
        bases = [basis]
        for bit in range(tps.bit_length() - 2, 0, -1):
            bases += [swap(one, "tp", tps, 1 << bit) for one in bases]
        even = {}
        for at, one in enumerate(bases):
            even[sum(1 << bit for place, bit in enumerate(range(tps.bit_length() - 2, 0, -1)) if at >> place & 1)] = one
        bases = []
        for offset in range(0, tps, 2):
            bases += [even[offset], swap(even[offset], "tp", tps, 1)]
        rights = []
        for half in range(halves):
            parts = grid_call(
                functools.partial(right_kernel, per_tp),
                "right",
                ids,
                (per_half,),
                [whole_spec(tp_rows, width), whole_spec(tp_rows, width), term_spec, term_spec],
                [whole_spec(right_part, LANES)] * replicas,
                [shape(right_part, LANES)] * replicas,
                (*bases[2 * half : 2 * half + 2], *terms[half]),
                [pltpu.VMEM((right_part * replicas, LANES), F32), pltpu.VMEM((2 * tp_rows, cols), F32)],
                flops=flops,
                moved=4 * elements,
            )
            met = scattered(parts, replicas)
            part = whole_call(functools.partial(sum_kernel, 1.0 / replicas), "right_sum", shape(right_part, LANES), met)
            rights.append(spread(part, "rep", replicas))
        if power_pass < ROUNDS - 1:
            for half in range(halves):
                lefts[2 * half : 2 * half + 2] = grid_call(
                    functools.partial(left_kernel, per_tp),
                    "left",
                    ids,
                    (per_half,),
                    [term_spec, term_spec] + [whole_spec(right_part, LANES)] * replicas,
                    left_specs,
                    left_shapes,
                    (*terms[half], *rights[half]),
                    [pltpu.VMEM((right_part * replicas, LANES), F32), pltpu.VMEM((2 * tp_rows, cols), F32)],
                    flops=flops,
                    moved=4 * elements,
                )

    all_bases = jnp.concatenate(bases, axis=0)
    late = tps - EARLY
    rep_rows = tps * own_rows
    unit = math.gcd(rep_rows, width)
    right, *blocks = whole_call(
        functools.partial(late_kernel, tps, EARLY, unit, per_tp, rank),
        "late_rows",
        [shape(matrices * rank, cols)] + [shape(own_rows, cols, dtype=BF16)] * late,
        [all_bases, *[part for parts in rights for part in parts], *base[EARLY:]],
        ids,
        [pltpu.VMEM((right_part * replicas, LANES), F32), pltpu.VMEM((rep_rows, cols), F32)],
    )
    late_rows = [lax.all_gather(block, "rep") for block in blocks]

    new_error, weights = grid_call(
        functools.partial(update_kernel, EARLY, per_tp, rank),
        "update",
        ids,
        (tps, per_tp),
        [
            pl.BlockSpec((tp_rows, width), lambda s, j, at: (s, 0)),
            pl.BlockSpec((tp_rows, cols), lambda s, j, at: (at[1] ^ s, 0)),
        ]
        + [pl.BlockSpec((replicas // tps, own_rows, cols), lambda s, j, at: (at[1] ^ s, 0, 0))] * EARLY
        + [
            pl.BlockSpec(
                (1, width, cols),
                lambda s, j, at, half=half: (jnp.clip(s * per_tp + j - half * per_half, 0, per_half - 1), 0, 0),
            )
            for half in range(halves)
            for _ in range(2)
        ],
        [
            pl.BlockSpec((1, 1, width, cols), lambda s, j, at: (0, (at[1] ^ s) * per_tp + j, 0, 0)),
            pl.BlockSpec((replicas // tps, tps, own_rows, cols), lambda s, j, at: (at[1] ^ s, 0, 0, 0)),
        ],
        [shape(*error.shape), shape(replicas, tps, own_rows, cols, dtype=BF16)],
        (all_bases, right, *gathered, *[term for pair in terms for term in pair]),
        [pltpu.VMEM((per_tp * width, cols), F32)],
        flops=2 * 3 * rank * error.size,
        moved=12 * error.size,
        mib=36,
    )

    spans = -(-(width - unit + rep_rows) // width)
    first = jnp.minimum(rep * rep_rows // width, matrices - spans)
    near = lax.dynamic_slice_in_dim(right, first * rank, spans * rank, 0)
    near = jnp.stack(spread(near, "tp", tps))
    wide = pl.BlockSpec((own_rows, cols), lambda s, at: (0, at[1] ^ s))
    new_momentum, new_master = grid_call(
        functools.partial(flat_kernel, unit, per_tp, rank, matrices),
        "flat_rows",
        ids,
        (tps,),
        [
            whole_spec(matrices * rank, width),
            pl.BlockSpec((1, spans * rank, cols), lambda s, at: (s, 0, 0)),
            wide,
            wide,
        ],
        [wide, wide],
        [shape(*momentum.shape), shape(*master.shape)],
        (all_bases, near, momentum, master),
        [pltpu.VMEM((rep_rows, cols), F32)],
        flops=2 * 3 * rank * momentum.size * tps,
        moved=16 * momentum.size,
    )

    for which in range(late):
        groups = 2
        weights = grid_call(
            place_kernel,
            "place_late",
            ids,
            (groups,),
            [
                pl.BlockSpec((replicas // groups, own_rows, cols), lambda q, at: (q, 0, 0)),
                pl.BlockSpec(memory_space=pl.ANY),
            ],
            pl.BlockSpec(
                (replicas // groups, 1, own_rows, cols), lambda q, at, which=which: (q, at[1] ^ (EARLY + which), 0, 0)
            ),
            shape(*weights.shape, dtype=BF16),
            (late_rows[which], weights),
            aliases={2: 0},
        )
    weights = weights.reshape(matrices, width, cols)
    return (new_error, right.reshape(matrices, rank, cols), new_momentum, new_master, weights)


def plain_orthonormal(factor):
    def gram_of(x):
        return jnp.einsum("krd,ksd->krs", x, x, precision=HIGHEST)

    gram_now = gram_of(factor)
    factor_scale = lax.rsqrt(jnp.trace(gram_now, axis1=1, axis2=2)[:, None, None] + NORM_EPSILON)
    ortho_basis = factor * factor_scale
    gram_now = gram_now * (factor_scale * factor_scale)
    for iteration in range(NS_STEPS):
        if iteration > 0:
            gram_now = gram_of(ortho_basis)
        ortho_basis = 1.5 * ortho_basis - 0.5 * jnp.einsum("krs,ksd->krd", gram_now, ortho_basis, precision=HIGHEST)
    return ortho_basis


def plain_local(grads, error, query, momentum, master):
    corrected = grads[0].astype(F32) + error[0]
    current = query
    replicas = lax.axis_size("rep")
    for _ in range(ROUNDS):
        partial_factor = jnp.einsum("kdf,krf->krd", corrected, current, precision=HIGHEST)
        ortho_basis = plain_orthonormal(lax.psum(partial_factor, ("rep", "tp")))
        partial_query = jnp.einsum("kdf,krd->krf", corrected, ortho_basis, precision=HIGHEST)
        current = lax.psum(partial_query, "rep") / replicas
    approx = jnp.einsum("krd,krf->kdf", ortho_basis, current, precision=HIGHEST)
    new_error = (corrected - approx)[None]
    matrices, width, cols = approx.shape
    block_rows = matrices * width // replicas
    own_block = lax.dynamic_slice_in_dim(
        approx.reshape(matrices * width, cols), lax.axis_index("rep") * block_rows, block_rows, 0
    )
    flat_approx = lax.all_to_all(own_block, "tp", split_axis=0, concat_axis=1, tiled=True)
    new_momentum = MOMENTUM_DECAY * momentum + flat_approx
    new_master = master - LEARNING_RATE * new_momentum
    by_columns = lax.all_to_all(new_master.astype(BF16), "tp", split_axis=1, concat_axis=0, tiled=True)
    weights = lax.all_gather(by_columns, "rep", axis=0, tiled=True).reshape(matrices, width, cols)
    return (new_error, current, new_momentum, new_master, weights)


def divides(mesh, matrices, rank, width, cols):
    replicas, tps = mesh.shape["rep"], mesh.shape["tp"]
    if replicas & (replicas - 1) or tps & (tps - 1) or tps < 4 or replicas % tps or matrices % tps or cols % (tps * LANES) or width % LANES:
        return False
    if math.gcd(matrices * width // replicas, width) % LANES:
        return False
    tp_rows = matrices // tps * rank
    tiles = 8 * LANES * replicas
    return tp_rows * width % tiles == 0 and 2 * tp_rows * (cols // tps) % tiles == 0


def solution(mesh):
    placed = (
        P("rep", None, None, "tp"),
        P("rep", None, None, "tp"),
        P(None, None, "tp"),
        P(("rep", "tp"), None),
        P(("rep", "tp"), None),
    )

    def step(grads, error, query, momentum, master):
        fits = divides(mesh, grads.shape[1], query.shape[1], grads.shape[2], grads.shape[3])
        return jax.shard_map(
            local if fits else plain_local,
            mesh=mesh,
            in_specs=placed,
            out_specs=(
                P("rep", None, None, "tp"),
                P(None, None, "tp"),
                P(("rep", "tp"), None),
                P(("rep", "tp"), None),
                P(None, None, "tp"),
            ),
            check_vma=False,
        )(grads, error, query, momentum, master)

    return step
```

```python
import functools
import math

import jax
import jax.numpy as jnp
from jax import lax
from jax.experimental import pallas as pl
from jax.experimental.pallas import tpu as pltpu
from jax.sharding import PartitionSpec as P

ROUNDS = 2
NS_STEPS = 5


NORM_EPSILON = 1e-06
MOMENTUM_DECAY = 0.9
LEARNING_RATE = 0.5
HIGHEST = lax.Precision.HIGHEST
LANES = 128
EARLY = 2
F32, BF16 = jnp.float32, jnp.bfloat16
SCALARS = pl.BlockSpec(memory_space=pltpu.SMEM)


def two_terms(x):
    high = x.astype(BF16)
    return high, (x - high.astype(F32)).astype(BF16)


def dot(a, b, transposed=False):
    dims = (((1,), (1 if transposed else 0,)), ((), ()))
    return lax.dot_general(a, b, dims, preferred_element_type=F32)


def small_by_large(small, high, low, transposed):
    rows = small.shape[0]
    small_high, small_low = two_terms(small)
    both = dot(jnp.concatenate([small_high, small_low], axis=0), high, transposed)
    return both[:rows] + both[rows:] + dot(small_high, low, transposed)


def dot3(a, b):
    a_high, a_low = two_terms(a)
    b_high, b_low = two_terms(b)
    return dot(
        jnp.concatenate([a_high, a_low, a_high], axis=1),
        jnp.concatenate([b_high, b_high, b_low], axis=0),
    )


def stacked(right):
    right_high, right_low = two_terms(right)
    return jnp.concatenate([right_high, right_high, right_low], axis=0)


def lay_lanes(scratch, value):
    rows = value.shape[0]
    for block in range(value.shape[1] // LANES):
        scratch[block * rows : (block + 1) * rows] = value[:, block * LANES : (block + 1) * LANES]


def read_lanes(scratch, rows):
    blocks = scratch.shape[0] // rows
    return jnp.concatenate([scratch[block * rows : (block + 1) * rows] for block in range(blocks)], axis=1)


def part_at(index, rows):
    return pl.ds(pl.multiple_of(index * rows, 8), rows)


def split_parts(scratch, me, part_refs):
    rows = part_refs[0].shape[0]
    for offset, part_ref in enumerate(part_refs):
        part_ref[...] = scratch[part_at(me ^ offset, rows), :]


def join_parts(scratch, me, part_refs):
    rows = part_refs[0].shape[0]
    for offset, part_ref in enumerate(part_refs):
        scratch[part_at(me ^ offset, rows), :] = part_ref[...]


def sum_of(refs):
    values = [ref[...] for ref in refs]
    while len(values) > 1:
        values = [sum(values[at : at + 2][1:], values[at]) for at in range(0, len(values), 2)]
    return values[0]


def streamed(sources, buffers, sems, picked=lambda k: (k,)):
    step = pl.program_id(0)

    def copies(k):
        return [
            pltpu.make_async_copy(source.at[picked(k)], buffer.at[k], sems.at[which, k])
            for which, (source, buffer) in enumerate(zip(sources, buffers))
        ]

    @pl.when(step == 0)
    def _():
        for k in range(buffers[0].shape[0]):
            for copy in copies(k):
                copy.start()

    for copy in copies(step):
        copy.wait()
    return [buffer[step] for buffer in buffers]


def put_left(left, step, left_refs, per_tp):
    for which, left_ref in enumerate(left_refs):

        @pl.when(step // per_tp == which)
        def _():
            left_ref[...] = left


def first_left_kernel(per_tp, picked, ids_ref, grads_ref, error_ref, query_ref, high_ref, low_ref, *refs):
    left_refs, (grads_buffer, error_buffer, sems) = refs[:-3], refs[-3:]
    grads, error = streamed(
        (grads_ref, error_ref), (grads_buffer, error_buffer), sems, lambda k: (0, picked(k, ids_ref))
    )
    high, low = two_terms(grads.astype(F32) + error)
    high_ref[0] = high
    low_ref[0] = low
    put_left(small_by_large(query_ref[0], high, low, True), pl.program_id(0), left_refs, per_tp)


def left_kernel(per_tp, half, ids_ref, high_ref, low_ref, *refs):
    parts, left_refs, (scratch, current), stream = refs[:-7], refs[-7:-5], refs[-5:-3], refs[-3:]
    step = pl.program_id(0)
    rank = left_refs[0].shape[0]
    rows = current.shape[0]
    lanes = rows * (current.shape[1] // LANES)

    @pl.when(step == 0)
    def _():
        join_parts(scratch, ids_ref[0], parts)
        current[...] = read_lanes(scratch.at[half * lanes : (half + 1) * lanes], rows)

    high, low = streamed((high_ref, low_ref), stream[:2], stream[2])
    own = current[part_at(step, rank), :]
    put_left(small_by_large(own, high, low, True), step, left_refs, per_tp)


def split_kernel(tps, *refs):
    lay_lanes(refs[-1], sum_of(refs[:tps]))


def total_kernel(parts_ref, out_ref):
    summed = sum_of([parts_ref.at[part] for part in range(parts_ref.shape[0])])
    for part in range(parts_ref.shape[0]):
        out_ref[part] = summed


def sum_kernel(scale, *refs):
    summed = sum_of(refs[:-1])
    refs[-1][...] = summed if scale == 1.0 else summed * scale


def mixing(left, rank):
    rows = left.shape[0]
    row_id = lax.broadcasted_iota(jnp.int32, (rows, rows), 0)
    col_id = lax.broadcasted_iota(jnp.int32, (rows, rows), 1)
    same = (row_id // rank) == (col_id // rank)
    eye = (row_id == col_id).astype(F32)
    left_high, left_low = two_terms(left)
    cross = dot(left_high, left_low, True)
    gram = jnp.where(same, dot(left_high, left_high, True) + cross + cross.T, 0.0)
    diagonal = jnp.sum(gram * eye, axis=0, keepdims=True)
    trace = jnp.sum(jnp.where(same, diagonal, 0.0), axis=1, keepdims=True) + NORM_EPSILON
    scale = lax.rsqrt(trace)
    scale = scale * (1.5 - 0.5 * trace * scale * scale)
    gram = gram * (scale * scale)
    step = 1.5 * eye - 0.5 * gram
    mixed = step * scale
    for _ in range(NS_STEPS - 1):
        gram = dot3(dot3(step, gram), step)
        step = 1.5 * eye - 0.5 * gram
        mixed = dot3(step, mixed)
    return mixed


def basis_kernel(rank, left_ref, basis_ref):
    rows = basis_ref.shape[0]
    left = read_lanes(left_ref, rows)
    padded = jnp.concatenate([left, jnp.zeros((-rows % LANES, left.shape[1]), F32)], axis=0)
    basis_ref[...] = dot3(mixing(padded, rank), padded)[:rows]


def right_kernel(per_tp, ids_ref, first_ref, second_ref, high_ref, low_ref, *refs):
    step = pl.program_id(0)
    rank = first_ref.shape[0] // per_tp
    at = part_at(step % per_tp, rank)
    own = jnp.where(step // per_tp == 0, first_ref[at, :], second_ref[at, :])
    refs, stream = refs[:-3], refs[-3:]
    high, low = streamed((high_ref, low_ref), stream[:2], stream[2])
    product_now = small_by_large(own, high, low, False)
    if len(refs) == 1:
        refs[0][...] = product_now
        return
    before_ref, part_refs, (scratch, right) = refs[0], refs[1:-2], refs[-2:]
    right[part_at(step, rank), :] = product_now

    @pl.when(step == pl.num_programs(0) - 1)
    def _():
        lanes = scratch.shape[0] // 2
        lay_lanes(scratch.at[:lanes], before_ref[...])
        lay_lanes(scratch.at[lanes:], right[...])
        split_parts(scratch, ids_ref[0], part_refs)


def rows_of_update(basis_ref, right_ref, scratch, first_unit, unit, per_tp, rank, tp, first_matrix):
    per_matrix = basis_ref.shape[1] // unit
    for u in range(scratch.shape[0] // unit):
        at = first_unit + u
        matrix = at // per_matrix
        slot = ((matrix // per_tp) ^ tp) * per_tp + matrix % per_tp
        lanes = pl.ds(pl.multiple_of((at % per_matrix) * unit, LANES), unit)
        factor = basis_ref[part_at(slot, rank), lanes]
        right = right_ref[part_at(matrix - first_matrix, rank), :]
        scratch[u * unit : (u + 1) * unit] = product(factor, right)


def product(factor, right):
    high, low = two_terms(factor.T)
    return dot(jnp.concatenate([high, low, high], axis=1), stacked(right))


def late_kernel(early, unit, per_tp, rank, ids_ref, basis_ref, *refs):
    query_ref, weights_ref, lanes, approx = refs[-4:]
    late = weights_ref.shape[0]
    part_refs, base_refs = refs[: -4 - late], refs[-4 - late : -4]
    rows = query_ref.shape[0] // 2
    tp = ids_ref[1]
    join_parts(lanes, ids_ref[0], part_refs)
    for half in range(2):
        per_half = lanes.shape[0] // 2
        value = read_lanes(lanes.at[half * per_half : (half + 1) * per_half], rows)
        for which in range(2):
            owner = tp ^ (2 * half + which)
            query_ref[part_at(owner, rows // 2), :] = value[which * (rows // 2) : (which + 1) * (rows // 2)]
    units = approx.shape[0] // unit
    rows_of_update(basis_ref, query_ref, approx, ids_ref[0] * units, unit, per_tp, rank, tp, 0)
    for which in range(late):
        base = base_refs[which][...]
        owner = tp ^ (early + which)
        own = approx[part_at(owner, base.shape[0]), :]
        weights_ref[owner % late] = (base - LEARNING_RATE * own).astype(BF16)


def owner_of(step, rep, replicas):
    half = replicas // 2
    return ((rep ^ (step // half)) + 2 * replicas - 2 * (step % half)) % replicas


def place_kernel(ids_ref, *refs):
    for at, part_ref in enumerate(refs[:-2]):

        @pl.when(pl.program_id(0) == at)
        def _():
            refs[-1][0] = part_ref[...]


def update_kernel(early, per_tp, rank, ids_ref, basis_ref, right_ref, *refs):
    new_error_ref, weights_ref, approx = refs[-3:]
    base_refs, (high_ref, low_ref) = refs[:early], refs[early : early + 2]
    matrix = pl.program_id(1)
    at = part_at(matrix, rank)
    own = product(basis_ref[at, :], right_ref[at, :])
    approx[part_at(matrix, own.shape[0]), :] = own
    new_error_ref[0, 0] = high_ref[0].astype(F32) + low_ref[0].astype(F32) - own

    @pl.when(matrix == per_tp - 1)
    def _():
        replicas, tps, own_rows, _ = weights_ref.shape
        for replica in range(replicas):
            for offset, base_ref in enumerate(base_refs):
                owner = ids_ref[1] ^ offset
                rows = approx[part_at(replica * tps + owner, own_rows), :]
                weights_ref[replica, owner] = (base_ref[replica] - LEARNING_RATE * rows).astype(BF16)


def flat_kernel(unit, per_tp, rank, matrices, ids_ref, basis_ref, near_ref, momentum_ref, master_ref, new_momentum_ref, new_master_ref, approx):
    units = approx.shape[0] // unit
    spans = near_ref.shape[1] // rank
    first_unit = ids_ref[0] * units
    first = jnp.minimum(first_unit // (basis_ref.shape[1] // unit), matrices - spans)
    rows_of_update(basis_ref, near_ref.at[0], approx, first_unit, unit, per_tp, rank, ids_ref[1], first)
    own = approx[part_at(ids_ref[1], momentum_ref.shape[0]), :]
    new_momentum = MOMENTUM_DECAY * momentum_ref[...] + own
    new_momentum_ref[...] = new_momentum
    new_master_ref[...] = master_ref[...] - LEARNING_RATE * new_momentum


def shape(*dims, dtype=F32):
    return jax.ShapeDtypeStruct(dims, dtype)


def grant(mib):
    return pltpu.CompilerParams(vmem_limit_bytes=mib * 2**20)


def whole_call(kernel, name, out_shape, operands, ids=None, scratch=()):
    specs = [pl.BlockSpec(memory_space=pltpu.VMEM)] * len(operands)
    many = isinstance(out_shape, (list, tuple))
    out_spec = pl.BlockSpec(memory_space=pltpu.VMEM)
    moved = sum(4 * x.size for x in operands)
    if ids is not None:
        operands, specs = [ids, *operands], [SCALARS, *specs]
    return pl.pallas_call(
        kernel,
        in_specs=specs,
        out_specs=[out_spec] * len(out_shape) if many else out_spec,
        out_shape=out_shape,
        scratch_shapes=list(scratch),
        compiler_params=grant(12),
        name=name,
        cost_estimate=pl.CostEstimate(flops=moved, bytes_accessed=2 * moved, transcendentals=0),
    )(*operands)


def grid_call(kernel, name, ids, grid, in_specs, out_specs, out_shape, operands, scratch=(), aliases=None, flops=0, moved=0):
    return pl.pallas_call(
        kernel,
        grid_spec=pltpu.PrefetchScalarGridSpec(
            num_scalar_prefetch=1,
            grid=grid,
            in_specs=in_specs,
            out_specs=out_specs,
            scratch_shapes=list(scratch),
        ),
        out_shape=out_shape,
        input_output_aliases=aliases or {},
        compiler_params=grant(60),
        name=name,
        cost_estimate=pl.CostEstimate(flops=flops, bytes_accessed=moved, transcendentals=0),
    )(ids, *operands)


def swap(x, axis, size, offset):
    return lax.ppermute(x, axis, [(index, index ^ offset) for index in range(size)])


def scattered(parts, replicas):
    return [parts[0]] + [swap(parts[offset], "rep", replicas, offset) for offset in range(1, replicas)]


def spread(part, axis, size):
    return [part] + [swap(part, axis, size, offset) for offset in range(1, size)]


def local(grads, error, query, momentum, master):
    replicas, tps = lax.axis_size("rep"), lax.axis_size("tp")
    rep, tp = lax.axis_index("rep"), lax.axis_index("tp")
    ids = jnp.stack([rep, tp]).astype(jnp.int32)
    _, matrices, width, cols = grads.shape
    rank = query.shape[1]
    per_tp = matrices // tps
    per_half = 2 * per_tp
    halves = tps // 2
    tp_rows = per_tp * rank
    left_part = tp_rows * width // LANES // replicas
    right_part = tps * tp_rows * cols // LANES // replicas
    own_rows = momentum.shape[0]
    flops = 2 * 3 * per_half * rank * width * cols
    elements = per_half * width * cols

    def matrix_of(half, k, at):
        return (at[1] ^ (2 * half + k // per_tp)) * per_tp + k % per_tp

    term_spec = pl.BlockSpec((1, width, cols), lambda k, at: (k, 0, 0))
    read_spec = pl.BlockSpec(memory_space=pl.ANY)
    streams = [
        pltpu.VMEM((per_half, width, cols), BF16),
        pltpu.VMEM((per_half, width, cols), BF16),
        pltpu.SemaphoreType.DMA((2, per_half)),
    ]
    term_shape = shape(per_half, width, cols, dtype=BF16)
    left_specs = [
        pl.BlockSpec((rank, width), lambda k, at, which=which: (jnp.clip(k - which * per_tp, 0, per_tp - 1), 0))
        for which in range(2)
    ]
    left_shapes = [shape(tp_rows, width)] * 2

    def whole_spec(*dims):
        return pl.BlockSpec(dims, lambda k, at: (0,) * len(dims))

    terms, lefts = [None] * halves, [None] * tps
    for half in reversed(range(halves)):
        picked = functools.partial(matrix_of, half)
        high, low, *out = grid_call(
            functools.partial(first_left_kernel, per_tp, picked),
            "first_left",
            ids,
            (per_half,),
            [
                read_spec,
                read_spec,
                pl.BlockSpec((1, rank, cols), lambda k, at, picked=picked: (picked(k, at), 0, 0)),
            ],
            [term_spec, term_spec, *left_specs],
            [term_shape, term_shape, *left_shapes],
            (grads, error, query),
            [
                pltpu.VMEM((per_half, width, cols), BF16),
                pltpu.VMEM((per_half, width, cols), F32),
                pltpu.SemaphoreType.DMA((2, per_half)),
            ],
            flops=flops,
            moved=10 * elements,
        )
        terms[half] = (high, low)
        lefts[2 * half : 2 * half + 2] = out

    def base_at(offset, new_values, old_values):
        column = (tp ^ offset) * cols
        piece = lax.dynamic_slice_in_dim(new_values, column, cols, 1)
        piece = piece - (LEARNING_RATE * MOMENTUM_DECAY) * lax.dynamic_slice_in_dim(old_values, column, cols, 1)
        return piece if offset == 0 else swap(piece, "tp", tps, offset)

    base = [base_at(0, master, momentum)]
    gathered = [lax.all_gather(base[0], "rep")]
    for power_pass in range(ROUNDS):
        met = [lefts[0]] + [swap(lefts[offset], "tp", tps, offset) for offset in range(1, tps)]
        parts = whole_call(
            functools.partial(split_kernel, tps), "left_split", shape(left_part * replicas, LANES), met
        )
        if power_pass == 0:
            parts, new_values, old_values = lax.optimization_barrier((parts, master, momentum))
            base += [base_at(offset, new_values, old_values) for offset in range(1, tps)]
            gathered += [lax.all_gather(base[offset], "rep") for offset in range(1, EARLY)]
        parts = parts.reshape(replicas, left_part, LANES)
        parts = lax.all_to_all(parts, "rep", split_axis=0, concat_axis=0, tiled=True)
        parts = whole_call(total_kernel, "left_sum", shape(*parts.shape), [parts])
        parts = lax.all_to_all(parts, "rep", split_axis=0, concat_axis=0, tiled=True)
        basis = whole_call(
            functools.partial(basis_kernel, rank), "basis", shape(tp_rows, width), [parts.reshape(-1, LANES)]
        )
        across = swap(basis, "tp", tps, 2)
        bases = [basis, swap(basis, "tp", tps, 1)]
        before = grid_call(
            functools.partial(right_kernel, per_tp),
            "right_near",
            ids,
            (per_half,),
            [whole_spec(tp_rows, width), whole_spec(tp_rows, width), read_spec, read_spec],
            pl.BlockSpec((rank, cols), lambda k, at: (k, 0)),
            shape(2 * tp_rows, cols),
            (*bases, *terms[0]),
            streams,
            flops=flops,
            moved=4 * elements,
        )
        before, across = lax.optimization_barrier((before, across))
        bases += [across, swap(across, "tp", tps, 1)]
        parts = grid_call(
            functools.partial(right_kernel, per_tp),
            "right_far",
            ids,
            (per_half,),
            [whole_spec(tp_rows, width), whole_spec(tp_rows, width), read_spec, read_spec, whole_spec(2 * tp_rows, cols)],
            [whole_spec(right_part, LANES)] * replicas,
            [shape(right_part, LANES)] * replicas,
            (*bases[2:], *terms[1], before),
            [pltpu.VMEM((right_part * replicas, LANES), F32), pltpu.VMEM((2 * tp_rows, cols), F32), *streams],
            flops=flops,
            moved=4 * elements,
        )
        met = scattered(parts, replicas)
        part = whole_call(functools.partial(sum_kernel, 1.0 / replicas), "right_sum", shape(right_part, LANES), met)
        rights = spread(part, "rep", replicas)
        if power_pass < ROUNDS - 1:
            near_parts = rights
            for half in reversed(range(halves)):
                lefts[2 * half : 2 * half + 2] = grid_call(
                    functools.partial(left_kernel, per_tp, half),
                    "left",
                    ids,
                    (per_half,),
                    [read_spec, read_spec] + [whole_spec(right_part, LANES)] * replicas,
                    left_specs,
                    left_shapes,
                    (*terms[half], *near_parts),
                    [pltpu.VMEM((right_part * replicas, LANES), F32), pltpu.VMEM((2 * tp_rows, cols), F32), *streams],
                    flops=flops,
                    moved=4 * elements,
                )
                if half:
                    far, near_parts = lax.optimization_barrier((lefts[2 * half : 2 * half + 2], rights))
                    lefts[2 * half : 2 * half + 2] = far

    all_bases = jnp.concatenate(bases, axis=0)
    late = tps - EARLY
    rep_rows = tps * own_rows
    unit = math.gcd(rep_rows, width)
    right, block = whole_call(
        functools.partial(late_kernel, EARLY, unit, per_tp, rank),
        "late_rows",
        [shape(matrices * rank, cols), shape(late, own_rows, cols, dtype=BF16)],
        [all_bases, *rights, *base[EARLY:]],
        ids,
        [pltpu.VMEM((right_part * replicas, LANES), F32), pltpu.VMEM((rep_rows, cols), F32)],
    )
    spans = -(-(width - unit + rep_rows) // width)
    first = jnp.minimum(rep * rep_rows // width, matrices - spans)
    near = lax.dynamic_slice_in_dim(right, first * rank, spans * rank, 0)

    def update(half, ids, outs):
        def owner(s, at):
            return at[1] ^ (2 * half + s)

        return grid_call(
            functools.partial(update_kernel, EARLY, per_tp, rank),
            "update",
            ids,
            (2, per_tp),
            [
                pl.BlockSpec((tp_rows, width), lambda s, j, at: (2 * half + s, 0)),
                pl.BlockSpec((tp_rows, cols), lambda s, j, at: (owner(s, at), 0)),
            ]
            + [pl.BlockSpec((replicas // tps, own_rows, cols), lambda s, j, at: (owner(s, at), 0, 0))] * EARLY
            + [pl.BlockSpec((1, width, cols), lambda s, j, at: (s * per_tp + j, 0, 0))] * 2
            + [pl.BlockSpec(memory_space=pl.ANY)] * len(outs),
            [
                pl.BlockSpec((1, 1, width, cols), lambda s, j, at: (0, owner(s, at) * per_tp + j, 0, 0)),
                pl.BlockSpec((replicas // tps, tps, own_rows, cols), lambda s, j, at: (owner(s, at), 0, 0, 0)),
            ],
            [shape(*error.shape), shape(replicas, tps, own_rows, cols, dtype=BF16)],
            (all_bases, right, *gathered, *terms[half], *outs),
            [pltpu.VMEM((per_tp * width, cols), F32)],
            aliases={5 + EARLY + at: at for at in range(len(outs))},
            flops=2 * 3 * rank * error.size // 2,
            moved=6 * error.size,
        )

    def flat_rows(ids, all_bases, near):
        wide = pl.BlockSpec((own_rows, cols), lambda s, at: (0, at[1] ^ s))
        return grid_call(
            functools.partial(flat_kernel, unit, per_tp, rank, matrices),
            "flat_rows",
            ids,
            (tps,),
            [
                whole_spec(matrices * rank, width),
                pl.BlockSpec((1, spans * rank, cols), lambda s, at: (s, 0, 0)),
                wide,
                wide,
            ],
            [wide, wide],
            [shape(*momentum.shape), shape(*master.shape)],
            (all_bases, near, momentum, master),
            [pltpu.VMEM((rep_rows, cols), F32)],
            flops=2 * 3 * rank * momentum.size * tps,
            moved=16 * momentum.size,
        )

    ring = [(index, (index + 2) % replicas) for index in range(replicas)]
    held, beside = [block], []
    stages = replicas // 2
    outs, flat = (), ()
    for stage in range(stages):
        beside.append(swap(held[-1], "rep", replicas, 1))
        if stage < stages - 1:
            held.append(lax.ppermute(held[-1], "rep", ring))
        if stage == 0:
            near = spread(near, "tp", tps)
        if stage < 2:
            outs = tuple(update(stage, ids, outs))
        elif stage == 2:
            flat = flat_rows(ids, all_bases, jnp.stack(near))
        if stage < stages - 1:
            ids, outs, flat, held, beside, near = lax.optimization_barrier((ids, outs, flat, held, beside, near))
    new_momentum, new_master = flat
    new_error, weights = outs
    pieces = [*held, *beside]
    for some in (range(len(pieces) - 1), range(len(pieces) - 1, len(pieces))):
        weights = grid_call(
            place_kernel,
            "place_late",
            ids,
            (len(some),),
            [pl.BlockSpec((late, own_rows, cols), lambda k, at: (0, 0, 0))] * len(some) + [pl.BlockSpec(memory_space=pl.ANY)],
            pl.BlockSpec(
                (1, late, own_rows, cols),
                lambda k, at, some=some: (owner_of(k + some[0], at[0], replicas), (at[1] ^ EARLY) // late, 0, 0),
            ),
            shape(*weights.shape, dtype=BF16),
            (*[pieces[at] for at in some], weights),
            aliases={1 + len(some): 0},
        )
    weights = weights.reshape(matrices, width, cols)
    return (new_error, right.reshape(matrices, rank, cols), new_momentum, new_master, weights)


def plain_orthonormal(factor):
    def gram_of(x):
        return jnp.einsum("krd,ksd->krs", x, x, precision=HIGHEST)

    gram_now = gram_of(factor)
    factor_scale = lax.rsqrt(jnp.trace(gram_now, axis1=1, axis2=2)[:, None, None] + NORM_EPSILON)
    ortho_basis = factor * factor_scale
    gram_now = gram_now * (factor_scale * factor_scale)
    for iteration in range(NS_STEPS):
        if iteration > 0:
            gram_now = gram_of(ortho_basis)
        ortho_basis = 1.5 * ortho_basis - 0.5 * jnp.einsum("krs,ksd->krd", gram_now, ortho_basis, precision=HIGHEST)
    return ortho_basis


def plain_local(grads, error, query, momentum, master):
    corrected = grads[0].astype(F32) + error[0]
    current = query
    replicas = lax.axis_size("rep")
    for _ in range(ROUNDS):
        partial_factor = jnp.einsum("kdf,krf->krd", corrected, current, precision=HIGHEST)
        ortho_basis = plain_orthonormal(lax.psum(partial_factor, ("rep", "tp")))
        partial_query = jnp.einsum("kdf,krd->krf", corrected, ortho_basis, precision=HIGHEST)
        current = lax.psum(partial_query, "rep") / replicas
    approx = jnp.einsum("krd,krf->kdf", ortho_basis, current, precision=HIGHEST)
    new_error = (corrected - approx)[None]
    matrices, width, cols = approx.shape
    block_rows = matrices * width // replicas
    own_block = lax.dynamic_slice_in_dim(
        approx.reshape(matrices * width, cols), lax.axis_index("rep") * block_rows, block_rows, 0
    )
    flat_approx = lax.all_to_all(own_block, "tp", split_axis=0, concat_axis=1, tiled=True)
    new_momentum = MOMENTUM_DECAY * momentum + flat_approx
    new_master = master - LEARNING_RATE * new_momentum
    by_columns = lax.all_to_all(new_master.astype(BF16), "tp", split_axis=1, concat_axis=0, tiled=True)
    weights = lax.all_gather(by_columns, "rep", axis=0, tiled=True).reshape(matrices, width, cols)
    return (new_error, current, new_momentum, new_master, weights)


def divides(mesh, matrices, rank, width, cols):
    replicas, tps = mesh.shape["rep"], mesh.shape["tp"]
    if replicas & (replicas - 1) or tps != 4 or replicas < 8 or matrices % tps or cols % (tps * LANES) or width % LANES:
        return False
    if math.gcd(matrices * width // replicas, width) % LANES:
        return False
    tp_rows = matrices // tps * rank
    tiles = 8 * LANES * replicas
    return tp_rows * width % tiles == 0 and tps * tp_rows * (cols // tps) % tiles == 0


def solution(mesh):
    placed = (
        P("rep", None, None, "tp"),
        P("rep", None, None, "tp"),
        P(None, None, "tp"),
        P(("rep", "tp"), None),
        P(("rep", "tp"), None),
    )

    def step(grads, error, query, momentum, master):
        fits = divides(mesh, grads.shape[1], query.shape[1], grads.shape[2], grads.shape[3])
        return jax.shard_map(
            local if fits else plain_local,
            mesh=mesh,
            in_specs=placed,
            out_specs=(
                P("rep", None, None, "tp"),
                P(None, None, "tp"),
                P(("rep", "tp"), None),
                P(("rep", "tp"), None),
                P(None, None, "tp"),
            ),
            check_vma=False,
        )(grads, error, query, momentum, master)

    return step
```

```python
import functools
import math

import jax
import jax.numpy as jnp
from jax import lax
from jax.experimental import pallas as pl
from jax.experimental.pallas import tpu as pltpu
from jax.sharding import PartitionSpec as P

ROUNDS = 2
NS_STEPS = 5


NORM_EPSILON = 1e-06
MOMENTUM_DECAY = 0.9
LEARNING_RATE = 0.5
HIGHEST = lax.Precision.HIGHEST
LANES = 128
F32, BF16 = jnp.float32, jnp.bfloat16
SCALARS = pl.BlockSpec(memory_space=pltpu.SMEM)


def two_terms(x):
    high = x.astype(BF16)
    return high, (x - high.astype(F32)).astype(BF16)


def dot(a, b, transposed=False):
    dims = (((1,), (1 if transposed else 0,)), ((), ()))
    return lax.dot_general(a, b, dims, preferred_element_type=F32)


def small_by_large(small, high, low, transposed):
    rows = small.shape[0]
    small_high, small_low = two_terms(small)
    both = dot(jnp.concatenate([small_high, small_low], axis=0), high, transposed)
    return both[:rows] + both[rows:] + dot(small_high, low, transposed)


def dot3(a, b):
    a_high, a_low = two_terms(a)
    b_high, b_low = two_terms(b)
    return dot(
        jnp.concatenate([a_high, a_low, a_high], axis=1),
        jnp.concatenate([b_high, b_high, b_low], axis=0),
    )


def stacked(right):
    right_high, right_low = two_terms(right)
    return jnp.concatenate([right_high, right_high, right_low], axis=0)


def lay_lanes(scratch, value):
    rows = value.shape[0]
    for block in range(value.shape[1] // LANES):
        scratch[block * rows : (block + 1) * rows] = value[:, block * LANES : (block + 1) * LANES]


def read_lanes(scratch, rows):
    blocks = scratch.shape[0] // rows
    return jnp.concatenate([scratch[block * rows : (block + 1) * rows] for block in range(blocks)], axis=1)


def part_at(index, rows):
    return pl.ds(pl.multiple_of(index * rows, 8), rows)


def split_parts(scratch, me, part_refs):
    rows = part_refs[0].shape[0]
    for offset, part_ref in enumerate(part_refs):
        part_ref[...] = scratch[part_at(me ^ offset, rows), :]


def join_parts(scratch, me, part_refs):
    rows = part_refs[0].shape[0]
    for offset, part_ref in enumerate(part_refs):
        scratch[part_at(me ^ offset, rows), :] = part_ref[...]


def sum_of(refs):
    values = [ref[...] for ref in refs]
    while len(values) > 1:
        values = [sum(values[at : at + 2][1:], values[at]) for at in range(0, len(values), 2)]
    return values[0]


def put_left(left, step, left_refs, per_tp):
    for which, left_ref in enumerate(left_refs):

        @pl.when(step // per_tp == which)
        def _():
            left_ref[...] = left


def first_left_kernel(per_tp, ids_ref, grads_ref, error_ref, query_ref, high_ref, low_ref, *left_refs):
    high, low = two_terms(grads_ref[0, 0].astype(F32) + error_ref[0, 0])
    high_ref[0] = high
    low_ref[0] = low
    put_left(small_by_large(query_ref[0], high, low, True), pl.program_id(0), left_refs, per_tp)


def left_kernel(per_tp, half, ids_ref, high_ref, low_ref, *refs):
    parts, left_refs, (scratch, current) = refs[:-4], refs[-4:-2], refs[-2:]
    step = pl.program_id(0)
    rank = left_refs[0].shape[0]
    rows = current.shape[0]
    lanes = rows * (current.shape[1] // LANES)

    @pl.when(step == 0)
    def _():
        join_parts(scratch, ids_ref[0], parts)
        current[...] = read_lanes(scratch.at[half * lanes : (half + 1) * lanes], rows)

    own = current[part_at(step, rank), :]
    put_left(small_by_large(own, high_ref[0], low_ref[0], True), step, left_refs, per_tp)


def split_kernel(tps, *refs):
    lay_lanes(refs[-1], sum_of(refs[:tps]))


def total_kernel(parts_ref, out_ref):
    summed = sum_of([parts_ref.at[part] for part in range(parts_ref.shape[0])])
    for part in range(parts_ref.shape[0]):
        out_ref[part] = summed


def sum_kernel(scale, *refs):
    summed = sum_of(refs[:-1])
    refs[-1][...] = summed if scale == 1.0 else summed * scale


def mixing(left, rank):
    rows = left.shape[0]
    row_id = lax.broadcasted_iota(jnp.int32, (rows, rows), 0)
    col_id = lax.broadcasted_iota(jnp.int32, (rows, rows), 1)
    same = (row_id // rank) == (col_id // rank)
    eye = (row_id == col_id).astype(F32)
    left_high, left_low = two_terms(left)
    cross = dot(left_high, left_low, True)
    gram = jnp.where(same, dot(left_high, left_high, True) + cross + cross.T, 0.0)
    diagonal = jnp.sum(gram * eye, axis=0, keepdims=True)
    trace = jnp.sum(jnp.where(same, diagonal, 0.0), axis=1, keepdims=True) + NORM_EPSILON
    scale = lax.rsqrt(trace)
    scale = scale * (1.5 - 0.5 * trace * scale * scale)
    gram = gram * (scale * scale)
    step = 1.5 * eye - 0.5 * gram
    mixed = step * scale
    for _ in range(NS_STEPS - 1):
        gram = dot3(dot3(step, gram), step)
        step = 1.5 * eye - 0.5 * gram
        mixed = dot3(step, mixed)
    return mixed


def basis_kernel(rank, left_ref, basis_ref):
    rows = basis_ref.shape[0]
    left = read_lanes(left_ref, rows)
    padded = jnp.concatenate([left, jnp.zeros((-rows % LANES, left.shape[1]), F32)], axis=0)
    basis_ref[...] = dot3(mixing(padded, rank), padded)[:rows]


def right_kernel(per_tp, ids_ref, first_ref, second_ref, high_ref, low_ref, *refs):
    step = pl.program_id(0)
    rank = first_ref.shape[0] // per_tp
    at = part_at(step % per_tp, rank)
    own = jnp.where(step // per_tp == 0, first_ref[at, :], second_ref[at, :])
    product_now = small_by_large(own, high_ref[0], low_ref[0], False)
    if len(refs) == 1:
        refs[0][...] = product_now
        return
    before_ref, part_refs, (scratch, right) = refs[0], refs[1:-2], refs[-2:]
    right[part_at(step, rank), :] = product_now

    @pl.when(step == pl.num_programs(0) - 1)
    def _():
        lanes = scratch.shape[0] // 2
        lay_lanes(scratch.at[:lanes], before_ref[...])
        lay_lanes(scratch.at[lanes:], right[...])
        split_parts(scratch, ids_ref[0], part_refs)


def rows_of_update(basis_ref, right_ref, scratch, first_unit, unit, per_tp, rank, tp, first_matrix):
    per_matrix = basis_ref.shape[1] // unit
    for u in range(scratch.shape[0] // unit):
        at = first_unit + u
        matrix = at // per_matrix
        slot = ((matrix // per_tp) ^ tp) * per_tp + matrix % per_tp
        lanes = pl.ds(pl.multiple_of((at % per_matrix) * unit, LANES), unit)
        factor = basis_ref[part_at(slot, rank), lanes]
        right = right_ref[part_at(matrix - first_matrix, rank), :]
        scratch[u * unit : (u + 1) * unit] = product(factor, right)


def product(factor, right):
    high, low = two_terms(factor.T)
    return dot(jnp.concatenate([high, low, high], axis=1), stacked(right))


def late_kernel(unit, per_tp, rank, ids_ref, basis_ref, *refs):
    query_ref, *weight_refs, lanes, approx = refs[-5:]
    tps = query_ref.shape[0] // (per_tp * rank)
    part_refs, base_refs = refs[: -5 - tps], refs[-5 - tps : -5]
    rows = query_ref.shape[0] // 2
    tp = ids_ref[1]
    join_parts(lanes, ids_ref[0], part_refs)
    for half in range(2):
        per_half = lanes.shape[0] // 2
        value = read_lanes(lanes.at[half * per_half : (half + 1) * per_half], rows)
        for which in range(2):
            owner = tp ^ (2 * half + which)
            query_ref[part_at(owner, rows // 2), :] = value[which * (rows // 2) : (which + 1) * (rows // 2)]
    units = approx.shape[0] // unit
    rows_of_update(basis_ref, query_ref, approx, ids_ref[0] * units, unit, per_tp, rank, tp, 0)
    for offset, base_ref in enumerate(base_refs):
        at = part_at(tp ^ offset, base_ref.shape[0])
        approx[at, :] = base_ref[...] - LEARNING_RATE * approx[at, :]
    for half, weight_ref in enumerate(weight_refs):
        per_half = weight_ref.shape[0]
        weight_ref[...] = approx[half * per_half : (half + 1) * per_half].astype(BF16)


def owner_of(step, rep, replicas):
    half = replicas // 2
    return ((rep ^ (step // half)) + 2 * replicas - 2 * (step % half)) % replicas


def place_kernel(count, ids_ref, *refs):
    for at, part_ref in enumerate(refs[:count]):

        @pl.when(pl.program_id(0) == at)
        def _():
            refs[-1][0, 0] = part_ref[...]


def update_kernel(rank, ids_ref, basis_ref, right_ref, high_ref, low_ref, *refs):
    at = part_at(pl.program_id(0), rank)
    approx = product(basis_ref[at, :], right_ref[at, :])
    refs[-1][0, 0] = high_ref[0].astype(F32) + low_ref[0].astype(F32) - approx


def flat_kernel(unit, per_tp, rank, matrices, ids_ref, basis_ref, near_ref, momentum_ref, master_ref, new_momentum_ref, new_master_ref, approx):
    units = approx.shape[0] // unit
    spans = near_ref.shape[1] // rank
    first_unit = ids_ref[0] * units
    first = jnp.minimum(first_unit // (basis_ref.shape[1] // unit), matrices - spans)
    rows_of_update(basis_ref, near_ref.at[0], approx, first_unit, unit, per_tp, rank, ids_ref[1], first)
    own = approx[part_at(ids_ref[1], momentum_ref.shape[0]), :]
    new_momentum = MOMENTUM_DECAY * momentum_ref[...] + own
    new_momentum_ref[...] = new_momentum
    new_master_ref[...] = master_ref[...] - LEARNING_RATE * new_momentum


def shape(*dims, dtype=F32):
    return jax.ShapeDtypeStruct(dims, dtype)


def grant(mib):
    return pltpu.CompilerParams(vmem_limit_bytes=mib * 2**20)


def whole_call(kernel, name, out_shape, operands, ids=None, scratch=()):
    specs = [pl.BlockSpec(memory_space=pltpu.VMEM)] * len(operands)
    many = isinstance(out_shape, (list, tuple))
    out_spec = pl.BlockSpec(memory_space=pltpu.VMEM)
    moved = sum(4 * x.size for x in operands)
    if ids is not None:
        operands, specs = [ids, *operands], [SCALARS, *specs]
    return pl.pallas_call(
        kernel,
        in_specs=specs,
        out_specs=[out_spec] * len(out_shape) if many else out_spec,
        out_shape=out_shape,
        scratch_shapes=list(scratch),
        compiler_params=grant(12),
        name=name,
        cost_estimate=pl.CostEstimate(flops=moved, bytes_accessed=2 * moved, transcendentals=0),
    )(*operands)


def grid_call(kernel, name, ids, grid, in_specs, out_specs, out_shape, operands, scratch=(), aliases=None, flops=0, moved=0):
    return pl.pallas_call(
        kernel,
        grid_spec=pltpu.PrefetchScalarGridSpec(
            num_scalar_prefetch=1,
            grid=grid,
            in_specs=in_specs,
            out_specs=out_specs,
            scratch_shapes=list(scratch),
        ),
        out_shape=out_shape,
        input_output_aliases=aliases or {},
        compiler_params=grant(20),
        name=name,
        cost_estimate=pl.CostEstimate(flops=flops, bytes_accessed=moved, transcendentals=0),
    )(ids, *operands)


def swap(x, axis, size, offset):
    return lax.ppermute(x, axis, [(index, index ^ offset) for index in range(size)])


def scattered(parts, replicas):
    return [parts[0]] + [swap(parts[offset], "rep", replicas, offset) for offset in range(1, replicas)]


def spread(part, axis, size):
    return [part] + [swap(part, axis, size, offset) for offset in range(1, size)]


def local(grads, error, query, momentum, master):
    replicas, tps = lax.axis_size("rep"), lax.axis_size("tp")
    rep, tp = lax.axis_index("rep"), lax.axis_index("tp")
    ids = jnp.stack([rep, tp]).astype(jnp.int32)
    _, matrices, width, cols = grads.shape
    rank = query.shape[1]
    per_tp = matrices // tps
    per_half = 2 * per_tp
    halves = tps // 2
    tp_rows = per_tp * rank
    left_part = tp_rows * width // LANES // replicas
    right_part = tps * tp_rows * cols // LANES // replicas
    own_rows = momentum.shape[0]
    flops = 2 * 3 * per_half * rank * width * cols
    elements = per_half * width * cols

    def matrix_of(half, k, at):
        return (at[1] ^ (2 * half + k // per_tp)) * per_tp + k % per_tp

    term_spec = pl.BlockSpec((1, width, cols), lambda k, at: (k, 0, 0))
    term_shape = shape(per_half, width, cols, dtype=BF16)
    left_specs = [
        pl.BlockSpec((rank, width), lambda k, at, which=which: (jnp.clip(k - which * per_tp, 0, per_tp - 1), 0))
        for which in range(2)
    ]
    left_shapes = [shape(tp_rows, width)] * 2

    def whole_spec(*dims):
        return pl.BlockSpec(dims, lambda k, at: (0,) * len(dims))

    terms, lefts = [None] * halves, [None] * tps
    for half in reversed(range(halves)):
        picked = functools.partial(matrix_of, half)
        high, low, *out = grid_call(
            functools.partial(first_left_kernel, per_tp),
            "first_left",
            ids,
            (per_half,),
            [
                pl.BlockSpec((1, 1, width, cols), lambda k, at, picked=picked: (0, picked(k, at), 0, 0)),
                pl.BlockSpec((1, 1, width, cols), lambda k, at, picked=picked: (0, picked(k, at), 0, 0)),
                pl.BlockSpec((1, rank, cols), lambda k, at, picked=picked: (picked(k, at), 0, 0)),
            ],
            [term_spec, term_spec, *left_specs],
            [term_shape, term_shape, *left_shapes],
            (grads, error, query),
            flops=flops,
            moved=10 * elements,
        )
        terms[half] = (high, low)
        lefts[2 * half : 2 * half + 2] = out

    for power_pass in range(ROUNDS):
        met = [lefts[0]] + [swap(lefts[offset], "tp", tps, offset) for offset in range(1, tps)]
        parts = whole_call(
            functools.partial(split_kernel, tps), "left_split", shape(left_part * replicas, LANES), met
        )
        if power_pass == 0:
            parts, new_values, old_values = lax.optimization_barrier((parts, master, momentum))
            base = []
            for offset in range(tps):
                column = (tp ^ offset) * cols
                piece = lax.dynamic_slice_in_dim(new_values, column, cols, 1)
                piece = piece - (LEARNING_RATE * MOMENTUM_DECAY) * lax.dynamic_slice_in_dim(old_values, column, cols, 1)
                base.append(piece if offset == 0 else swap(piece, "tp", tps, offset))
        parts = parts.reshape(replicas, left_part, LANES)
        parts = lax.all_to_all(parts, "rep", split_axis=0, concat_axis=0, tiled=True)
        parts = whole_call(total_kernel, "left_sum", shape(*parts.shape), [parts])
        parts = lax.all_to_all(parts, "rep", split_axis=0, concat_axis=0, tiled=True)
        basis = whole_call(
            functools.partial(basis_kernel, rank), "basis", shape(tp_rows, width), [parts.reshape(-1, LANES)]
        )
        across = swap(basis, "tp", tps, 2)
        bases = [basis, swap(basis, "tp", tps, 1)]
        before = grid_call(
            functools.partial(right_kernel, per_tp),
            "right_near",
            ids,
            (per_half,),
            [whole_spec(tp_rows, width), whole_spec(tp_rows, width), term_spec, term_spec],
            pl.BlockSpec((rank, cols), lambda k, at: (k, 0)),
            shape(2 * tp_rows, cols),
            (*bases, *terms[0]),
            flops=flops,
            moved=4 * elements,
        )
        before, across = lax.optimization_barrier((before, across))
        bases += [across, swap(across, "tp", tps, 1)]
        parts = grid_call(
            functools.partial(right_kernel, per_tp),
            "right_far",
            ids,
            (per_half,),
            [whole_spec(tp_rows, width), whole_spec(tp_rows, width), term_spec, term_spec, whole_spec(2 * tp_rows, cols)],
            [whole_spec(right_part, LANES)] * replicas,
            [shape(right_part, LANES)] * replicas,
            (*bases[2:], *terms[1], before),
            [pltpu.VMEM((right_part * replicas, LANES), F32), pltpu.VMEM((2 * tp_rows, cols), F32)],
            flops=flops,
            moved=4 * elements,
        )
        met = scattered(parts, replicas)
        part = whole_call(functools.partial(sum_kernel, 1.0 / replicas), "right_sum", shape(right_part, LANES), met)
        rights = spread(part, "rep", replicas)
        if power_pass < ROUNDS - 1:
            for half in reversed(range(halves)):
                lefts[2 * half : 2 * half + 2] = grid_call(
                    functools.partial(left_kernel, per_tp, half),
                    "left",
                    ids,
                    (per_half,),
                    [term_spec, term_spec] + [whole_spec(right_part, LANES)] * replicas,
                    left_specs,
                    left_shapes,
                    (*terms[half], *rights),
                    [pltpu.VMEM((right_part * replicas, LANES), F32), pltpu.VMEM((2 * tp_rows, cols), F32)],
                    flops=flops,
                    moved=10 * elements,
                )

    all_bases = jnp.concatenate(bases, axis=0)
    rep_rows = tps * own_rows
    unit = math.gcd(rep_rows, width)
    right, *block = whole_call(
        functools.partial(late_kernel, unit, per_tp, rank),
        "late_rows",
        [shape(matrices * rank, cols)] + [shape(rep_rows // 2, cols, dtype=BF16)] * 2,
        [all_bases, *rights, *base],
        ids,
        [pltpu.VMEM((right_part * replicas, LANES), F32), pltpu.VMEM((rep_rows, cols), F32)],
    )
    spans = -(-(width - unit + rep_rows) // width)
    first = jnp.minimum(rep * rep_rows // width, matrices - spans)
    near = lax.dynamic_slice_in_dim(right, first * rank, spans * rank, 0)

    def update(slot, ids, before):
        half, start = slot // 2, slot % 2 * per_tp
        return grid_call(
            functools.partial(update_kernel, rank),
            "update",
            ids,
            (per_tp,),
            [
                pl.BlockSpec((tp_rows, width), lambda j, at: (slot, 0)),
                pl.BlockSpec((tp_rows, cols), lambda j, at: (at[1] ^ slot, 0)),
                pl.BlockSpec((1, width, cols), lambda j, at: (start + j, 0, 0)),
                pl.BlockSpec((1, width, cols), lambda j, at: (start + j, 0, 0)),
            ]
            + [pl.BlockSpec(memory_space=pl.ANY)] * len(before),
            pl.BlockSpec((1, 1, width, cols), lambda j, at: (0, (at[1] ^ slot) * per_tp + j, 0, 0)),
            shape(*error.shape),
            (all_bases, right, *terms[half], *before),
            aliases={5: 0} if before else None,
            flops=2 * 3 * rank * error.size // tps,
            moved=8 * error.size // tps,
        )

    def place(pieces, ids, before):
        count = len(pieces)

        def where(k, at):
            at_half, step = pieces[-1][1:]
            for index in range(count - 1):
                at_half = jnp.where(k == index, pieces[index][1], at_half)
                step = jnp.where(k == index, pieces[index][2], step)
            return (owner_of(step, at[0], replicas), at_half, 0, 0)

        return grid_call(
            functools.partial(place_kernel, count),
            "place",
            ids,
            (count,),
            [pl.BlockSpec((rep_rows // 2, cols), lambda k, at: (0, 0))] * count
            + [pl.BlockSpec(memory_space=pl.ANY)] * len(before),
            pl.BlockSpec((1, 1, rep_rows // 2, cols), where),
            shape(replicas, 2, rep_rows // 2, cols, dtype=BF16),
            (*[piece[0] for piece in pieces], *before),
            aliases={1 + count: 0} if before else None,
            moved=4 * count * rep_rows * cols,
        )

    def flat_rows(ids, all_bases, near):
        wide = pl.BlockSpec((own_rows, cols), lambda s, at: (0, at[1] ^ s))
        return grid_call(
            functools.partial(flat_kernel, unit, per_tp, rank, matrices),
            "flat_rows",
            ids,
            (tps,),
            [
                whole_spec(matrices * rank, width),
                pl.BlockSpec((1, spans * rank, cols), lambda s, at: (s, 0, 0)),
                wide,
                wide,
            ],
            [wide, wide],
            [shape(*momentum.shape), shape(*master.shape)],
            (all_bases, near, momentum, master),
            [pltpu.VMEM((rep_rows, cols), F32)],
            flops=2 * 3 * rank * momentum.size * tps,
            moved=16 * momentum.size,
        )

    ring = [(index, (index + 2) % replicas) for index in range(replicas)]
    stages = replicas // 2
    held, beside = block, [None, None]
    pieces = [(block[half], half, 0) for half in range(2)]
    errors, flat, weights = (), (), ()
    for stage in range(stages):
        if stage < stages - 1:
            onward = [lax.ppermute(held[half], "rep", ring) for half in range(2)]
            beside = [swap(held[half], "rep", replicas, 1) for half in range(2)]
            arrived = [(onward[half], half, stage + 1) for half in range(2)]
            arrived += [(beside[half], half, stages + stage) for half in range(2)]
        else:
            arrived = [
                (swap(held[0], "rep", replicas, 1), 0, 2 * stages - 1),
                (lax.ppermute(beside[1], "rep", ring), 1, 2 * stages - 1),
            ]
        if stage == 0:
            near = spread(near, "tp", tps)
            for slot in range(tps):
                errors = (update(slot, ids, errors),)
        if stage == 1:
            flat = flat_rows(ids, all_bases, jnp.stack(near))
        if stage > 0:
            weights = (place(pieces, ids, weights),)
        arrays = [piece[0] for piece in arrived]
        if stage < stages - 1:
            ids, errors, flat, weights, near, arrays = lax.optimization_barrier((ids, errors, flat, weights, near, arrays))
            held, beside = arrays[:2], arrays[2:]
        if stage == 0:
            arrived = [(block[half], half, 0) for half in range(2)] + arrived
            arrays = [*block, *arrays]
        pieces = [(array, *piece[1:]) for array, piece in zip(arrays, arrived)]
    weights = place(pieces, ids, weights).reshape(matrices, width, cols)
    (new_error,) = errors
    new_momentum, new_master = flat
    return (new_error, right.reshape(matrices, rank, cols), new_momentum, new_master, weights)


def plain_orthonormal(factor):
    def gram_of(x):
        return jnp.einsum("krd,ksd->krs", x, x, precision=HIGHEST)

    gram_now = gram_of(factor)
    factor_scale = lax.rsqrt(jnp.trace(gram_now, axis1=1, axis2=2)[:, None, None] + NORM_EPSILON)
    ortho_basis = factor * factor_scale
    gram_now = gram_now * (factor_scale * factor_scale)
    for iteration in range(NS_STEPS):
        if iteration > 0:
            gram_now = gram_of(ortho_basis)
        ortho_basis = 1.5 * ortho_basis - 0.5 * jnp.einsum("krs,ksd->krd", gram_now, ortho_basis, precision=HIGHEST)
    return ortho_basis


def plain_local(grads, error, query, momentum, master):
    corrected = grads[0].astype(F32) + error[0]
    current = query
    replicas = lax.axis_size("rep")
    for _ in range(ROUNDS):
        partial_factor = jnp.einsum("kdf,krf->krd", corrected, current, precision=HIGHEST)
        ortho_basis = plain_orthonormal(lax.psum(partial_factor, ("rep", "tp")))
        partial_query = jnp.einsum("kdf,krd->krf", corrected, ortho_basis, precision=HIGHEST)
        current = lax.psum(partial_query, "rep") / replicas
    approx = jnp.einsum("krd,krf->kdf", ortho_basis, current, precision=HIGHEST)
    new_error = (corrected - approx)[None]
    matrices, width, cols = approx.shape
    block_rows = matrices * width // replicas
    own_block = lax.dynamic_slice_in_dim(
        approx.reshape(matrices * width, cols), lax.axis_index("rep") * block_rows, block_rows, 0
    )
    flat_approx = lax.all_to_all(own_block, "tp", split_axis=0, concat_axis=1, tiled=True)
    new_momentum = MOMENTUM_DECAY * momentum + flat_approx
    new_master = master - LEARNING_RATE * new_momentum
    by_columns = lax.all_to_all(new_master.astype(BF16), "tp", split_axis=1, concat_axis=0, tiled=True)
    weights = lax.all_gather(by_columns, "rep", axis=0, tiled=True).reshape(matrices, width, cols)
    return (new_error, current, new_momentum, new_master, weights)


def divides(mesh, matrices, rank, width, cols):
    replicas, tps = mesh.shape["rep"], mesh.shape["tp"]
    if replicas & (replicas - 1) or tps != 4 or replicas < 8 or matrices % tps or cols % (tps * LANES) or width % LANES:
        return False
    if math.gcd(matrices * width // replicas, width) % LANES:
        return False
    tp_rows = matrices // tps * rank
    tiles = 8 * LANES * replicas
    return tp_rows * width % tiles == 0 and tps * tp_rows * (cols // tps) % tiles == 0


def solution(mesh):
    placed = (
        P("rep", None, None, "tp"),
        P("rep", None, None, "tp"),
        P(None, None, "tp"),
        P(("rep", "tp"), None),
        P(("rep", "tp"), None),
    )

    def step(grads, error, query, momentum, master):
        fits = divides(mesh, grads.shape[1], query.shape[1], grads.shape[2], grads.shape[3])
        return jax.shard_map(
            local if fits else plain_local,
            mesh=mesh,
            in_specs=placed,
            out_specs=(
                P("rep", None, None, "tp"),
                P(None, None, "tp"),
                P(("rep", "tp"), None),
                P(("rep", "tp"), None),
                P(None, None, "tp"),
            ),
            check_vma=False,
        )(grads, error, query, momentum, master)

    return step
```

```python
import functools
import math

import jax
import jax.numpy as jnp
from jax import lax
from jax.experimental import pallas as pl
from jax.experimental.pallas import tpu as pltpu
from jax.sharding import PartitionSpec as P

ROUNDS = 2
NS_STEPS = 5


NORM_EPSILON = 1e-06
MOMENTUM_DECAY = 0.9
LEARNING_RATE = 0.5
HIGHEST = lax.Precision.HIGHEST
LANES = 128
F32, BF16 = jnp.float32, jnp.bfloat16
SCALARS = pl.BlockSpec(memory_space=pltpu.SMEM)


def two_terms(x):
    high = x.astype(BF16)
    return high, (x - high.astype(F32)).astype(BF16)


def dot(a, b, transposed=False):
    dims = (((1,), (1 if transposed else 0,)), ((), ()))
    return lax.dot_general(a, b, dims, preferred_element_type=F32)


def small_by_large(small, high, low, transposed):
    rows = small.shape[0]
    small_high, small_low = two_terms(small)
    both = dot(jnp.concatenate([small_high, small_low], axis=0), high, transposed)
    return both[:rows] + both[rows:] + dot(small_high, low, transposed)


def dot3(a, b):
    a_high, a_low = two_terms(a)
    b_high, b_low = two_terms(b)
    return dot(
        jnp.concatenate([a_high, a_low, a_high], axis=1),
        jnp.concatenate([b_high, b_high, b_low], axis=0),
    )


def stacked(right):
    right_high, right_low = two_terms(right)
    return jnp.concatenate([right_high, right_high, right_low], axis=0)


def lay_lanes(scratch, value):
    rows = value.shape[0]
    for block in range(value.shape[1] // LANES):
        scratch[block * rows : (block + 1) * rows] = value[:, block * LANES : (block + 1) * LANES]


def read_lanes(scratch, rows):
    blocks = scratch.shape[0] // rows
    return jnp.concatenate([scratch[block * rows : (block + 1) * rows] for block in range(blocks)], axis=1)


def part_at(index, rows):
    return pl.ds(pl.multiple_of(index * rows, 8), rows)


def split_parts(scratch, me, part_refs):
    rows = part_refs[0].shape[0]
    for offset, part_ref in enumerate(part_refs):
        part_ref[...] = scratch[part_at(me ^ offset, rows), :]


def join_parts(scratch, me, part_refs):
    rows = part_refs[0].shape[0]
    for offset, part_ref in enumerate(part_refs):
        scratch[part_at(me ^ offset, rows), :] = part_ref[...]


def sum_of(refs):
    values = [ref[...] for ref in refs]
    while len(values) > 1:
        values = [sum(values[at : at + 2][1:], values[at]) for at in range(0, len(values), 2)]
    return values[0]


def put_left(left, step, left_refs, per_tp):
    for which, left_ref in enumerate(left_refs):

        @pl.when(step // per_tp == which)
        def _():
            left_ref[...] = left


def first_left_kernel(per_tp, ids_ref, grads_ref, error_ref, query_ref, high_ref, low_ref, *left_refs):
    high, low = two_terms(grads_ref[0, 0].astype(F32) + error_ref[0, 0])
    high_ref[0] = high
    low_ref[0] = low
    put_left(small_by_large(query_ref[0], high, low, True), pl.program_id(0), left_refs, per_tp)


def left_kernel(per_tp, half, ids_ref, high_ref, low_ref, *refs):
    parts, left_refs, (scratch, current) = refs[:-4], refs[-4:-2], refs[-2:]
    step = pl.program_id(0)
    rank = left_refs[0].shape[0]
    rows = current.shape[0]
    lanes = rows * (current.shape[1] // LANES)

    @pl.when(step == 0)
    def _():
        join_parts(scratch, ids_ref[0], parts)
        current[...] = read_lanes(scratch.at[half * lanes : (half + 1) * lanes], rows)

    own = current[part_at(step, rank), :]
    put_left(small_by_large(own, high_ref[0], low_ref[0], True), step, left_refs, per_tp)


def split_kernel(tps, *refs):
    lay_lanes(refs[-1], sum_of(refs[:tps]))


def total_kernel(parts_ref, out_ref):
    summed = sum_of([parts_ref.at[part] for part in range(parts_ref.shape[0])])
    for part in range(parts_ref.shape[0]):
        out_ref[part] = summed


def sum_kernel(scale, *refs):
    summed = sum_of(refs[:-1])
    refs[-1][...] = summed if scale == 1.0 else summed * scale


def mixing(left, rank):
    rows = left.shape[0]
    row_id = lax.broadcasted_iota(jnp.int32, (rows, rows), 0)
    col_id = lax.broadcasted_iota(jnp.int32, (rows, rows), 1)
    same = (row_id // rank) == (col_id // rank)
    eye = (row_id == col_id).astype(F32)
    left_high, left_low = two_terms(left)
    cross = dot(left_high, left_low, True)
    gram = jnp.where(same, dot(left_high, left_high, True) + cross + cross.T, 0.0)
    diagonal = jnp.sum(gram * eye, axis=0, keepdims=True)
    trace = jnp.sum(jnp.where(same, diagonal, 0.0), axis=1, keepdims=True) + NORM_EPSILON
    scale = lax.rsqrt(trace)
    scale = scale * (1.5 - 0.5 * trace * scale * scale)
    gram = gram * (scale * scale)
    step = 1.5 * eye - 0.5 * gram
    mixed = step * scale
    for _ in range(NS_STEPS - 1):
        gram = dot3(dot3(step, gram), step)
        step = 1.5 * eye - 0.5 * gram
        mixed = dot3(step, mixed)
    return mixed


def basis_kernel(rank, left_ref, basis_ref):
    rows = basis_ref.shape[0]
    left = read_lanes(left_ref, rows)
    padded = jnp.concatenate([left, jnp.zeros((-rows % LANES, left.shape[1]), F32)], axis=0)
    basis_ref[...] = dot3(mixing(padded, rank), padded)[:rows]


def right_kernel(per_tp, ids_ref, first_ref, second_ref, high_ref, low_ref, *refs):
    step = pl.program_id(0)
    rank = first_ref.shape[0] // per_tp
    at = part_at(step % per_tp, rank)
    own = jnp.where(step // per_tp == 0, first_ref[at, :], second_ref[at, :])
    product_now = small_by_large(own, high_ref[0], low_ref[0], False)
    if len(refs) == 1:
        refs[0][...] = product_now
        return
    before_ref, part_refs, (scratch, right) = refs[0], refs[1:-2], refs[-2:]
    right[part_at(step, rank), :] = product_now

    @pl.when(step == pl.num_programs(0) - 1)
    def _():
        lanes = scratch.shape[0] // 2
        lay_lanes(scratch.at[:lanes], before_ref[...])
        lay_lanes(scratch.at[lanes:], right[...])
        split_parts(scratch, ids_ref[0], part_refs)


def rows_of_update(basis_ref, right_ref, scratch, first_unit, unit, per_tp, rank, tp, first_matrix):
    per_matrix = basis_ref.shape[1] // unit
    for u in range(scratch.shape[0] // unit):
        at = first_unit + u
        matrix = at // per_matrix
        slot = ((matrix // per_tp) ^ tp) * per_tp + matrix % per_tp
        lanes = pl.ds(pl.multiple_of((at % per_matrix) * unit, LANES), unit)
        factor = basis_ref[part_at(slot, rank), lanes]
        right = right_ref[part_at(matrix - first_matrix, rank), :]
        scratch[u * unit : (u + 1) * unit] = product(factor, right)


def product(factor, right):
    high, low = two_terms(factor.T)
    return dot(jnp.concatenate([high, low, high], axis=1), stacked(right))


def late_kernel(unit, per_tp, rank, ids_ref, basis_ref, *refs):
    query_ref, *weight_refs, lanes, approx = refs[-5:]
    tps = query_ref.shape[0] // (per_tp * rank)
    part_refs, base_refs = refs[: -5 - tps], refs[-5 - tps : -5]
    rows = query_ref.shape[0] // 2
    tp = ids_ref[1]
    join_parts(lanes, ids_ref[0], part_refs)
    for half in range(2):
        per_half = lanes.shape[0] // 2
        value = read_lanes(lanes.at[half * per_half : (half + 1) * per_half], rows)
        for which in range(2):
            owner = tp ^ (2 * half + which)
            query_ref[part_at(owner, rows // 2), :] = value[which * (rows // 2) : (which + 1) * (rows // 2)]
    units = approx.shape[0] // unit
    rows_of_update(basis_ref, query_ref, approx, ids_ref[0] * units, unit, per_tp, rank, tp, 0)
    for offset, base_ref in enumerate(base_refs):
        at = part_at(tp ^ offset, base_ref.shape[0])
        approx[at, :] = base_ref[...] - LEARNING_RATE * approx[at, :]
    for half, weight_ref in enumerate(weight_refs):
        per_half = weight_ref.shape[0]
        weight_ref[...] = approx[half * per_half : (half + 1) * per_half].astype(BF16)


def owner_of(step, rep, replicas):
    half = replicas // 2
    return ((rep ^ (step // half)) + 2 * replicas - 2 * (step % half)) % replicas


def place_kernel(count, ids_ref, *refs):
    for at, part_ref in enumerate(refs[:count]):

        @pl.when(pl.program_id(0) == at)
        def _():
            refs[-1][0, 0] = part_ref[...]


def update_kernel(rank, ids_ref, basis_ref, right_ref, high_ref, low_ref, *refs):
    at = part_at(pl.program_id(0), rank)
    approx = product(basis_ref[at, :], right_ref[at, :])
    refs[-1][0, 0] = high_ref[0].astype(F32) + low_ref[0].astype(F32) - approx


def flat_kernel(unit, per_tp, rank, matrices, ids_ref, basis_ref, near_ref, momentum_ref, master_ref, new_momentum_ref, new_master_ref, approx):
    units = approx.shape[0] // unit
    spans = near_ref.shape[1] // rank
    first_unit = ids_ref[0] * units
    first = jnp.minimum(first_unit // (basis_ref.shape[1] // unit), matrices - spans)
    rows_of_update(basis_ref, near_ref.at[0], approx, first_unit, unit, per_tp, rank, ids_ref[1], first)
    own = approx[part_at(ids_ref[1], momentum_ref.shape[0]), :]
    new_momentum = MOMENTUM_DECAY * momentum_ref[...] + own
    new_momentum_ref[...] = new_momentum
    new_master_ref[...] = master_ref[...] - LEARNING_RATE * new_momentum


def shape(*dims, dtype=F32):
    return jax.ShapeDtypeStruct(dims, dtype)


def grant(mib):
    return pltpu.CompilerParams(vmem_limit_bytes=mib * 2**20)


def whole_call(kernel, name, out_shape, operands, ids=None, scratch=()):
    specs = [pl.BlockSpec(memory_space=pltpu.VMEM)] * len(operands)
    many = isinstance(out_shape, (list, tuple))
    out_spec = pl.BlockSpec(memory_space=pltpu.VMEM)
    moved = sum(4 * x.size for x in operands)
    if ids is not None:
        operands, specs = [ids, *operands], [SCALARS, *specs]
    return pl.pallas_call(
        kernel,
        in_specs=specs,
        out_specs=[out_spec] * len(out_shape) if many else out_spec,
        out_shape=out_shape,
        scratch_shapes=list(scratch),
        compiler_params=grant(12),
        name=name,
        cost_estimate=pl.CostEstimate(flops=moved, bytes_accessed=2 * moved, transcendentals=0),
    )(*operands)


def grid_call(kernel, name, ids, grid, in_specs, out_specs, out_shape, operands, scratch=(), aliases=None, flops=0, moved=0):
    return pl.pallas_call(
        kernel,
        grid_spec=pltpu.PrefetchScalarGridSpec(
            num_scalar_prefetch=1,
            grid=grid,
            in_specs=in_specs,
            out_specs=out_specs,
            scratch_shapes=list(scratch),
        ),
        out_shape=out_shape,
        input_output_aliases=aliases or {},
        compiler_params=grant(20),
        name=name,
        cost_estimate=pl.CostEstimate(flops=flops, bytes_accessed=moved, transcendentals=0),
    )(ids, *operands)


def swap(x, axis, size, offset):
    return lax.ppermute(x, axis, [(index, index ^ offset) for index in range(size)])


def scattered(parts, replicas):
    return [parts[0]] + [swap(parts[offset], "rep", replicas, offset) for offset in range(1, replicas)]


def spread(part, axis, size):
    return [part] + [swap(part, axis, size, offset) for offset in range(1, size)]


def local(grads, error, query, momentum, master):
    replicas, tps = lax.axis_size("rep"), lax.axis_size("tp")
    rep, tp = lax.axis_index("rep"), lax.axis_index("tp")
    ids = jnp.stack([rep, tp]).astype(jnp.int32)
    _, matrices, width, cols = grads.shape
    rank = query.shape[1]
    per_tp = matrices // tps
    per_half = 2 * per_tp
    halves = tps // 2
    tp_rows = per_tp * rank
    left_part = tp_rows * width // LANES // replicas
    right_part = tps * tp_rows * cols // LANES // replicas
    own_rows = momentum.shape[0]
    flops = 2 * 3 * per_half * rank * width * cols
    elements = per_half * width * cols

    def matrix_of(half, k, at):
        return (at[1] ^ (2 * half + k // per_tp)) * per_tp + k % per_tp

    term_spec = pl.BlockSpec((1, width, cols), lambda k, at: (k, 0, 0))
    term_shape = shape(per_half, width, cols, dtype=BF16)
    left_specs = [
        pl.BlockSpec((rank, width), lambda k, at, which=which: (jnp.clip(k - which * per_tp, 0, per_tp - 1), 0))
        for which in range(2)
    ]
    left_shapes = [shape(tp_rows, width)] * 2

    def whole_spec(*dims):
        return pl.BlockSpec(dims, lambda k, at: (0,) * len(dims))

    terms, lefts = [None] * halves, [None] * tps
    for half in reversed(range(halves)):
        picked = functools.partial(matrix_of, half)
        high, low, *out = grid_call(
            functools.partial(first_left_kernel, per_tp),
            "first_left",
            ids,
            (per_half,),
            [
                pl.BlockSpec((1, 1, width, cols), lambda k, at, picked=picked: (0, picked(k, at), 0, 0)),
                pl.BlockSpec((1, 1, width, cols), lambda k, at, picked=picked: (0, picked(k, at), 0, 0)),
                pl.BlockSpec((1, rank, cols), lambda k, at, picked=picked: (picked(k, at), 0, 0)),
            ],
            [term_spec, term_spec, *left_specs],
            [term_shape, term_shape, *left_shapes],
            (grads, error, query),
            flops=flops,
            moved=10 * elements,
        )
        terms[half] = (high, low)
        lefts[2 * half : 2 * half + 2] = out
        ids, _ = lax.optimization_barrier((ids, out[0]))

    for power_pass in range(ROUNDS):
        met = [lefts[0]] + [swap(lefts[offset], "tp", tps, offset) for offset in reversed(range(1, tps))]
        parts = whole_call(
            functools.partial(split_kernel, tps), "left_split", shape(left_part * replicas, LANES), met
        )
        if power_pass == 0:
            parts, new_values, old_values = lax.optimization_barrier((parts, master, momentum))
            base = []
            for offset in range(tps):
                column = (tp ^ offset) * cols
                piece = lax.dynamic_slice_in_dim(new_values, column, cols, 1)
                piece = piece - (LEARNING_RATE * MOMENTUM_DECAY) * lax.dynamic_slice_in_dim(old_values, column, cols, 1)
                base.append(piece if offset == 0 else swap(piece, "tp", tps, offset))
        parts = parts.reshape(replicas, left_part, LANES)
        parts = lax.all_to_all(parts, "rep", split_axis=0, concat_axis=0, tiled=True)
        parts = whole_call(total_kernel, "left_sum", shape(*parts.shape), [parts])
        parts = lax.all_to_all(parts, "rep", split_axis=0, concat_axis=0, tiled=True)
        if power_pass == 0:
            parts, base = lax.optimization_barrier((parts, base))
        basis = whole_call(
            functools.partial(basis_kernel, rank), "basis", shape(tp_rows, width), [parts.reshape(-1, LANES)]
        )
        across = swap(basis, "tp", tps, 2)
        bases = [basis, swap(basis, "tp", tps, 1)]
        before = grid_call(
            functools.partial(right_kernel, per_tp),
            "right_near",
            ids,
            (per_half,),
            [whole_spec(tp_rows, width), whole_spec(tp_rows, width), term_spec, term_spec],
            pl.BlockSpec((rank, cols), lambda k, at: (k, 0)),
            shape(2 * tp_rows, cols),
            (*bases, *terms[0]),
            flops=flops,
            moved=4 * elements,
        )
        before, across = lax.optimization_barrier((before, across))
        bases += [across, swap(across, "tp", tps, 1)]
        parts = grid_call(
            functools.partial(right_kernel, per_tp),
            "right_far",
            ids,
            (per_half,),
            [whole_spec(tp_rows, width), whole_spec(tp_rows, width), term_spec, term_spec, whole_spec(2 * tp_rows, cols)],
            [whole_spec(right_part, LANES)] * replicas,
            [shape(right_part, LANES)] * replicas,
            (*bases[2:], *terms[1], before),
            [pltpu.VMEM((right_part * replicas, LANES), F32), pltpu.VMEM((2 * tp_rows, cols), F32)],
            flops=flops,
            moved=4 * elements,
        )
        met = scattered(parts, replicas)
        part = whole_call(functools.partial(sum_kernel, 1.0 / replicas), "right_sum", shape(right_part, LANES), met)
        rights = spread(part, "rep", replicas)
        if power_pass < ROUNDS - 1:
            for half in reversed(range(halves)):
                lefts[2 * half : 2 * half + 2] = grid_call(
                    functools.partial(left_kernel, per_tp, half),
                    "left",
                    ids,
                    (per_half,),
                    [term_spec, term_spec] + [whole_spec(right_part, LANES)] * replicas,
                    left_specs,
                    left_shapes,
                    (*terms[half], *rights),
                    [pltpu.VMEM((right_part * replicas, LANES), F32), pltpu.VMEM((2 * tp_rows, cols), F32)],
                    flops=flops,
                    moved=10 * elements,
                )

    all_bases = jnp.concatenate(bases, axis=0)
    rep_rows = tps * own_rows
    unit = math.gcd(rep_rows, width)
    right, *block = whole_call(
        functools.partial(late_kernel, unit, per_tp, rank),
        "late_rows",
        [shape(matrices * rank, cols)] + [shape(rep_rows // 2, cols, dtype=BF16)] * 2,
        [all_bases, *rights, *base],
        ids,
        [pltpu.VMEM((right_part * replicas, LANES), F32), pltpu.VMEM((rep_rows, cols), F32)],
    )
    spans = -(-(width - unit + rep_rows) // width)
    first = jnp.minimum(rep * rep_rows // width, matrices - spans)
    near = lax.dynamic_slice_in_dim(right, first * rank, spans * rank, 0)

    def update(slot, ids, before):
        half, start = slot // 2, slot % 2 * per_tp
        return grid_call(
            functools.partial(update_kernel, rank),
            "update",
            ids,
            (per_tp,),
            [
                pl.BlockSpec((tp_rows, width), lambda j, at: (slot, 0)),
                pl.BlockSpec((tp_rows, cols), lambda j, at: (at[1] ^ slot, 0)),
                pl.BlockSpec((1, width, cols), lambda j, at: (start + j, 0, 0)),
                pl.BlockSpec((1, width, cols), lambda j, at: (start + j, 0, 0)),
            ]
            + [pl.BlockSpec(memory_space=pl.ANY)] * len(before),
            pl.BlockSpec((1, 1, width, cols), lambda j, at: (0, (at[1] ^ slot) * per_tp + j, 0, 0)),
            shape(*error.shape),
            (all_bases, right, *terms[half], *before),
            aliases={5: 0} if before else None,
            flops=2 * 3 * rank * error.size // tps,
            moved=8 * error.size // tps,
        )

    def place(pieces, ids, before):
        count = len(pieces)

        def where(k, at):
            at_half, step = pieces[-1][1:]
            for index in range(count - 1):
                at_half = jnp.where(k == index, pieces[index][1], at_half)
                step = jnp.where(k == index, pieces[index][2], step)
            return (owner_of(step, at[0], replicas), at_half, 0, 0)

        return grid_call(
            functools.partial(place_kernel, count),
            "place",
            ids,
            (count,),
            [pl.BlockSpec((rep_rows // 2, cols), lambda k, at: (0, 0))] * count
            + [pl.BlockSpec(memory_space=pl.ANY)] * len(before),
            pl.BlockSpec((1, 1, rep_rows // 2, cols), where),
            shape(replicas, 2, rep_rows // 2, cols, dtype=BF16),
            (*[piece[0] for piece in pieces], *before),
            aliases={1 + count: 0} if before else None,
            moved=4 * count * rep_rows * cols,
        )

    def flat_rows(ids, all_bases, near):
        wide = pl.BlockSpec((own_rows, cols), lambda s, at: (0, at[1] ^ s))
        return grid_call(
            functools.partial(flat_kernel, unit, per_tp, rank, matrices),
            "flat_rows",
            ids,
            (tps,),
            [
                whole_spec(matrices * rank, width),
                pl.BlockSpec((1, spans * rank, cols), lambda s, at: (s, 0, 0)),
                wide,
                wide,
            ],
            [wide, wide],
            [shape(*momentum.shape), shape(*master.shape)],
            (all_bases, near, momentum, master),
            [pltpu.VMEM((rep_rows, cols), F32)],
            flops=2 * 3 * rank * momentum.size * tps,
            moved=16 * momentum.size,
        )

    ring = [(index, (index + 2) % replicas) for index in range(replicas)]
    stages = replicas // 2
    last = 2 * stages - 1
    held, beside = list(block), [None, None]
    pieces = [(block[half], half, 0) for half in range(2)]
    errors, flat, weights = (), (), ()
    jobs = {1: "update update", 2: "update", 3: "update", 4: "place", 6: "place", 2 * stages - 1: "place flat"}
    updated = 0
    for step in range(2 * stages):
        stage, half = step // 2, step % 2
        if stage > 0:
            arrived = (held[half], beside[half])
            ids, errors, flat, weights, arrived = lax.optimization_barrier((ids, errors, flat, weights, arrived))
            held[half], beside[half] = arrived
            pieces += [(held[half], half, stage), (beside[half], half, stages + stage - 1)]
        if stage < stages - 1:
            here = held[half]
            held[half] = lax.ppermute(here, "rep", ring)
            beside[half] = swap(here, "rep", replicas, 1)
        elif half == 0:
            beside[half] = swap(held[half], "rep", replicas, 1)
        else:
            beside[half] = lax.ppermute(beside[half], "rep", ring)
        if step == 2 * stages - 1:
            near = spread(near, "tp", tps)
        for job in jobs.get(step, "").split():
            if job == "update":
                errors = (update(updated, ids, errors),)
                updated += 1
            elif job == "flat":
                flat = flat_rows(ids, all_bases, jnp.stack(near))
            else:
                weights = (place(pieces, ids, weights),)
                pieces = []
    weights = place([(beside[half], half, last) for half in range(2)], ids, weights).reshape(matrices, width, cols)
    (new_error,) = errors
    new_momentum, new_master = flat
    return (new_error, right.reshape(matrices, rank, cols), new_momentum, new_master, weights)


def plain_orthonormal(factor):
    def gram_of(x):
        return jnp.einsum("krd,ksd->krs", x, x, precision=HIGHEST)

    gram_now = gram_of(factor)
    factor_scale = lax.rsqrt(jnp.trace(gram_now, axis1=1, axis2=2)[:, None, None] + NORM_EPSILON)
    ortho_basis = factor * factor_scale
    gram_now = gram_now * (factor_scale * factor_scale)
    for iteration in range(NS_STEPS):
        if iteration > 0:
            gram_now = gram_of(ortho_basis)
        ortho_basis = 1.5 * ortho_basis - 0.5 * jnp.einsum("krs,ksd->krd", gram_now, ortho_basis, precision=HIGHEST)
    return ortho_basis


def plain_local(grads, error, query, momentum, master):
    corrected = grads[0].astype(F32) + error[0]
    current = query
    replicas = lax.axis_size("rep")
    for _ in range(ROUNDS):
        partial_factor = jnp.einsum("kdf,krf->krd", corrected, current, precision=HIGHEST)
        ortho_basis = plain_orthonormal(lax.psum(partial_factor, ("rep", "tp")))
        partial_query = jnp.einsum("kdf,krd->krf", corrected, ortho_basis, precision=HIGHEST)
        current = lax.psum(partial_query, "rep") / replicas
    approx = jnp.einsum("krd,krf->kdf", ortho_basis, current, precision=HIGHEST)
    new_error = (corrected - approx)[None]
    matrices, width, cols = approx.shape
    block_rows = matrices * width // replicas
    own_block = lax.dynamic_slice_in_dim(
        approx.reshape(matrices * width, cols), lax.axis_index("rep") * block_rows, block_rows, 0
    )
    flat_approx = lax.all_to_all(own_block, "tp", split_axis=0, concat_axis=1, tiled=True)
    new_momentum = MOMENTUM_DECAY * momentum + flat_approx
    new_master = master - LEARNING_RATE * new_momentum
    by_columns = lax.all_to_all(new_master.astype(BF16), "tp", split_axis=1, concat_axis=0, tiled=True)
    weights = lax.all_gather(by_columns, "rep", axis=0, tiled=True).reshape(matrices, width, cols)
    return (new_error, current, new_momentum, new_master, weights)


def divides(mesh, matrices, rank, width, cols):
    replicas, tps = mesh.shape["rep"], mesh.shape["tp"]
    if replicas & (replicas - 1) or tps != 4 or replicas < 8 or matrices % tps or cols % (tps * LANES) or width % LANES:
        return False
    if math.gcd(matrices * width // replicas, width) % LANES:
        return False
    tp_rows = matrices // tps * rank
    tiles = 8 * LANES * replicas
    return tp_rows * width % tiles == 0 and tps * tp_rows * (cols // tps) % tiles == 0


def solution(mesh):
    placed = (
        P("rep", None, None, "tp"),
        P("rep", None, None, "tp"),
        P(None, None, "tp"),
        P(("rep", "tp"), None),
        P(("rep", "tp"), None),
    )

    def step(grads, error, query, momentum, master):
        fits = divides(mesh, grads.shape[1], query.shape[1], grads.shape[2], grads.shape[3])
        return jax.shard_map(
            local if fits else plain_local,
            mesh=mesh,
            in_specs=placed,
            out_specs=(
                P("rep", None, None, "tp"),
                P(None, None, "tp"),
                P(("rep", "tp"), None),
                P(("rep", "tp"), None),
                P(None, None, "tp"),
            ),
            check_vma=False,
        )(grads, error, query, momentum, master)

    return step
```

```python
import functools
import math

import jax
import jax.numpy as jnp
from jax import lax
from jax.experimental import pallas as pl
from jax.experimental.pallas import tpu as pltpu
from jax.sharding import PartitionSpec as P

ROUNDS = 2
NS_STEPS = 5


NORM_EPSILON = 1e-06
MOMENTUM_DECAY = 0.9
LEARNING_RATE = 0.5
HIGHEST = lax.Precision.HIGHEST
LANES = 128
F32, BF16 = jnp.float32, jnp.bfloat16
SCALARS = pl.BlockSpec(memory_space=pltpu.SMEM)


def two_terms(x):
    high = x.astype(BF16)
    return high, (x - high.astype(F32)).astype(BF16)


def dot(a, b, transposed=False):
    dims = (((1,), (1 if transposed else 0,)), ((), ()))
    return lax.dot_general(a, b, dims, preferred_element_type=F32)


def small_by_large(small, high, low, transposed):
    rows = small.shape[0]
    small_high, small_low = two_terms(small)
    both = dot(jnp.concatenate([small_high, small_low], axis=0), high, transposed)
    return both[:rows] + both[rows:] + dot(small_high, low, transposed)


def dot3(a, b):
    a_high, a_low = two_terms(a)
    b_high, b_low = two_terms(b)
    return dot(
        jnp.concatenate([a_high, a_low, a_high], axis=1),
        jnp.concatenate([b_high, b_high, b_low], axis=0),
    )


def stacked(right):
    right_high, right_low = two_terms(right)
    return jnp.concatenate([right_high, right_high, right_low], axis=0)


def lay_lanes(scratch, value):
    rows = value.shape[0]
    for block in range(value.shape[1] // LANES):
        scratch[block * rows : (block + 1) * rows] = value[:, block * LANES : (block + 1) * LANES]


def read_lanes(scratch, rows):
    blocks = scratch.shape[0] // rows
    return jnp.concatenate([scratch[block * rows : (block + 1) * rows] for block in range(blocks)], axis=1)


def part_at(index, rows):
    return pl.ds(pl.multiple_of(index * rows, 8), rows)


def split_parts(scratch, me, part_refs):
    rows = part_refs[0].shape[0]
    for offset, part_ref in enumerate(part_refs):
        part_ref[...] = scratch[part_at(me ^ offset, rows), :]


def join_parts(scratch, me, part_refs):
    rows = part_refs[0].shape[0]
    for offset, part_ref in enumerate(part_refs):
        scratch[part_at(me ^ offset, rows), :] = part_ref[...]


def sum_of(refs):
    values = [ref[...] for ref in refs]
    while len(values) > 1:
        values = [sum(values[at : at + 2][1:], values[at]) for at in range(0, len(values), 2)]
    return values[0]


def put_left(left, step, left_refs, per_tp):
    for which, left_ref in enumerate(left_refs):

        @pl.when(step // per_tp == which)
        def _():
            left_ref[...] = left


def first_left_kernel(per_tp, picked, ids_ref, grads_ref, error_ref, query_ref, high_ref, low_ref, *refs):
    left_refs, (grads_buffer, error_buffer, sems) = refs[:-3], refs[-3:]
    step = pl.program_id(0)

    def copies(k):
        matrix = picked(k, ids_ref)
        return [
            pltpu.make_async_copy(source.at[0, matrix], buffer.at[k], sems.at[which, k])
            for which, (source, buffer) in enumerate(((grads_ref, grads_buffer), (error_ref, error_buffer)))
        ]

    @pl.when(step == 0)
    def _():
        for k in range(grads_buffer.shape[0]):
            for copy in copies(k):
                copy.start()

    for copy in copies(step):
        copy.wait()
    high, low = two_terms(grads_buffer[step].astype(F32) + error_buffer[step])
    high_ref[0] = high
    low_ref[0] = low
    put_left(small_by_large(query_ref[0], high, low, True), step, left_refs, per_tp)


def left_kernel(per_tp, half, ids_ref, high_ref, low_ref, *refs):
    parts, left_refs, (scratch, current) = refs[:-4], refs[-4:-2], refs[-2:]
    step = pl.program_id(0)
    rank = left_refs[0].shape[0]
    rows = current.shape[0]
    lanes = rows * (current.shape[1] // LANES)

    @pl.when(step == 0)
    def _():
        join_parts(scratch, ids_ref[0], parts)
        current[...] = read_lanes(scratch.at[half * lanes : (half + 1) * lanes], rows)

    own = current[part_at(step, rank), :]
    put_left(small_by_large(own, high_ref[0], low_ref[0], True), step, left_refs, per_tp)


def split_kernel(tps, *refs):
    lay_lanes(refs[-1], sum_of(refs[:tps]))


def total_kernel(parts_ref, out_ref):
    summed = sum_of([parts_ref.at[part] for part in range(parts_ref.shape[0])])
    for part in range(parts_ref.shape[0]):
        out_ref[part] = summed


def sum_kernel(scale, *refs):
    summed = sum_of(refs[:-1])
    refs[-1][...] = summed if scale == 1.0 else summed * scale


def mixing(left, rank):
    rows = left.shape[0]
    row_id = lax.broadcasted_iota(jnp.int32, (rows, rows), 0)
    col_id = lax.broadcasted_iota(jnp.int32, (rows, rows), 1)
    same = (row_id // rank) == (col_id // rank)
    eye = (row_id == col_id).astype(F32)
    left_high, left_low = two_terms(left)
    cross = dot(left_high, left_low, True)
    gram = jnp.where(same, dot(left_high, left_high, True) + cross + cross.T, 0.0)
    diagonal = jnp.sum(gram * eye, axis=0, keepdims=True)
    trace = jnp.sum(jnp.where(same, diagonal, 0.0), axis=1, keepdims=True) + NORM_EPSILON
    scale = lax.rsqrt(trace)
    scale = scale * (1.5 - 0.5 * trace * scale * scale)
    gram = gram * (scale * scale)
    step = 1.5 * eye - 0.5 * gram
    mixed = step * scale
    for _ in range(NS_STEPS - 1):
        gram = dot3(dot3(step, gram), step)
        step = 1.5 * eye - 0.5 * gram
        mixed = dot3(step, mixed)
    return mixed


def basis_kernel(rank, left_ref, basis_ref):
    rows = basis_ref.shape[0]
    left = read_lanes(left_ref, rows)
    padded = jnp.concatenate([left, jnp.zeros((-rows % LANES, left.shape[1]), F32)], axis=0)
    basis_ref[...] = dot3(mixing(padded, rank), padded)[:rows]


def right_kernel(per_tp, ids_ref, first_ref, second_ref, high_ref, low_ref, *refs):
    step = pl.program_id(0)
    rank = first_ref.shape[0] // per_tp
    at = part_at(step % per_tp, rank)
    own = jnp.where(step // per_tp == 0, first_ref[at, :], second_ref[at, :])
    product_now = small_by_large(own, high_ref[0], low_ref[0], False)
    if len(refs) == 1:
        refs[0][...] = product_now
        return
    before_ref, part_refs, (scratch, right) = refs[0], refs[1:-2], refs[-2:]
    right[part_at(step, rank), :] = product_now

    @pl.when(step == pl.num_programs(0) - 1)
    def _():
        lanes = scratch.shape[0] // 2
        lay_lanes(scratch.at[:lanes], before_ref[...])
        lay_lanes(scratch.at[lanes:], right[...])
        split_parts(scratch, ids_ref[0], part_refs)


def rows_of_update(basis_ref, right_ref, scratch, first_unit, unit, per_tp, rank, tp, first_matrix):
    per_matrix = basis_ref.shape[1] // unit
    for u in range(scratch.shape[0] // unit):
        at = first_unit + u
        matrix = at // per_matrix
        slot = ((matrix // per_tp) ^ tp) * per_tp + matrix % per_tp
        lanes = pl.ds(pl.multiple_of((at % per_matrix) * unit, LANES), unit)
        factor = basis_ref[part_at(slot, rank), lanes]
        right = right_ref[part_at(matrix - first_matrix, rank), :]
        scratch[u * unit : (u + 1) * unit] = product(factor, right)


def product(factor, right):
    high, low = two_terms(factor.T)
    return dot(jnp.concatenate([high, low, high], axis=1), stacked(right))


def late_kernel(unit, per_tp, rank, ids_ref, basis_ref, *refs):
    query_ref, *weight_refs, lanes, approx = refs[-5:]
    tps = query_ref.shape[0] // (per_tp * rank)
    part_refs, base_refs = refs[: -5 - tps], refs[-5 - tps : -5]
    rows = query_ref.shape[0] // 2
    tp = ids_ref[1]
    join_parts(lanes, ids_ref[0], part_refs)
    for half in range(2):
        per_half = lanes.shape[0] // 2
        value = read_lanes(lanes.at[half * per_half : (half + 1) * per_half], rows)
        for which in range(2):
            owner = tp ^ (2 * half + which)
            query_ref[part_at(owner, rows // 2), :] = value[which * (rows // 2) : (which + 1) * (rows // 2)]
    units = approx.shape[0] // unit
    rows_of_update(basis_ref, query_ref, approx, ids_ref[0] * units, unit, per_tp, rank, tp, 0)
    for offset, base_ref in enumerate(base_refs):
        at = part_at(tp ^ offset, base_ref.shape[0])
        approx[at, :] = base_ref[...] - LEARNING_RATE * approx[at, :]
    for half, weight_ref in enumerate(weight_refs):
        per_half = weight_ref.shape[0]
        weight_ref[...] = approx[half * per_half : (half + 1) * per_half].astype(BF16)


def owner_of(step, rep, replicas):
    half = replicas // 2
    return ((rep ^ (step // half)) + 2 * replicas - 2 * (step % half)) % replicas


def place_kernel(count, ids_ref, *refs):
    for at, part_ref in enumerate(refs[:count]):

        @pl.when(pl.program_id(0) == at)
        def _():
            refs[-1][0, 0] = part_ref[...]


def update_kernel(rank, ids_ref, basis_ref, right_ref, high_ref, low_ref, *refs):
    at = part_at(pl.program_id(0), rank)
    approx = product(basis_ref[at, :], right_ref[at, :])
    refs[-1][0, 0] = high_ref[0].astype(F32) + low_ref[0].astype(F32) - approx


def flat_kernel(unit, per_tp, rank, matrices, ids_ref, basis_ref, near_ref, momentum_ref, master_ref, new_momentum_ref, new_master_ref, approx):
    units = approx.shape[0] // unit
    spans = near_ref.shape[1] // rank
    first_unit = ids_ref[0] * units
    first = jnp.minimum(first_unit // (basis_ref.shape[1] // unit), matrices - spans)
    rows_of_update(basis_ref, near_ref.at[0], approx, first_unit, unit, per_tp, rank, ids_ref[1], first)
    own = approx[part_at(ids_ref[1], momentum_ref.shape[0]), :]
    new_momentum = MOMENTUM_DECAY * momentum_ref[...] + own
    new_momentum_ref[...] = new_momentum
    new_master_ref[...] = master_ref[...] - LEARNING_RATE * new_momentum


def shape(*dims, dtype=F32):
    return jax.ShapeDtypeStruct(dims, dtype)


def grant(mib):
    return pltpu.CompilerParams(vmem_limit_bytes=mib * 2**20)


def whole_call(kernel, name, out_shape, operands, ids=None, scratch=()):
    specs = [pl.BlockSpec(memory_space=pltpu.VMEM)] * len(operands)
    many = isinstance(out_shape, (list, tuple))
    out_spec = pl.BlockSpec(memory_space=pltpu.VMEM)
    moved = sum(4 * x.size for x in operands)
    if ids is not None:
        operands, specs = [ids, *operands], [SCALARS, *specs]
    return pl.pallas_call(
        kernel,
        in_specs=specs,
        out_specs=[out_spec] * len(out_shape) if many else out_spec,
        out_shape=out_shape,
        scratch_shapes=list(scratch),
        compiler_params=grant(12),
        name=name,
        cost_estimate=pl.CostEstimate(flops=moved, bytes_accessed=2 * moved, transcendentals=0),
    )(*operands)


def grid_call(kernel, name, ids, grid, in_specs, out_specs, out_shape, operands, scratch=(), aliases=None, flops=0, moved=0, mib=14):
    return pl.pallas_call(
        kernel,
        grid_spec=pltpu.PrefetchScalarGridSpec(
            num_scalar_prefetch=1,
            grid=grid,
            in_specs=in_specs,
            out_specs=out_specs,
            scratch_shapes=list(scratch),
        ),
        out_shape=out_shape,
        input_output_aliases=aliases or {},
        compiler_params=grant(mib),
        name=name,
        cost_estimate=pl.CostEstimate(flops=flops, bytes_accessed=moved, transcendentals=0),
    )(ids, *operands)


def swap(x, axis, size, offset):
    return lax.ppermute(x, axis, [(index, index ^ offset) for index in range(size)])


def scattered(parts, replicas):
    return [parts[0]] + [swap(parts[offset], "rep", replicas, offset) for offset in range(1, replicas)]


def spread(part, axis, size):
    return [part] + [swap(part, axis, size, offset) for offset in range(1, size)]


def local(grads, error, query, momentum, master):
    replicas, tps = lax.axis_size("rep"), lax.axis_size("tp")
    rep, tp = lax.axis_index("rep"), lax.axis_index("tp")
    ids = jnp.stack([rep, tp]).astype(jnp.int32)
    _, matrices, width, cols = grads.shape
    rank = query.shape[1]
    per_tp = matrices // tps
    per_half = 2 * per_tp
    halves = tps // 2
    tp_rows = per_tp * rank
    left_part = tp_rows * width // LANES // replicas
    right_part = tps * tp_rows * cols // LANES // replicas
    own_rows = momentum.shape[0]
    flops = 2 * 3 * per_half * rank * width * cols
    elements = per_half * width * cols

    def matrix_of(half, k, at):
        return (at[1] ^ (2 * half + k // per_tp)) * per_tp + k % per_tp

    term_spec = pl.BlockSpec((1, width, cols), lambda k, at: (k, 0, 0))
    term_shape = shape(per_half, width, cols, dtype=BF16)
    left_specs = [
        pl.BlockSpec((rank, width), lambda k, at, which=which: (jnp.clip(k - which * per_tp, 0, per_tp - 1), 0))
        for which in range(2)
    ]
    left_shapes = [shape(tp_rows, width)] * 2

    def whole_spec(*dims):
        return pl.BlockSpec(dims, lambda k, at: (0,) * len(dims))

    terms, lefts = [None] * halves, [None] * tps
    for half in reversed(range(halves)):
        picked = functools.partial(matrix_of, half)
        high, low, *out = grid_call(
            functools.partial(first_left_kernel, per_tp, picked),
            "first_left",
            ids,
            (per_half,),
            [
                pl.BlockSpec(memory_space=pltpu.HBM),
                pl.BlockSpec(memory_space=pltpu.HBM),
                pl.BlockSpec((1, rank, cols), lambda k, at, picked=picked: (picked(k, at), 0, 0)),
            ],
            [term_spec, term_spec, *left_specs],
            [term_shape, term_shape, *left_shapes],
            (grads, error, query),
            [
                pltpu.VMEM((per_half, width, cols), BF16),
                pltpu.VMEM((per_half, width, cols), F32),
                pltpu.SemaphoreType.DMA((2, per_half)),
            ],
            mib=26,
            flops=flops,
            moved=10 * elements,
        )
        terms[half] = (high, low)
        lefts[2 * half : 2 * half + 2] = out
        ids, _ = lax.optimization_barrier((ids, out[0]))

    base = []
    for power_pass in range(ROUNDS):
        met = [lefts[0]] + [swap(lefts[offset], "tp", tps, offset) for offset in reversed(range(1, tps))]
        parts = whole_call(
            functools.partial(split_kernel, tps), "left_split", shape(left_part * replicas, LANES), met
        )
        parts, new_values, old_values = lax.optimization_barrier((parts, master, momentum))
        some = []
        for offset in range(3 * power_pass, 3 + power_pass):
            column = (tp ^ offset) * cols
            piece = lax.dynamic_slice_in_dim(new_values, column, cols, 1)
            piece = piece - (LEARNING_RATE * MOMENTUM_DECAY) * lax.dynamic_slice_in_dim(old_values, column, cols, 1)
            some.append(piece if offset == 0 else swap(piece, "tp", tps, offset))
        parts = parts.reshape(replicas, left_part, LANES)
        parts = lax.all_to_all(parts, "rep", split_axis=0, concat_axis=0, tiled=True)
        parts = whole_call(total_kernel, "left_sum", shape(*parts.shape), [parts])
        parts = lax.all_to_all(parts, "rep", split_axis=0, concat_axis=0, tiled=True)
        parts, some = lax.optimization_barrier((parts, some))
        base += some
        basis = whole_call(
            functools.partial(basis_kernel, rank), "basis", shape(tp_rows, width), [parts.reshape(-1, LANES)]
        )
        across = swap(basis, "tp", tps, 2)
        bases = [basis, swap(basis, "tp", tps, 1)]
        before = grid_call(
            functools.partial(right_kernel, per_tp),
            "right_near",
            ids,
            (per_half,),
            [whole_spec(tp_rows, width), whole_spec(tp_rows, width), term_spec, term_spec],
            pl.BlockSpec((rank, cols), lambda k, at: (k, 0)),
            shape(2 * tp_rows, cols),
            (*bases, *terms[0]),
            flops=flops,
            moved=4 * elements,
        )
        before, across = lax.optimization_barrier((before, across))
        bases += [across, swap(across, "tp", tps, 1)]
        parts = grid_call(
            functools.partial(right_kernel, per_tp),
            "right_far",
            ids,
            (per_half,),
            [whole_spec(tp_rows, width), whole_spec(tp_rows, width), term_spec, term_spec, whole_spec(2 * tp_rows, cols)],
            [whole_spec(right_part, LANES)] * replicas,
            [shape(right_part, LANES)] * replicas,
            (*bases[2:], *terms[1], before),
            [pltpu.VMEM((right_part * replicas, LANES), F32), pltpu.VMEM((2 * tp_rows, cols), F32)],
            flops=flops,
            moved=4 * elements,
        )
        met = scattered(parts, replicas)
        part = whole_call(functools.partial(sum_kernel, 1.0 / replicas), "right_sum", shape(right_part, LANES), met)
        rights = spread(part, "rep", replicas)
        if power_pass < ROUNDS - 1:
            for half in reversed(range(halves)):
                lefts[2 * half : 2 * half + 2] = grid_call(
                    functools.partial(left_kernel, per_tp, half),
                    "left",
                    ids,
                    (per_half,),
                    [term_spec, term_spec] + [whole_spec(right_part, LANES)] * replicas,
                    left_specs,
                    left_shapes,
                    (*terms[half], *rights),
                    [pltpu.VMEM((right_part * replicas, LANES), F32), pltpu.VMEM((2 * tp_rows, cols), F32)],
                    flops=flops,
                    moved=10 * elements,
                )

    all_bases = jnp.concatenate(bases, axis=0)
    rep_rows = tps * own_rows
    unit = math.gcd(rep_rows, width)
    right, *block = whole_call(
        functools.partial(late_kernel, unit, per_tp, rank),
        "late_rows",
        [shape(matrices * rank, cols)] + [shape(rep_rows // 2, cols, dtype=BF16)] * 2,
        [all_bases, *rights, *base],
        ids,
        [pltpu.VMEM((right_part * replicas, LANES), F32), pltpu.VMEM((rep_rows, cols), F32)],
    )
    spans = -(-(width - unit + rep_rows) // width)
    first = jnp.minimum(rep * rep_rows // width, matrices - spans)
    near = lax.dynamic_slice_in_dim(right, first * rank, spans * rank, 0)

    def update(slot, ids, before):
        half, start = slot // 2, slot % 2 * per_tp
        return grid_call(
            functools.partial(update_kernel, rank),
            "update",
            ids,
            (per_tp,),
            [
                pl.BlockSpec((tp_rows, width), lambda j, at: (slot, 0)),
                pl.BlockSpec((tp_rows, cols), lambda j, at: (at[1] ^ slot, 0)),
                pl.BlockSpec((1, width, cols), lambda j, at: (start + j, 0, 0)),
                pl.BlockSpec((1, width, cols), lambda j, at: (start + j, 0, 0)),
            ]
            + [pl.BlockSpec(memory_space=pl.ANY)] * len(before),
            pl.BlockSpec((1, 1, width, cols), lambda j, at: (0, (at[1] ^ slot) * per_tp + j, 0, 0)),
            shape(*error.shape),
            (all_bases, right, *terms[half], *before),
            aliases={5: 0} if before else None,
            flops=2 * 3 * rank * error.size // tps,
            moved=8 * error.size // tps,
        )

    def place(pieces, ids, before):
        count = len(pieces)

        def where(k, at):
            at_half, step = pieces[-1][1:]
            for index in range(count - 1):
                at_half = jnp.where(k == index, pieces[index][1], at_half)
                step = jnp.where(k == index, pieces[index][2], step)
            return (owner_of(step, at[0], replicas), at_half, 0, 0)

        return grid_call(
            functools.partial(place_kernel, count),
            "place",
            ids,
            (count,),
            [pl.BlockSpec((rep_rows // 2, cols), lambda k, at: (0, 0))] * count
            + [pl.BlockSpec(memory_space=pl.ANY)] * len(before),
            pl.BlockSpec((1, 1, rep_rows // 2, cols), where),
            shape(replicas, 2, rep_rows // 2, cols, dtype=BF16),
            (*[piece[0] for piece in pieces], *before),
            aliases={1 + count: 0} if before else None,
            moved=4 * count * rep_rows * cols,
        )

    def flat_rows(ids, all_bases, near):
        wide = pl.BlockSpec((own_rows, cols), lambda s, at: (0, at[1] ^ s))
        return grid_call(
            functools.partial(flat_kernel, unit, per_tp, rank, matrices),
            "flat_rows",
            ids,
            (tps,),
            [
                whole_spec(matrices * rank, width),
                pl.BlockSpec((1, spans * rank, cols), lambda s, at: (s, 0, 0)),
                wide,
                wide,
            ],
            [wide, wide],
            [shape(*momentum.shape), shape(*master.shape)],
            (all_bases, near, momentum, master),
            [pltpu.VMEM((rep_rows, cols), F32)],
            flops=2 * 3 * rank * momentum.size * tps,
            moved=16 * momentum.size,
        )

    ring = [(index, (index + 2) % replicas) for index in range(replicas)]
    stages = replicas // 2
    last = 2 * stages - 1
    held, beside = list(block), [None, None]
    pieces = [(block[half], half, 0) for half in range(2)]
    errors, flat, weights = (), (), ()
    jobs = {1: "update update", 2: "update", 3: "update", 4: "flat", 5: "place", 2 * stages - 2: "place", 2 * stages - 1: "place"}
    near = spread(near, "tp", tps)
    updated = 0
    for step in range(2 * stages):
        stage, half = step // 2, step % 2
        if stage > 0:
            arrived = (held[half], beside[half])
            ids, errors, flat, weights, near, arrived = lax.optimization_barrier((ids, errors, flat, weights, near, arrived))
            held[half], beside[half] = arrived
            pieces += [(held[half], half, stage), (beside[half], half, stages + stage - 1)]
        if stage < stages - 1:
            here = held[half]
            held[half] = lax.ppermute(here, "rep", ring)
            beside[half] = swap(here, "rep", replicas, 1)
        elif half == 0:
            beside[half] = swap(held[half], "rep", replicas, 1)
        else:
            beside[half] = lax.ppermute(beside[half], "rep", ring)
        for job in jobs.get(step, "").split():
            if job == "update":
                errors = (update(updated, ids, errors),)
                updated += 1
            elif job == "flat":
                flat = flat_rows(ids, all_bases, jnp.stack(near))
            else:
                weights = (place(pieces, ids, weights),)
                pieces = []
    weights = place([(beside[half], half, last) for half in range(2)], ids, weights).reshape(matrices, width, cols)
    (new_error,) = errors
    new_momentum, new_master = flat
    return (new_error, right.reshape(matrices, rank, cols), new_momentum, new_master, weights)


def plain_orthonormal(factor):
    def gram_of(x):
        return jnp.einsum("krd,ksd->krs", x, x, precision=HIGHEST)

    gram_now = gram_of(factor)
    factor_scale = lax.rsqrt(jnp.trace(gram_now, axis1=1, axis2=2)[:, None, None] + NORM_EPSILON)
    ortho_basis = factor * factor_scale
    gram_now = gram_now * (factor_scale * factor_scale)
    for iteration in range(NS_STEPS):
        if iteration > 0:
            gram_now = gram_of(ortho_basis)
        ortho_basis = 1.5 * ortho_basis - 0.5 * jnp.einsum("krs,ksd->krd", gram_now, ortho_basis, precision=HIGHEST)
    return ortho_basis


def plain_local(grads, error, query, momentum, master):
    corrected = grads[0].astype(F32) + error[0]
    current = query
    replicas = lax.axis_size("rep")
    for _ in range(ROUNDS):
        partial_factor = jnp.einsum("kdf,krf->krd", corrected, current, precision=HIGHEST)
        ortho_basis = plain_orthonormal(lax.psum(partial_factor, ("rep", "tp")))
        partial_query = jnp.einsum("kdf,krd->krf", corrected, ortho_basis, precision=HIGHEST)
        current = lax.psum(partial_query, "rep") / replicas
    approx = jnp.einsum("krd,krf->kdf", ortho_basis, current, precision=HIGHEST)
    new_error = (corrected - approx)[None]
    matrices, width, cols = approx.shape
    block_rows = matrices * width // replicas
    own_block = lax.dynamic_slice_in_dim(
        approx.reshape(matrices * width, cols), lax.axis_index("rep") * block_rows, block_rows, 0
    )
    flat_approx = lax.all_to_all(own_block, "tp", split_axis=0, concat_axis=1, tiled=True)
    new_momentum = MOMENTUM_DECAY * momentum + flat_approx
    new_master = master - LEARNING_RATE * new_momentum
    by_columns = lax.all_to_all(new_master.astype(BF16), "tp", split_axis=1, concat_axis=0, tiled=True)
    weights = lax.all_gather(by_columns, "rep", axis=0, tiled=True).reshape(matrices, width, cols)
    return (new_error, current, new_momentum, new_master, weights)


def divides(mesh, matrices, rank, width, cols):
    replicas, tps = mesh.shape["rep"], mesh.shape["tp"]
    if replicas & (replicas - 1) or tps != 4 or replicas < 8 or matrices % tps or cols % (tps * LANES) or width % LANES:
        return False
    if math.gcd(matrices * width // replicas, width) % LANES:
        return False
    tp_rows = matrices // tps * rank
    tiles = 8 * LANES * replicas
    return tp_rows * width % tiles == 0 and tps * tp_rows * (cols // tps) % tiles == 0


def solution(mesh):
    placed = (
        P("rep", None, None, "tp"),
        P("rep", None, None, "tp"),
        P(None, None, "tp"),
        P(("rep", "tp"), None),
        P(("rep", "tp"), None),
    )

    def step(grads, error, query, momentum, master):
        fits = divides(mesh, grads.shape[1], query.shape[1], grads.shape[2], grads.shape[3])
        return jax.shard_map(
            local if fits else plain_local,
            mesh=mesh,
            in_specs=placed,
            out_specs=(
                P("rep", None, None, "tp"),
                P(None, None, "tp"),
                P(("rep", "tp"), None),
                P(("rep", "tp"), None),
                P(None, None, "tp"),
            ),
            check_vma=False,
        )(grads, error, query, momentum, master)

    return step
```

```python
import functools
import math

import jax
import jax.numpy as jnp
from jax import lax
from jax.experimental import pallas as pl
from jax.experimental.pallas import tpu as pltpu
from jax.sharding import PartitionSpec as P

ROUNDS = 2
NS_STEPS = 5


NORM_EPSILON = 1e-06
MOMENTUM_DECAY = 0.9
LEARNING_RATE = 0.5
HIGHEST = lax.Precision.HIGHEST
LANES = 128
F32, BF16 = jnp.float32, jnp.bfloat16
SCALARS = pl.BlockSpec(memory_space=pltpu.SMEM)


def two_terms(x):
    high = x.astype(BF16)
    return high, (x - high.astype(F32)).astype(BF16)


def dot(a, b, transposed=False):
    dims = (((1,), (1 if transposed else 0,)), ((), ()))
    return lax.dot_general(a, b, dims, preferred_element_type=F32)


def small_by_large(small, high, low, transposed):
    rows = small.shape[0]
    small_high, small_low = two_terms(small)
    both = dot(jnp.concatenate([small_high, small_low], axis=0), high, transposed)
    return both[:rows] + both[rows:] + dot(small_high, low, transposed)


def dot3(a, b):
    a_high, a_low = two_terms(a)
    b_high, b_low = two_terms(b)
    return dot(
        jnp.concatenate([a_high, a_low, a_high], axis=1),
        jnp.concatenate([b_high, b_high, b_low], axis=0),
    )


def stacked(right):
    right_high, right_low = two_terms(right)
    return jnp.concatenate([right_high, right_high, right_low], axis=0)


def lay_lanes(scratch, value):
    rows = value.shape[0]
    for block in range(value.shape[1] // LANES):
        scratch[block * rows : (block + 1) * rows] = value[:, block * LANES : (block + 1) * LANES]


def read_lanes(scratch, rows):
    blocks = scratch.shape[0] // rows
    return jnp.concatenate([scratch[block * rows : (block + 1) * rows] for block in range(blocks)], axis=1)


def part_at(index, rows):
    return pl.ds(pl.multiple_of(index * rows, 8), rows)


def split_parts(scratch, me, part_refs):
    rows = part_refs[0].shape[0]
    for offset, part_ref in enumerate(part_refs):
        part_ref[...] = scratch[part_at(me ^ offset, rows), :]


def join_parts(scratch, me, part_refs):
    rows = part_refs[0].shape[0]
    for offset, part_ref in enumerate(part_refs):
        scratch[part_at(me ^ offset, rows), :] = part_ref[...]


def sum_of(refs):
    values = [ref[...] for ref in refs]
    while len(values) > 1:
        values = [sum(values[at : at + 2][1:], values[at]) for at in range(0, len(values), 2)]
    return values[0]


def put_left(left, step, left_refs, per_tp):
    for which, left_ref in enumerate(left_refs):

        @pl.when(step // per_tp == which)
        def _():
            left_ref[...] = left


def first_left_kernel(per_tp, picked, ids_ref, grads_ref, error_ref, query_ref, high_ref, low_ref, *refs):
    left_refs, (grads_buffer, error_buffer, sems) = refs[:-3], refs[-3:]
    step = pl.program_id(0)

    def copies(k):
        matrix = picked(k, ids_ref)
        return [
            pltpu.make_async_copy(source.at[0, matrix], buffer.at[k], sems.at[which, k])
            for which, (source, buffer) in enumerate(((grads_ref, grads_buffer), (error_ref, error_buffer)))
        ]

    @pl.when(step == 0)
    def _():
        for k in range(grads_buffer.shape[0]):
            for copy in copies(k):
                copy.start()

    for copy in copies(step):
        copy.wait()
    high, low = two_terms(grads_buffer[step].astype(F32) + error_buffer[step])
    high_ref[0] = high
    low_ref[0] = low
    put_left(small_by_large(query_ref[0], high, low, True), step, left_refs, per_tp)


def left_kernel(per_tp, half, ids_ref, high_ref, low_ref, *refs):
    parts, left_refs, (scratch, current) = refs[:-4], refs[-4:-2], refs[-2:]
    step = pl.program_id(0)
    rank = left_refs[0].shape[0]
    rows = current.shape[0]
    lanes = rows * (current.shape[1] // LANES)

    @pl.when(step == 0)
    def _():
        join_parts(scratch, ids_ref[0], parts)
        current[...] = read_lanes(scratch.at[half * lanes : (half + 1) * lanes], rows)

    own = current[part_at(step, rank), :]
    put_left(small_by_large(own, high_ref[0], low_ref[0], True), step, left_refs, per_tp)


def split_kernel(tps, *refs):
    lay_lanes(refs[-1], sum_of(refs[:tps]))


def total_kernel(parts_ref, out_ref):
    summed = sum_of([parts_ref.at[part] for part in range(parts_ref.shape[0])])
    for part in range(parts_ref.shape[0]):
        out_ref[part] = summed


def sum_kernel(scale, *refs):
    summed = sum_of(refs[:-1])
    refs[-1][...] = summed if scale == 1.0 else summed * scale


def mixing(left, rank):
    rows = left.shape[0]
    row_id = lax.broadcasted_iota(jnp.int32, (rows, rows), 0)
    col_id = lax.broadcasted_iota(jnp.int32, (rows, rows), 1)
    same = (row_id // rank) == (col_id // rank)
    eye = (row_id == col_id).astype(F32)
    left_high, left_low = two_terms(left)
    cross = dot(left_high, left_low, True)
    gram = jnp.where(same, dot(left_high, left_high, True) + cross + cross.T, 0.0)
    diagonal = jnp.sum(gram * eye, axis=0, keepdims=True)
    trace = jnp.sum(jnp.where(same, diagonal, 0.0), axis=1, keepdims=True) + NORM_EPSILON
    scale = lax.rsqrt(trace)
    scale = scale * (1.5 - 0.5 * trace * scale * scale)
    gram = gram * (scale * scale)
    step = 1.5 * eye - 0.5 * gram
    mixed = step * scale
    for _ in range(NS_STEPS - 1):
        gram = dot3(dot3(step, gram), step)
        step = 1.5 * eye - 0.5 * gram
        mixed = dot3(step, mixed)
    return mixed


def basis_kernel(rank, left_ref, basis_ref):
    rows = basis_ref.shape[0]
    left = read_lanes(left_ref, rows)
    padded = jnp.concatenate([left, jnp.zeros((-rows % LANES, left.shape[1]), F32)], axis=0)
    basis_ref[...] = dot3(mixing(padded, rank), padded)[:rows]


def right_kernel(per_tp, ids_ref, first_ref, second_ref, high_ref, low_ref, *refs):
    step = pl.program_id(0)
    rank = first_ref.shape[0] // per_tp
    at = part_at(step % per_tp, rank)
    own = jnp.where(step // per_tp == 0, first_ref[at, :], second_ref[at, :])
    product_now = small_by_large(own, high_ref[0], low_ref[0], False)
    if len(refs) == 1:
        refs[0][...] = product_now
        return
    before_ref, part_refs, (scratch, right) = refs[0], refs[1:-2], refs[-2:]
    right[part_at(step, rank), :] = product_now

    @pl.when(step == pl.num_programs(0) - 1)
    def _():
        lanes = scratch.shape[0] // 2
        lay_lanes(scratch.at[:lanes], before_ref[...])
        lay_lanes(scratch.at[lanes:], right[...])
        split_parts(scratch, ids_ref[0], part_refs)


def rows_of_update(basis_ref, right_ref, scratch, first_unit, unit, per_tp, rank, tp, first_matrix):
    per_matrix = basis_ref.shape[1] // unit
    for u in range(scratch.shape[0] // unit):
        at = first_unit + u
        matrix = at // per_matrix
        slot = ((matrix // per_tp) ^ tp) * per_tp + matrix % per_tp
        lanes = pl.ds(pl.multiple_of((at % per_matrix) * unit, LANES), unit)
        factor = basis_ref[part_at(slot, rank), lanes]
        right = right_ref[part_at(matrix - first_matrix, rank), :]
        scratch[u * unit : (u + 1) * unit] = product(factor, right)


def product(factor, right):
    high, low = two_terms(factor.T)
    return dot(jnp.concatenate([high, low, high], axis=1), stacked(right))


def late_kernel(unit, per_tp, rank, ids_ref, basis_ref, *refs):
    query_ref, *weight_refs, lanes, approx = refs[-5:]
    tps = query_ref.shape[0] // (per_tp * rank)
    part_refs, base_refs = refs[: -5 - tps], refs[-5 - tps : -5]
    rows = query_ref.shape[0] // 2
    tp = ids_ref[1]
    join_parts(lanes, ids_ref[0], part_refs)
    for half in range(2):
        per_half = lanes.shape[0] // 2
        value = read_lanes(lanes.at[half * per_half : (half + 1) * per_half], rows)
        for which in range(2):
            owner = tp ^ (2 * half + which)
            query_ref[part_at(owner, rows // 2), :] = value[which * (rows // 2) : (which + 1) * (rows // 2)]
    units = approx.shape[0] // unit
    rows_of_update(basis_ref, query_ref, approx, ids_ref[0] * units, unit, per_tp, rank, tp, 0)
    for offset, base_ref in enumerate(base_refs):
        at = part_at(tp ^ offset, base_ref.shape[0])
        approx[at, :] = base_ref[...] - LEARNING_RATE * approx[at, :]
    for half, weight_ref in enumerate(weight_refs):
        per_half = weight_ref.shape[0]
        weight_ref[...] = approx[half * per_half : (half + 1) * per_half].astype(BF16)


def owner_of(step, rep, replicas):
    half = replicas // 2
    return ((rep ^ (step // half)) + 2 * replicas - 2 * (step % half)) % replicas


def place_kernel(count, ids_ref, *refs):
    for at, part_ref in enumerate(refs[:count]):

        @pl.when(pl.program_id(0) == at)
        def _():
            refs[-1][0, 0] = part_ref[...]


def update_kernel(rank, ids_ref, basis_ref, right_ref, high_ref, low_ref, *refs):
    at = part_at(pl.program_id(0), rank)
    approx = product(basis_ref[at, :], right_ref[at, :])
    refs[-1][0, 0] = high_ref[0].astype(F32) + low_ref[0].astype(F32) - approx


def flat_kernel(unit, per_tp, rank, matrices, ids_ref, basis_ref, near_ref, momentum_ref, master_ref, new_momentum_ref, new_master_ref, approx):
    units = approx.shape[0] // unit
    spans = near_ref.shape[1] // rank
    first_unit = ids_ref[0] * units
    first = jnp.minimum(first_unit // (basis_ref.shape[1] // unit), matrices - spans)
    rows_of_update(basis_ref, near_ref.at[0], approx, first_unit, unit, per_tp, rank, ids_ref[1], first)
    own = approx[part_at(ids_ref[1], momentum_ref.shape[0]), :]
    new_momentum = MOMENTUM_DECAY * momentum_ref[...] + own
    new_momentum_ref[...] = new_momentum
    new_master_ref[...] = master_ref[...] - LEARNING_RATE * new_momentum


def shape(*dims, dtype=F32):
    return jax.ShapeDtypeStruct(dims, dtype)


def grant(mib):
    return pltpu.CompilerParams(vmem_limit_bytes=mib * 2**20)


def whole_call(kernel, name, out_shape, operands, ids=None, scratch=()):
    specs = [pl.BlockSpec(memory_space=pltpu.VMEM)] * len(operands)
    many = isinstance(out_shape, (list, tuple))
    out_spec = pl.BlockSpec(memory_space=pltpu.VMEM)
    moved = sum(4 * x.size for x in operands)
    if ids is not None:
        operands, specs = [ids, *operands], [SCALARS, *specs]
    return pl.pallas_call(
        kernel,
        in_specs=specs,
        out_specs=[out_spec] * len(out_shape) if many else out_spec,
        out_shape=out_shape,
        scratch_shapes=list(scratch),
        compiler_params=grant(12),
        name=name,
        cost_estimate=pl.CostEstimate(flops=moved, bytes_accessed=2 * moved, transcendentals=0),
    )(*operands)


def grid_call(kernel, name, ids, grid, in_specs, out_specs, out_shape, operands, scratch=(), aliases=None, flops=0, moved=0, mib=14):
    return pl.pallas_call(
        kernel,
        grid_spec=pltpu.PrefetchScalarGridSpec(
            num_scalar_prefetch=1,
            grid=grid,
            in_specs=in_specs,
            out_specs=out_specs,
            scratch_shapes=list(scratch),
        ),
        out_shape=out_shape,
        input_output_aliases=aliases or {},
        compiler_params=grant(mib),
        name=name,
        cost_estimate=pl.CostEstimate(flops=flops, bytes_accessed=moved, transcendentals=0),
    )(ids, *operands)


def swap(x, axis, size, offset):
    return lax.ppermute(x, axis, [(index, index ^ offset) for index in range(size)])


def scattered(parts, replicas):
    return [parts[0]] + [swap(parts[offset], "rep", replicas, offset) for offset in range(1, replicas)]


def spread(part, axis, size):
    return [part] + [swap(part, axis, size, offset) for offset in range(1, size)]


def local(grads, error, query, momentum, master):
    replicas, tps = lax.axis_size("rep"), lax.axis_size("tp")
    rep, tp = lax.axis_index("rep"), lax.axis_index("tp")
    ids = jnp.stack([rep, tp]).astype(jnp.int32)
    _, matrices, width, cols = grads.shape
    rank = query.shape[1]
    per_tp = matrices // tps
    per_half = 2 * per_tp
    halves = tps // 2
    tp_rows = per_tp * rank
    left_part = tp_rows * width // LANES // replicas
    right_part = tps * tp_rows * cols // LANES // replicas
    own_rows = momentum.shape[0]
    flops = 2 * 3 * per_half * rank * width * cols
    elements = per_half * width * cols

    def matrix_of(half, k, at):
        return (at[1] ^ (2 * half + k // per_tp)) * per_tp + k % per_tp

    term_spec = pl.BlockSpec((1, width, cols), lambda k, at: (k, 0, 0))
    term_shape = pltpu.VMEM((per_half, width, cols), BF16)
    left_specs = [
        pl.BlockSpec((rank, width), lambda k, at, which=which: (jnp.clip(k - which * per_tp, 0, per_tp - 1), 0))
        for which in range(2)
    ]
    left_shapes = [shape(tp_rows, width)] * 2

    def whole_spec(*dims):
        return pl.BlockSpec(dims, lambda k, at: (0,) * len(dims))

    terms, lefts = [None] * halves, [None] * tps
    for half in reversed(range(halves)):
        picked = functools.partial(matrix_of, half)
        high, low, *out = grid_call(
            functools.partial(first_left_kernel, per_tp, picked),
            "first_left",
            ids,
            (per_half,),
            [
                pl.BlockSpec(memory_space=pltpu.HBM),
                pl.BlockSpec(memory_space=pltpu.HBM),
                pl.BlockSpec((1, rank, cols), lambda k, at, picked=picked: (picked(k, at), 0, 0)),
            ],
            [term_spec, term_spec, *left_specs],
            [term_shape, term_shape, *left_shapes],
            (*(pltpu.with_memory_space_constraint(x, pltpu.HBM) for x in (grads, error)), query),
            [
                pltpu.VMEM((per_half, width, cols), BF16),
                pltpu.VMEM((per_half, width, cols), F32),
                pltpu.SemaphoreType.DMA((2, per_half)),
            ],
            mib=26,
            flops=flops,
            moved=10 * elements,
        )
        terms[half] = tuple(pltpu.with_memory_space_constraint(term, pltpu.VMEM) for term in (high, low))
        lefts[2 * half : 2 * half + 2] = out
        ids, _ = lax.optimization_barrier((ids, out[0]))

    base = []
    for power_pass in range(ROUNDS):
        met = [lefts[0]] + [swap(lefts[offset], "tp", tps, offset) for offset in reversed(range(1, tps))]
        parts = whole_call(
            functools.partial(split_kernel, tps), "left_split", shape(left_part * replicas, LANES), met
        )
        parts, new_values, old_values = lax.optimization_barrier((parts, master, momentum))
        some = []
        for offset in range(3 * power_pass, 3 + power_pass):
            column = (tp ^ offset) * cols
            piece = lax.dynamic_slice_in_dim(new_values, column, cols, 1)
            piece = piece - (LEARNING_RATE * MOMENTUM_DECAY) * lax.dynamic_slice_in_dim(old_values, column, cols, 1)
            some.append(piece if offset == 0 else swap(piece, "tp", tps, offset))
        parts = parts.reshape(replicas, left_part, LANES)
        parts = lax.all_to_all(parts, "rep", split_axis=0, concat_axis=0, tiled=True)
        parts = whole_call(total_kernel, "left_sum", shape(*parts.shape), [parts])
        parts = lax.all_to_all(parts, "rep", split_axis=0, concat_axis=0, tiled=True)
        parts, some = lax.optimization_barrier((parts, some))
        base += some
        basis = whole_call(
            functools.partial(basis_kernel, rank), "basis", shape(tp_rows, width), [parts.reshape(-1, LANES)]
        )
        across = swap(basis, "tp", tps, 2)
        bases = [basis, swap(basis, "tp", tps, 1)]
        before = grid_call(
            functools.partial(right_kernel, per_tp),
            "right_near",
            ids,
            (per_half,),
            [whole_spec(tp_rows, width), whole_spec(tp_rows, width), term_spec, term_spec],
            pl.BlockSpec((rank, cols), lambda k, at: (k, 0)),
            shape(2 * tp_rows, cols),
            (*bases, *terms[0]),
            flops=flops,
            moved=4 * elements,
        )
        before, across = lax.optimization_barrier((before, across))
        bases += [across, swap(across, "tp", tps, 1)]
        parts = grid_call(
            functools.partial(right_kernel, per_tp),
            "right_far",
            ids,
            (per_half,),
            [whole_spec(tp_rows, width), whole_spec(tp_rows, width), term_spec, term_spec, whole_spec(2 * tp_rows, cols)],
            [whole_spec(right_part, LANES)] * replicas,
            [shape(right_part, LANES)] * replicas,
            (*bases[2:], *terms[1], before),
            [pltpu.VMEM((right_part * replicas, LANES), F32), pltpu.VMEM((2 * tp_rows, cols), F32)],
            flops=flops,
            moved=4 * elements,
        )
        met = scattered(parts, replicas)
        part = whole_call(functools.partial(sum_kernel, 1.0 / replicas), "right_sum", shape(right_part, LANES), met)
        rights = spread(part, "rep", replicas)
        if power_pass < ROUNDS - 1:
            for half in reversed(range(halves)):
                lefts[2 * half : 2 * half + 2] = grid_call(
                    functools.partial(left_kernel, per_tp, half),
                    "left",
                    ids,
                    (per_half,),
                    [term_spec, term_spec] + [whole_spec(right_part, LANES)] * replicas,
                    left_specs,
                    left_shapes,
                    (*terms[half], *rights),
                    [pltpu.VMEM((right_part * replicas, LANES), F32), pltpu.VMEM((2 * tp_rows, cols), F32)],
                    flops=flops,
                    moved=10 * elements,
                )

    all_bases = jnp.concatenate(bases, axis=0)
    rep_rows = tps * own_rows
    unit = math.gcd(rep_rows, width)
    right, *block = whole_call(
        functools.partial(late_kernel, unit, per_tp, rank),
        "late_rows",
        [shape(matrices * rank, cols)] + [shape(rep_rows // 2, cols, dtype=BF16)] * 2,
        [all_bases, *rights, *base],
        ids,
        [pltpu.VMEM((right_part * replicas, LANES), F32), pltpu.VMEM((rep_rows, cols), F32)],
    )
    spans = -(-(width - unit + rep_rows) // width)
    first = jnp.minimum(rep * rep_rows // width, matrices - spans)
    near = lax.dynamic_slice_in_dim(right, first * rank, spans * rank, 0)

    def update(slot, ids, before):
        half, start = slot // 2, slot % 2 * per_tp
        return grid_call(
            functools.partial(update_kernel, rank),
            "update",
            ids,
            (per_tp,),
            [
                pl.BlockSpec((tp_rows, width), lambda j, at: (slot, 0)),
                pl.BlockSpec((tp_rows, cols), lambda j, at: (at[1] ^ slot, 0)),
                pl.BlockSpec((1, width, cols), lambda j, at: (start + j, 0, 0)),
                pl.BlockSpec((1, width, cols), lambda j, at: (start + j, 0, 0)),
            ]
            + [pl.BlockSpec(memory_space=pl.ANY)] * len(before),
            pl.BlockSpec((1, 1, width, cols), lambda j, at: (0, (at[1] ^ slot) * per_tp + j, 0, 0)),
            shape(*error.shape),
            (all_bases, right, *terms[half], *before),
            aliases={5: 0} if before else None,
            flops=2 * 3 * rank * error.size // tps,
            moved=8 * error.size // tps,
        )

    def place(pieces, ids, before):
        count = len(pieces)

        def where(k, at):
            at_half, step = pieces[-1][1:]
            for index in range(count - 1):
                at_half = jnp.where(k == index, pieces[index][1], at_half)
                step = jnp.where(k == index, pieces[index][2], step)
            return (owner_of(step, at[0], replicas), at_half, 0, 0)

        return grid_call(
            functools.partial(place_kernel, count),
            "place",
            ids,
            (count,),
            [pl.BlockSpec((rep_rows // 2, cols), lambda k, at: (0, 0))] * count
            + [pl.BlockSpec(memory_space=pl.ANY)] * len(before),
            pl.BlockSpec((1, 1, rep_rows // 2, cols), where),
            shape(replicas, 2, rep_rows // 2, cols, dtype=BF16),
            (*[piece[0] for piece in pieces], *before),
            aliases={1 + count: 0} if before else None,
            moved=4 * count * rep_rows * cols,
        )

    def flat_rows(ids, all_bases, near):
        wide = pl.BlockSpec((own_rows, cols), lambda s, at: (0, at[1] ^ s))
        return grid_call(
            functools.partial(flat_kernel, unit, per_tp, rank, matrices),
            "flat_rows",
            ids,
            (tps,),
            [
                whole_spec(matrices * rank, width),
                pl.BlockSpec((1, spans * rank, cols), lambda s, at: (s, 0, 0)),
                wide,
                wide,
            ],
            [wide, wide],
            [shape(*momentum.shape), shape(*master.shape)],
            (all_bases, near, momentum, master),
            [pltpu.VMEM((rep_rows, cols), F32)],
            flops=2 * 3 * rank * momentum.size * tps,
            moved=16 * momentum.size,
        )

    ring = [(index, (index + 2) % replicas) for index in range(replicas)]
    stages = replicas // 2
    last = 2 * stages - 1
    held, beside = list(block), [None, None]
    pieces = [(block[half], half, 0) for half in range(2)]
    errors, flat, weights = (), (), ()
    jobs = {1: "update", 2: "update", 3: "update", 4: "update", 5: "flat place", 2 * stages - 2: "place", 2 * stages - 1: "place"}
    near = spread(near, "tp", tps)
    updated = 0
    for step in range(2 * stages):
        stage, half = step // 2, step % 2
        if stage > 0:
            arrived = (held[half], beside[half])
            ids, errors, flat, weights, near, arrived = lax.optimization_barrier((ids, errors, flat, weights, near, arrived))
            held[half], beside[half] = arrived
            pieces += [(held[half], half, stage), (beside[half], half, stages + stage - 1)]
        if stage < stages - 1:
            here = held[half]
            held[half] = lax.ppermute(here, "rep", ring)
            beside[half] = swap(here, "rep", replicas, 1)
        elif half == 0:
            beside[half] = swap(held[half], "rep", replicas, 1)
        else:
            beside[half] = lax.ppermute(beside[half], "rep", ring)
        for job in jobs.get(step, "").split():
            if job == "update":
                errors = (update(updated, ids, errors),)
                updated += 1
            elif job == "flat":
                flat = flat_rows(ids, all_bases, jnp.stack(near))
            else:
                weights = (place(pieces, ids, weights),)
                pieces = []
    weights = place([(beside[half], half, last) for half in range(2)], ids, weights).reshape(matrices, width, cols)
    (new_error,) = errors
    new_momentum, new_master = flat
    return (new_error, right.reshape(matrices, rank, cols), new_momentum, new_master, weights)


def plain_orthonormal(factor):
    def gram_of(x):
        return jnp.einsum("krd,ksd->krs", x, x, precision=HIGHEST)

    gram_now = gram_of(factor)
    factor_scale = lax.rsqrt(jnp.trace(gram_now, axis1=1, axis2=2)[:, None, None] + NORM_EPSILON)
    ortho_basis = factor * factor_scale
    gram_now = gram_now * (factor_scale * factor_scale)
    for iteration in range(NS_STEPS):
        if iteration > 0:
            gram_now = gram_of(ortho_basis)
        ortho_basis = 1.5 * ortho_basis - 0.5 * jnp.einsum("krs,ksd->krd", gram_now, ortho_basis, precision=HIGHEST)
    return ortho_basis


def plain_local(grads, error, query, momentum, master):
    corrected = grads[0].astype(F32) + error[0]
    current = query
    replicas = lax.axis_size("rep")
    for _ in range(ROUNDS):
        partial_factor = jnp.einsum("kdf,krf->krd", corrected, current, precision=HIGHEST)
        ortho_basis = plain_orthonormal(lax.psum(partial_factor, ("rep", "tp")))
        partial_query = jnp.einsum("kdf,krd->krf", corrected, ortho_basis, precision=HIGHEST)
        current = lax.psum(partial_query, "rep") / replicas
    approx = jnp.einsum("krd,krf->kdf", ortho_basis, current, precision=HIGHEST)
    new_error = (corrected - approx)[None]
    matrices, width, cols = approx.shape
    block_rows = matrices * width // replicas
    own_block = lax.dynamic_slice_in_dim(
        approx.reshape(matrices * width, cols), lax.axis_index("rep") * block_rows, block_rows, 0
    )
    flat_approx = lax.all_to_all(own_block, "tp", split_axis=0, concat_axis=1, tiled=True)
    new_momentum = MOMENTUM_DECAY * momentum + flat_approx
    new_master = master - LEARNING_RATE * new_momentum
    by_columns = lax.all_to_all(new_master.astype(BF16), "tp", split_axis=1, concat_axis=0, tiled=True)
    weights = lax.all_gather(by_columns, "rep", axis=0, tiled=True).reshape(matrices, width, cols)
    return (new_error, current, new_momentum, new_master, weights)


def divides(mesh, matrices, rank, width, cols):
    replicas, tps = mesh.shape["rep"], mesh.shape["tp"]
    if replicas & (replicas - 1) or tps != 4 or replicas < 8 or matrices % tps or cols % (tps * LANES) or width % LANES:
        return False
    if math.gcd(matrices * width // replicas, width) % LANES:
        return False
    tp_rows = matrices // tps * rank
    tiles = 8 * LANES * replicas
    return tp_rows * width % tiles == 0 and tps * tp_rows * (cols // tps) % tiles == 0


def solution(mesh):
    placed = (
        P("rep", None, None, "tp"),
        P("rep", None, None, "tp"),
        P(None, None, "tp"),
        P(("rep", "tp"), None),
        P(("rep", "tp"), None),
    )

    def step(grads, error, query, momentum, master):
        fits = divides(mesh, grads.shape[1], query.shape[1], grads.shape[2], grads.shape[3])
        return jax.shard_map(
            local if fits else plain_local,
            mesh=mesh,
            in_specs=placed,
            out_specs=(
                P("rep", None, None, "tp"),
                P(None, None, "tp"),
                P(("rep", "tp"), None),
                P(("rep", "tp"), None),
                P(None, None, "tp"),
            ),
            check_vma=False,
        )(grads, error, query, momentum, master)

    return step
```

```python
import functools
import math

import jax
import jax.numpy as jnp
from jax import lax
from jax.experimental import pallas as pl
from jax.experimental.pallas import tpu as pltpu
from jax.sharding import PartitionSpec as P

ROUNDS = 2
NS_STEPS = 5


NORM_EPSILON = 1e-06
MOMENTUM_DECAY = 0.9
LEARNING_RATE = 0.5
HIGHEST = lax.Precision.HIGHEST
LANES = 128
F32, BF16 = jnp.float32, jnp.bfloat16
SCALARS = pl.BlockSpec(memory_space=pltpu.SMEM)


def two_terms(x):
    high = x.astype(BF16)
    return high, (x - high.astype(F32)).astype(BF16)


def dot(a, b, transposed=False):
    dims = (((1,), (1 if transposed else 0,)), ((), ()))
    return lax.dot_general(a, b, dims, preferred_element_type=F32)


def small_by_large(small, high, low, transposed):
    rows = small.shape[0]
    small_high, small_low = two_terms(small)
    both = dot(jnp.concatenate([small_high, small_low], axis=0), high, transposed)
    return both[:rows] + both[rows:] + dot(small_high, low, transposed)


def dot3(a, b):
    a_high, a_low = two_terms(a)
    b_high, b_low = two_terms(b)
    return dot(
        jnp.concatenate([a_high, a_low, a_high], axis=1),
        jnp.concatenate([b_high, b_high, b_low], axis=0),
    )


def stacked(right):
    right_high, right_low = two_terms(right)
    return jnp.concatenate([right_high, right_high, right_low], axis=0)


def lay_lanes(scratch, value):
    rows = value.shape[0]
    for block in range(value.shape[1] // LANES):
        scratch[block * rows : (block + 1) * rows] = value[:, block * LANES : (block + 1) * LANES]


def read_lanes(scratch, rows):
    blocks = scratch.shape[0] // rows
    return jnp.concatenate([scratch[block * rows : (block + 1) * rows] for block in range(blocks)], axis=1)


def part_at(index, rows):
    return pl.ds(pl.multiple_of(index * rows, 8), rows)


def split_parts(scratch, me, part_refs):
    rows = part_refs[0].shape[0]
    for offset, part_ref in enumerate(part_refs):
        part_ref[...] = scratch[part_at(me ^ offset, rows), :]


def join_parts(scratch, me, part_refs):
    rows = part_refs[0].shape[0]
    for offset, part_ref in enumerate(part_refs):
        scratch[part_at(me ^ offset, rows), :] = part_ref[...]


def sum_of(refs):
    values = [ref[...] for ref in refs]
    while len(values) > 1:
        values = [sum(values[at : at + 2][1:], values[at]) for at in range(0, len(values), 2)]
    return values[0]


def put_left(left, step, left_refs, per_tp):
    for which, left_ref in enumerate(left_refs):

        @pl.when(step // per_tp == which)
        def _():
            left_ref[...] = left


def first_left_kernel(per_tp, picked, ids_ref, grads_ref, error_ref, query_ref, high_ref, low_ref, *refs):
    left_refs, (grads_buffer, error_buffer, sems) = refs[:-3], refs[-3:]
    step = pl.program_id(0)

    def copies(k):
        matrix = picked(k, ids_ref)
        return [
            pltpu.make_async_copy(source.at[0, matrix], buffer.at[k], sems.at[which, k])
            for which, (source, buffer) in enumerate(((grads_ref, grads_buffer), (error_ref, error_buffer)))
        ]

    @pl.when(step == 0)
    def _():
        for k in range(grads_buffer.shape[0]):
            for copy in copies(k):
                copy.start()

    for copy in copies(step):
        copy.wait()
    high, low = two_terms(grads_buffer[step].astype(F32) + error_buffer[step])
    high_ref[0] = high
    low_ref[0] = low
    put_left(small_by_large(query_ref[0], high, low, True), step, left_refs, per_tp)


def left_kernel(per_tp, half, ids_ref, high_ref, low_ref, *refs):
    parts, left_refs, (scratch, current) = refs[:-4], refs[-4:-2], refs[-2:]
    step = pl.program_id(0)
    rank = left_refs[0].shape[0]
    rows = current.shape[0]
    lanes = rows * (current.shape[1] // LANES)

    @pl.when(step == 0)
    def _():
        join_parts(scratch, ids_ref[0], parts)
        current[...] = read_lanes(scratch.at[half * lanes : (half + 1) * lanes], rows)

    own = current[part_at(step, rank), :]
    put_left(small_by_large(own, high_ref[0], low_ref[0], True), step, left_refs, per_tp)


def split_kernel(tps, *refs):
    lay_lanes(refs[-1], sum_of(refs[:tps]))


def total_kernel(parts_ref, out_ref):
    summed = sum_of([parts_ref.at[part] for part in range(parts_ref.shape[0])])
    for part in range(parts_ref.shape[0]):
        out_ref[part] = summed


def sum_kernel(scale, *refs):
    summed = sum_of(refs[:-1])
    refs[-1][...] = summed if scale == 1.0 else summed * scale


def mixing(left, rank):
    rows = left.shape[0]
    row_id = lax.broadcasted_iota(jnp.int32, (rows, rows), 0)
    col_id = lax.broadcasted_iota(jnp.int32, (rows, rows), 1)
    same = (row_id // rank) == (col_id // rank)
    eye = (row_id == col_id).astype(F32)
    left_high, left_low = two_terms(left)
    cross = dot(left_high, left_low, True)
    gram = jnp.where(same, dot(left_high, left_high, True) + cross + cross.T, 0.0)
    diagonal = jnp.sum(gram * eye, axis=0, keepdims=True)
    trace = jnp.sum(jnp.where(same, diagonal, 0.0), axis=1, keepdims=True) + NORM_EPSILON
    scale = lax.rsqrt(trace)
    scale = scale * (1.5 - 0.5 * trace * scale * scale)
    gram = gram * (scale * scale)
    step = 1.5 * eye - 0.5 * gram
    mixed = step * scale
    for _ in range(NS_STEPS - 1):
        gram = dot3(dot3(step, gram), step)
        step = 1.5 * eye - 0.5 * gram
        mixed = dot3(step, mixed)
    return mixed


def basis_kernel(rank, left_ref, basis_ref):
    rows = basis_ref.shape[0]
    left = read_lanes(left_ref, rows)
    padded = jnp.concatenate([left, jnp.zeros((-rows % LANES, left.shape[1]), F32)], axis=0)
    basis_ref[...] = dot3(mixing(padded, rank), padded)[:rows]


def right_kernel(per_tp, ids_ref, first_ref, second_ref, high_ref, low_ref, *refs):
    step = pl.program_id(0)
    rank = first_ref.shape[0] // per_tp
    at = part_at(step % per_tp, rank)
    own = jnp.where(step // per_tp == 0, first_ref[at, :], second_ref[at, :])
    product_now = small_by_large(own, high_ref[0], low_ref[0], False)
    if len(refs) == 1:
        refs[0][...] = product_now
        return
    before_ref, part_refs, (scratch, right) = refs[0], refs[1:-2], refs[-2:]
    right[part_at(step, rank), :] = product_now

    @pl.when(step == pl.num_programs(0) - 1)
    def _():
        lanes = scratch.shape[0] // 2
        lay_lanes(scratch.at[:lanes], before_ref[...])
        lay_lanes(scratch.at[lanes:], right[...])
        split_parts(scratch, ids_ref[0], part_refs)


def rows_of_update(basis_ref, right_ref, scratch, first_unit, unit, per_tp, rank, tp, first_matrix):
    per_matrix = basis_ref.shape[1] // unit
    for u in range(scratch.shape[0] // unit):
        at = first_unit + u
        matrix = at // per_matrix
        slot = ((matrix // per_tp) ^ tp) * per_tp + matrix % per_tp
        lanes = pl.ds(pl.multiple_of((at % per_matrix) * unit, LANES), unit)
        factor = basis_ref[part_at(slot, rank), lanes]
        right = right_ref[part_at(matrix - first_matrix, rank), :]
        scratch[u * unit : (u + 1) * unit] = product(factor, right)


def product(factor, right):
    high, low = two_terms(factor.T)
    return dot(jnp.concatenate([high, low, high], axis=1), stacked(right))


def late_kernel(unit, per_tp, rank, ids_ref, basis_ref, *refs):
    query_ref, *weight_refs, lanes, approx = refs[-5:]
    tps = query_ref.shape[0] // (per_tp * rank)
    part_refs, base_refs = refs[: -5 - tps], refs[-5 - tps : -5]
    rows = query_ref.shape[0] // 2
    tp = ids_ref[1]
    join_parts(lanes, ids_ref[0], part_refs)
    for half in range(2):
        per_half = lanes.shape[0] // 2
        value = read_lanes(lanes.at[half * per_half : (half + 1) * per_half], rows)
        for which in range(2):
            owner = tp ^ (2 * half + which)
            query_ref[part_at(owner, rows // 2), :] = value[which * (rows // 2) : (which + 1) * (rows // 2)]
    units = approx.shape[0] // unit
    rows_of_update(basis_ref, query_ref, approx, ids_ref[0] * units, unit, per_tp, rank, tp, 0)
    for offset, base_ref in enumerate(base_refs):
        at = part_at(tp ^ offset, base_ref.shape[0])
        approx[at, :] = base_ref[...] - LEARNING_RATE * approx[at, :]
    for half, weight_ref in enumerate(weight_refs):
        per_half = weight_ref.shape[0]
        weight_ref[...] = approx[half * per_half : (half + 1) * per_half].astype(BF16)


def owner_of(step, rep, replicas):
    half = replicas // 2
    return ((rep ^ (step // half)) + 2 * replicas - 2 * (step % half)) % replicas


def place_kernel(count, ids_ref, *refs):
    for at, part_ref in enumerate(refs[:count]):

        @pl.when(pl.program_id(0) == at)
        def _():
            refs[-1][0, 0] = part_ref[...]


def update_kernel(rank, ids_ref, basis_ref, right_ref, high_ref, low_ref, *refs):
    at = part_at(pl.program_id(0), rank)
    approx = product(basis_ref[at, :], right_ref[at, :])
    refs[-1][0, 0] = high_ref[0].astype(F32) + low_ref[0].astype(F32) - approx


def flat_kernel(unit, per_tp, rank, matrices, ids_ref, basis_ref, near_ref, momentum_ref, master_ref, new_momentum_ref, new_master_ref, approx):
    units = approx.shape[0] // unit
    spans = near_ref.shape[1] // rank
    first_unit = ids_ref[0] * units
    first = jnp.minimum(first_unit // (basis_ref.shape[1] // unit), matrices - spans)
    rows_of_update(basis_ref, near_ref.at[0], approx, first_unit, unit, per_tp, rank, ids_ref[1], first)
    own = approx[part_at(ids_ref[1], momentum_ref.shape[0]), :]
    new_momentum = MOMENTUM_DECAY * momentum_ref[...] + own
    new_momentum_ref[...] = new_momentum
    new_master_ref[...] = master_ref[...] - LEARNING_RATE * new_momentum


def shape(*dims, dtype=F32):
    return jax.ShapeDtypeStruct(dims, dtype)


def grant(mib):
    return pltpu.CompilerParams(vmem_limit_bytes=mib * 2**20)


def whole_call(kernel, name, out_shape, operands, ids=None, scratch=()):
    specs = [pl.BlockSpec(memory_space=pltpu.VMEM)] * len(operands)
    many = isinstance(out_shape, (list, tuple))
    out_spec = pl.BlockSpec(memory_space=pltpu.VMEM)
    moved = sum(4 * x.size for x in operands)
    if ids is not None:
        operands, specs = [ids, *operands], [SCALARS, *specs]
    return pl.pallas_call(
        kernel,
        in_specs=specs,
        out_specs=[out_spec] * len(out_shape) if many else out_spec,
        out_shape=out_shape,
        scratch_shapes=list(scratch),
        compiler_params=grant(12),
        name=name,
        cost_estimate=pl.CostEstimate(flops=moved, bytes_accessed=2 * moved, transcendentals=0),
    )(*operands)


def grid_call(kernel, name, ids, grid, in_specs, out_specs, out_shape, operands, scratch=(), aliases=None, flops=0, moved=0, mib=14):
    return pl.pallas_call(
        kernel,
        grid_spec=pltpu.PrefetchScalarGridSpec(
            num_scalar_prefetch=1,
            grid=grid,
            in_specs=in_specs,
            out_specs=out_specs,
            scratch_shapes=list(scratch),
        ),
        out_shape=out_shape,
        input_output_aliases=aliases or {},
        compiler_params=grant(mib),
        name=name,
        cost_estimate=pl.CostEstimate(flops=flops, bytes_accessed=moved, transcendentals=0),
    )(ids, *operands)


def swap(x, axis, size, offset):
    return lax.ppermute(x, axis, [(index, index ^ offset) for index in range(size)])


def scattered(parts, replicas):
    return [parts[0]] + [swap(parts[offset], "rep", replicas, offset) for offset in range(1, replicas)]


def spread(part, axis, size):
    return [part] + [swap(part, axis, size, offset) for offset in range(1, size)]


def local(grads, error, query, momentum, master):
    replicas, tps = lax.axis_size("rep"), lax.axis_size("tp")
    rep, tp = lax.axis_index("rep"), lax.axis_index("tp")
    ids = jnp.stack([rep, tp]).astype(jnp.int32)
    _, matrices, width, cols = grads.shape
    rank = query.shape[1]
    per_tp = matrices // tps
    per_half = 2 * per_tp
    halves = tps // 2
    tp_rows = per_tp * rank
    left_part = tp_rows * width // LANES // replicas
    right_part = tps * tp_rows * cols // LANES // replicas
    own_rows = momentum.shape[0]
    flops = 2 * 3 * per_half * rank * width * cols
    elements = per_half * width * cols

    def matrix_of(half, k, at):
        return (at[1] ^ (2 * half + k // per_tp)) * per_tp + k % per_tp

    term_spec = pl.BlockSpec((1, width, cols), lambda k, at: (k, 0, 0))
    term_shape = pltpu.VMEM((per_half, width, cols), BF16)
    left_specs = [
        pl.BlockSpec((rank, width), lambda k, at, which=which: (jnp.clip(k - which * per_tp, 0, per_tp - 1), 0))
        for which in range(2)
    ]
    left_shapes = [shape(tp_rows, width)] * 2

    def whole_spec(*dims):
        return pl.BlockSpec(dims, lambda k, at: (0,) * len(dims))

    terms, lefts = [None] * halves, [None] * tps
    for half in reversed(range(halves)):
        picked = functools.partial(matrix_of, half)
        high, low, *out = grid_call(
            functools.partial(first_left_kernel, per_tp, picked),
            "first_left",
            ids,
            (per_half,),
            [
                pl.BlockSpec(memory_space=pltpu.HBM),
                pl.BlockSpec(memory_space=pltpu.HBM),
                pl.BlockSpec((1, rank, cols), lambda k, at, picked=picked: (picked(k, at), 0, 0)),
            ],
            [term_spec, term_spec, *left_specs],
            [term_shape, term_shape, *left_shapes],
            (*(pltpu.with_memory_space_constraint(x, pltpu.HBM) for x in (grads, error)), query),
            [
                pltpu.VMEM((per_half, width, cols), BF16),
                pltpu.VMEM((per_half, width, cols), F32),
                pltpu.SemaphoreType.DMA((2, per_half)),
            ],
            mib=26,
            flops=flops,
            moved=10 * elements,
        )
        terms[half] = tuple(pltpu.with_memory_space_constraint(term, pltpu.VMEM) for term in (high, low))
        lefts[2 * half : 2 * half + 2] = out
        ids, _ = lax.optimization_barrier((ids, out[0]))

    base = []
    for power_pass in range(ROUNDS):
        met = [lefts[0]] + [swap(lefts[offset], "tp", tps, offset) for offset in reversed(range(1, tps))]
        parts = whole_call(
            functools.partial(split_kernel, tps), "left_split", shape(left_part * replicas, LANES), met
        )
        parts, new_values, old_values = lax.optimization_barrier((parts, master, momentum))
        some = []
        for offset in range(3 * power_pass, 3 + power_pass):
            column = (tp ^ offset) * cols
            piece = lax.dynamic_slice_in_dim(new_values, column, cols, 1)
            piece = piece - (LEARNING_RATE * MOMENTUM_DECAY) * lax.dynamic_slice_in_dim(old_values, column, cols, 1)
            some.append((piece, offset))
        parts, pieces = lax.optimization_barrier((parts, [piece for piece, _ in some]))
        some = [piece if offset == 0 else swap(piece, "tp", tps, offset) for piece, (_, offset) in zip(pieces, some)]
        parts = parts.reshape(replicas, left_part, LANES)
        parts = lax.all_to_all(parts, "rep", split_axis=0, concat_axis=0, tiled=True)
        parts = whole_call(total_kernel, "left_sum", shape(*parts.shape), [parts])
        parts = lax.all_to_all(parts, "rep", split_axis=0, concat_axis=0, tiled=True)
        parts, some = lax.optimization_barrier((parts, some))
        base += some
        basis = whole_call(
            functools.partial(basis_kernel, rank), "basis", shape(tp_rows, width), [parts.reshape(-1, LANES)]
        )
        across = swap(basis, "tp", tps, 2)
        bases = [basis, swap(basis, "tp", tps, 1)]
        before = grid_call(
            functools.partial(right_kernel, per_tp),
            "right_near",
            ids,
            (per_half,),
            [whole_spec(tp_rows, width), whole_spec(tp_rows, width), term_spec, term_spec],
            pl.BlockSpec((rank, cols), lambda k, at: (k, 0)),
            shape(2 * tp_rows, cols),
            (*bases, *terms[0]),
            flops=flops,
            moved=4 * elements,
        )
        before, across = lax.optimization_barrier((before, across))
        bases += [across, swap(across, "tp", tps, 1)]
        parts = grid_call(
            functools.partial(right_kernel, per_tp),
            "right_far",
            ids,
            (per_half,),
            [whole_spec(tp_rows, width), whole_spec(tp_rows, width), term_spec, term_spec, whole_spec(2 * tp_rows, cols)],
            [whole_spec(right_part, LANES)] * replicas,
            [shape(right_part, LANES)] * replicas,
            (*bases[2:], *terms[1], before),
            [pltpu.VMEM((right_part * replicas, LANES), F32), pltpu.VMEM((2 * tp_rows, cols), F32)],
            flops=flops,
            moved=4 * elements,
        )
        met = scattered(parts, replicas)
        part = whole_call(functools.partial(sum_kernel, 1.0 / replicas), "right_sum", shape(right_part, LANES), met)
        rights = spread(part, "rep", replicas)
        if power_pass < ROUNDS - 1:
            for half in reversed(range(halves)):
                lefts[2 * half : 2 * half + 2] = grid_call(
                    functools.partial(left_kernel, per_tp, half),
                    "left",
                    ids,
                    (per_half,),
                    [term_spec, term_spec] + [whole_spec(right_part, LANES)] * replicas,
                    left_specs,
                    left_shapes,
                    (*terms[half], *rights),
                    [pltpu.VMEM((right_part * replicas, LANES), F32), pltpu.VMEM((2 * tp_rows, cols), F32)],
                    flops=flops,
                    moved=10 * elements,
                )

    all_bases = jnp.concatenate(bases, axis=0)
    rep_rows = tps * own_rows
    unit = math.gcd(rep_rows, width)
    right, *block = whole_call(
        functools.partial(late_kernel, unit, per_tp, rank),
        "late_rows",
        [shape(matrices * rank, cols)] + [shape(rep_rows // 2, cols, dtype=BF16)] * 2,
        [all_bases, *rights, *base],
        ids,
        [pltpu.VMEM((right_part * replicas, LANES), F32), pltpu.VMEM((rep_rows, cols), F32)],
    )
    spans = -(-(width - unit + rep_rows) // width)
    first = jnp.minimum(rep * rep_rows // width, matrices - spans)
    near = lax.dynamic_slice_in_dim(right, first * rank, spans * rank, 0)

    def update(slot, ids, before):
        half, start = slot // 2, slot % 2 * per_tp
        return grid_call(
            functools.partial(update_kernel, rank),
            "update",
            ids,
            (per_tp,),
            [
                pl.BlockSpec((tp_rows, width), lambda j, at: (slot, 0)),
                pl.BlockSpec((tp_rows, cols), lambda j, at: (at[1] ^ slot, 0)),
                pl.BlockSpec((1, width, cols), lambda j, at: (start + j, 0, 0)),
                pl.BlockSpec((1, width, cols), lambda j, at: (start + j, 0, 0)),
            ]
            + [pl.BlockSpec(memory_space=pl.ANY)] * len(before),
            pl.BlockSpec((1, 1, width, cols), lambda j, at: (0, (at[1] ^ slot) * per_tp + j, 0, 0)),
            shape(*error.shape),
            (all_bases, right, *terms[half], *before),
            aliases={5: 0} if before else None,
            flops=2 * 3 * rank * error.size // tps,
            moved=8 * error.size // tps,
        )

    def place(pieces, ids, before):
        count = len(pieces)

        def where(k, at):
            at_half, step = pieces[-1][1:]
            for index in range(count - 1):
                at_half = jnp.where(k == index, pieces[index][1], at_half)
                step = jnp.where(k == index, pieces[index][2], step)
            return (owner_of(step, at[0], replicas), at_half, 0, 0)

        return grid_call(
            functools.partial(place_kernel, count),
            "place",
            ids,
            (count,),
            [pl.BlockSpec((rep_rows // 2, cols), lambda k, at: (0, 0))] * count
            + [pl.BlockSpec(memory_space=pl.ANY)] * len(before),
            pl.BlockSpec((1, 1, rep_rows // 2, cols), where),
            shape(replicas, 2, rep_rows // 2, cols, dtype=BF16),
            (*[piece[0] for piece in pieces], *before),
            aliases={1 + count: 0} if before else None,
            moved=4 * count * rep_rows * cols,
        )

    def flat_rows(ids, all_bases, near):
        wide = pl.BlockSpec((own_rows, cols), lambda s, at: (0, at[1] ^ s))
        return grid_call(
            functools.partial(flat_kernel, unit, per_tp, rank, matrices),
            "flat_rows",
            ids,
            (tps,),
            [
                whole_spec(matrices * rank, width),
                pl.BlockSpec((1, spans * rank, cols), lambda s, at: (s, 0, 0)),
                wide,
                wide,
            ],
            [wide, wide],
            [shape(*momentum.shape), shape(*master.shape)],
            (all_bases, near, momentum, master),
            [pltpu.VMEM((rep_rows, cols), F32)],
            flops=2 * 3 * rank * momentum.size * tps,
            moved=16 * momentum.size,
        )

    ring = [(index, (index + 2) % replicas) for index in range(replicas)]
    stages = replicas // 2
    last = 2 * stages - 1
    held, beside = list(block), [None, None]
    pieces = [(block[half], half, 0) for half in range(2)]
    errors, flat, weights = (), (), ()
    jobs = {1: "update", 2: "update", 3: "update", 4: "update", 5: "flat place", 2 * stages - 2: "place", 2 * stages - 1: "place"}
    near = spread(near, "tp", tps)
    updated = 0
    for step in range(2 * stages):
        stage, half = step // 2, step % 2
        if stage > 0:
            arrived = (held[half], beside[half])
            ids, errors, flat, weights, near, arrived = lax.optimization_barrier((ids, errors, flat, weights, near, arrived))
            held[half], beside[half] = arrived
            pieces += [(held[half], half, stage), (beside[half], half, stages + stage - 1)]
        if stage < stages - 1:
            here = held[half]
            held[half] = lax.ppermute(here, "rep", ring)
            beside[half] = swap(here, "rep", replicas, 1)
        elif half == 0:
            beside[half] = swap(held[half], "rep", replicas, 1)
        else:
            beside[half] = lax.ppermute(beside[half], "rep", ring)
        for job in jobs.get(step, "").split():
            if job == "update":
                errors = (update(updated, ids, errors),)
                updated += 1
            elif job == "flat":
                flat = flat_rows(ids, all_bases, jnp.stack(near))
            else:
                weights = (place(pieces, ids, weights),)
                pieces = []
    weights = place([(beside[half], half, last) for half in range(2)], ids, weights).reshape(matrices, width, cols)
    (new_error,) = errors
    new_momentum, new_master = flat
    return (new_error, right.reshape(matrices, rank, cols), new_momentum, new_master, weights)


def plain_orthonormal(factor):
    def gram_of(x):
        return jnp.einsum("krd,ksd->krs", x, x, precision=HIGHEST)

    gram_now = gram_of(factor)
    factor_scale = lax.rsqrt(jnp.trace(gram_now, axis1=1, axis2=2)[:, None, None] + NORM_EPSILON)
    ortho_basis = factor * factor_scale
    gram_now = gram_now * (factor_scale * factor_scale)
    for iteration in range(NS_STEPS):
        if iteration > 0:
            gram_now = gram_of(ortho_basis)
        ortho_basis = 1.5 * ortho_basis - 0.5 * jnp.einsum("krs,ksd->krd", gram_now, ortho_basis, precision=HIGHEST)
    return ortho_basis


def plain_local(grads, error, query, momentum, master):
    corrected = grads[0].astype(F32) + error[0]
    current = query
    replicas = lax.axis_size("rep")
    for _ in range(ROUNDS):
        partial_factor = jnp.einsum("kdf,krf->krd", corrected, current, precision=HIGHEST)
        ortho_basis = plain_orthonormal(lax.psum(partial_factor, ("rep", "tp")))
        partial_query = jnp.einsum("kdf,krd->krf", corrected, ortho_basis, precision=HIGHEST)
        current = lax.psum(partial_query, "rep") / replicas
    approx = jnp.einsum("krd,krf->kdf", ortho_basis, current, precision=HIGHEST)
    new_error = (corrected - approx)[None]
    matrices, width, cols = approx.shape
    block_rows = matrices * width // replicas
    own_block = lax.dynamic_slice_in_dim(
        approx.reshape(matrices * width, cols), lax.axis_index("rep") * block_rows, block_rows, 0
    )
    flat_approx = lax.all_to_all(own_block, "tp", split_axis=0, concat_axis=1, tiled=True)
    new_momentum = MOMENTUM_DECAY * momentum + flat_approx
    new_master = master - LEARNING_RATE * new_momentum
    by_columns = lax.all_to_all(new_master.astype(BF16), "tp", split_axis=1, concat_axis=0, tiled=True)
    weights = lax.all_gather(by_columns, "rep", axis=0, tiled=True).reshape(matrices, width, cols)
    return (new_error, current, new_momentum, new_master, weights)


def divides(mesh, matrices, rank, width, cols):
    replicas, tps = mesh.shape["rep"], mesh.shape["tp"]
    if replicas & (replicas - 1) or tps != 4 or replicas < 8 or matrices % tps or cols % (tps * LANES) or width % LANES:
        return False
    if math.gcd(matrices * width // replicas, width) % LANES:
        return False
    tp_rows = matrices // tps * rank
    tiles = 8 * LANES * replicas
    return tp_rows * width % tiles == 0 and tps * tp_rows * (cols // tps) % tiles == 0


def solution(mesh):
    placed = (
        P("rep", None, None, "tp"),
        P("rep", None, None, "tp"),
        P(None, None, "tp"),
        P(("rep", "tp"), None),
        P(("rep", "tp"), None),
    )

    def step(grads, error, query, momentum, master):
        fits = divides(mesh, grads.shape[1], query.shape[1], grads.shape[2], grads.shape[3])
        return jax.shard_map(
            local if fits else plain_local,
            mesh=mesh,
            in_specs=placed,
            out_specs=(
                P("rep", None, None, "tp"),
                P(None, None, "tp"),
                P(("rep", "tp"), None),
                P(("rep", "tp"), None),
                P(None, None, "tp"),
            ),
            check_vma=False,
        )(grads, error, query, momentum, master)

    return step
```

```python
import functools
import math

import jax
import jax.numpy as jnp
from jax import lax
from jax.experimental import pallas as pl
from jax.experimental.pallas import tpu as pltpu
from jax.sharding import PartitionSpec as P

ROUNDS = 2
NS_STEPS = 5


NORM_EPSILON = 1e-06
MOMENTUM_DECAY = 0.9
LEARNING_RATE = 0.5
HIGHEST = lax.Precision.HIGHEST
LANES = 128
F32, BF16 = jnp.float32, jnp.bfloat16
SCALARS = pl.BlockSpec(memory_space=pltpu.SMEM)


def two_terms(x):
    high = x.astype(BF16)
    return high, (x - high.astype(F32)).astype(BF16)


def dot(a, b, transposed=False):
    dims = (((1,), (1 if transposed else 0,)), ((), ()))
    return lax.dot_general(a, b, dims, preferred_element_type=F32)


def small_by_large(small, high, low, transposed):
    rows = small.shape[0]
    small_high, small_low = two_terms(small)
    both = dot(jnp.concatenate([small_high, small_low], axis=0), high, transposed)
    return both[:rows] + both[rows:] + dot(small_high, low, transposed)


def dot3(a, b):
    a_high, a_low = two_terms(a)
    b_high, b_low = two_terms(b)
    return dot(
        jnp.concatenate([a_high, a_low, a_high], axis=1),
        jnp.concatenate([b_high, b_high, b_low], axis=0),
    )


def stacked(right):
    right_high, right_low = two_terms(right)
    return jnp.concatenate([right_high, right_high, right_low], axis=0)


def lay_lanes(scratch, value):
    rows = value.shape[0]
    for block in range(value.shape[1] // LANES):
        scratch[block * rows : (block + 1) * rows] = value[:, block * LANES : (block + 1) * LANES]


def read_lanes(scratch, rows):
    blocks = scratch.shape[0] // rows
    return jnp.concatenate([scratch[block * rows : (block + 1) * rows] for block in range(blocks)], axis=1)


def part_at(index, rows):
    return pl.ds(pl.multiple_of(index * rows, 8), rows)


def split_parts(scratch, me, part_refs):
    rows = part_refs[0].shape[0]
    for offset, part_ref in enumerate(part_refs):
        part_ref[...] = scratch[part_at(me ^ offset, rows), :]


def join_parts(scratch, me, part_refs):
    rows = part_refs[0].shape[0]
    for offset, part_ref in enumerate(part_refs):
        scratch[part_at(me ^ offset, rows), :] = part_ref[...]


def sum_of(refs):
    values = [ref[...] for ref in refs]
    while len(values) > 1:
        values = [sum(values[at : at + 2][1:], values[at]) for at in range(0, len(values), 2)]
    return values[0]


def put_left(left, step, left_refs, per_tp):
    for which, left_ref in enumerate(left_refs):

        @pl.when(step // per_tp == which)
        def _():
            left_ref[...] = left


def first_left_kernel(per_tp, picked, ids_ref, grads_ref, error_ref, query_ref, high_ref, low_ref, *refs):
    left_refs, (grads_buffer, error_buffer, sems) = refs[:-3], refs[-3:]
    step = pl.program_id(0)

    def copies(k):
        matrix = picked(k, ids_ref)
        return [
            pltpu.make_async_copy(source.at[0, matrix], buffer.at[k], sems.at[which, k])
            for which, (source, buffer) in enumerate(((grads_ref, grads_buffer), (error_ref, error_buffer)))
        ]

    @pl.when(step == 0)
    def _():
        for k in range(grads_buffer.shape[0]):
            for copy in copies(k):
                copy.start()

    for copy in copies(step):
        copy.wait()
    high, low = two_terms(grads_buffer[step].astype(F32) + error_buffer[step])
    high_ref[0] = high
    low_ref[0] = low
    put_left(small_by_large(query_ref[0], high, low, True), step, left_refs, per_tp)


def left_kernel(per_tp, half, ids_ref, high_ref, low_ref, *refs):
    parts, left_refs, (scratch, current) = refs[:-4], refs[-4:-2], refs[-2:]
    step = pl.program_id(0)
    rank = left_refs[0].shape[0]
    rows = current.shape[0]
    lanes = rows * (current.shape[1] // LANES)

    @pl.when(step == 0)
    def _():
        join_parts(scratch, ids_ref[0], parts)
        current[...] = read_lanes(scratch.at[half * lanes : (half + 1) * lanes], rows)

    own = current[part_at(step, rank), :]
    put_left(small_by_large(own, high_ref[0], low_ref[0], True), step, left_refs, per_tp)


def split_kernel(tps, *refs):
    lay_lanes(refs[-1], sum_of(refs[:tps]))


def total_kernel(parts_ref, out_ref):
    summed = sum_of([parts_ref.at[part] for part in range(parts_ref.shape[0])])
    for part in range(parts_ref.shape[0]):
        out_ref[part] = summed


def sum_kernel(scale, *refs):
    summed = sum_of(refs[:-1])
    refs[-1][...] = summed if scale == 1.0 else summed * scale


def mixing(left, rank):
    rows = left.shape[0]
    row_id = lax.broadcasted_iota(jnp.int32, (rows, rows), 0)
    col_id = lax.broadcasted_iota(jnp.int32, (rows, rows), 1)
    same = (row_id // rank) == (col_id // rank)
    eye = (row_id == col_id).astype(F32)
    left_high, left_low = two_terms(left)
    cross = dot(left_high, left_low, True)
    gram = jnp.where(same, dot(left_high, left_high, True) + cross + cross.T, 0.0)
    diagonal = jnp.sum(gram * eye, axis=0, keepdims=True)
    trace = jnp.sum(jnp.where(same, diagonal, 0.0), axis=1, keepdims=True) + NORM_EPSILON
    scale = lax.rsqrt(trace)
    scale = scale * (1.5 - 0.5 * trace * scale * scale)
    gram = gram * (scale * scale)
    step = 1.5 * eye - 0.5 * gram
    mixed = step * scale
    for _ in range(NS_STEPS - 1):
        gram = dot3(dot3(step, gram), step)
        step = 1.5 * eye - 0.5 * gram
        mixed = dot3(step, mixed)
    return mixed


def basis_kernel(rank, left_ref, basis_ref):
    rows = basis_ref.shape[0]
    left = read_lanes(left_ref, rows)
    padded = jnp.concatenate([left, jnp.zeros((-rows % LANES, left.shape[1]), F32)], axis=0)
    basis_ref[...] = dot3(mixing(padded, rank), padded)[:rows]


def right_kernel(per_tp, ids_ref, first_ref, second_ref, high_ref, low_ref, *refs):
    step = pl.program_id(0)
    rank = first_ref.shape[0] // per_tp
    at = part_at(step % per_tp, rank)
    own = jnp.where(step // per_tp == 0, first_ref[at, :], second_ref[at, :])
    product_now = small_by_large(own, high_ref[0], low_ref[0], False)
    if len(refs) == 1:
        refs[0][...] = product_now
        return
    before_ref, part_refs, (scratch, right) = refs[0], refs[1:-2], refs[-2:]
    right[part_at(step, rank), :] = product_now

    @pl.when(step == pl.num_programs(0) - 1)
    def _():
        lanes = scratch.shape[0] // 2
        lay_lanes(scratch.at[:lanes], before_ref[...])
        lay_lanes(scratch.at[lanes:], right[...])
        split_parts(scratch, ids_ref[0], part_refs)


def rows_of_update(basis_ref, right_ref, scratch, first_unit, unit, per_tp, rank, tp, first_matrix):
    per_matrix = basis_ref.shape[1] // unit
    for u in range(scratch.shape[0] // unit):
        at = first_unit + u
        matrix = at // per_matrix
        slot = ((matrix // per_tp) ^ tp) * per_tp + matrix % per_tp
        lanes = pl.ds(pl.multiple_of((at % per_matrix) * unit, LANES), unit)
        factor = basis_ref[part_at(slot, rank), lanes]
        right = right_ref[part_at(matrix - first_matrix, rank), :]
        scratch[u * unit : (u + 1) * unit] = product(factor, right)


def product(factor, right):
    high, low = two_terms(factor.T)
    return dot(jnp.concatenate([high, low, high], axis=1), stacked(right))


def late_kernel(unit, per_tp, rank, ids_ref, basis_ref, *refs):
    query_ref, *weight_refs, lanes, approx = refs[-5:]
    tps = query_ref.shape[0] // (per_tp * rank)
    part_refs, base_refs = refs[: -5 - tps], refs[-5 - tps : -5]
    rows = query_ref.shape[0] // 2
    tp = ids_ref[1]
    join_parts(lanes, ids_ref[0], part_refs)
    for half in range(2):
        per_half = lanes.shape[0] // 2
        value = read_lanes(lanes.at[half * per_half : (half + 1) * per_half], rows)
        for which in range(2):
            owner = tp ^ (2 * half + which)
            query_ref[part_at(owner, rows // 2), :] = value[which * (rows // 2) : (which + 1) * (rows // 2)]
    units = approx.shape[0] // unit
    rows_of_update(basis_ref, query_ref, approx, ids_ref[0] * units, unit, per_tp, rank, tp, 0)
    for offset, base_ref in enumerate(base_refs):
        at = part_at(tp ^ offset, base_ref.shape[0])
        approx[at, :] = base_ref[...] - LEARNING_RATE * approx[at, :]
    for half, weight_ref in enumerate(weight_refs):
        per_half = weight_ref.shape[0]
        weight_ref[...] = approx[half * per_half : (half + 1) * per_half].astype(BF16)


def owner_of(step, rep, replicas):
    half = replicas // 2
    return ((rep ^ (step // half)) + 2 * replicas - 2 * (step % half)) % replicas


def place_kernel(count, ids_ref, *refs):
    for at, part_ref in enumerate(refs[:count]):

        @pl.when(pl.program_id(0) == at)
        def _():
            refs[-1][0, 0] = part_ref[...]


def update_kernel(rank, ids_ref, basis_ref, right_ref, high_ref, low_ref, *refs):
    at = part_at(pl.program_id(0), rank)
    approx = product(basis_ref[at, :], right_ref[at, :])
    refs[-1][0, 0] = high_ref[0].astype(F32) + low_ref[0].astype(F32) - approx


def flat_kernel(unit, per_tp, rank, matrices, ids_ref, basis_ref, near_ref, momentum_ref, master_ref, new_momentum_ref, new_master_ref, approx):
    units = approx.shape[0] // unit
    spans = near_ref.shape[1] // rank
    first_unit = ids_ref[0] * units
    first = jnp.minimum(first_unit // (basis_ref.shape[1] // unit), matrices - spans)
    rows_of_update(basis_ref, near_ref.at[0], approx, first_unit, unit, per_tp, rank, ids_ref[1], first)
    own = approx[part_at(ids_ref[1], momentum_ref.shape[0]), :]
    new_momentum = MOMENTUM_DECAY * momentum_ref[...] + own
    new_momentum_ref[...] = new_momentum
    new_master_ref[...] = master_ref[...] - LEARNING_RATE * new_momentum


def shape(*dims, dtype=F32):
    return jax.ShapeDtypeStruct(dims, dtype)


def grant(mib):
    return pltpu.CompilerParams(vmem_limit_bytes=mib * 2**20)


def whole_call(kernel, name, out_shape, operands, ids=None, scratch=()):
    specs = [pl.BlockSpec(memory_space=pltpu.VMEM)] * len(operands)
    many = isinstance(out_shape, (list, tuple))
    out_spec = pl.BlockSpec(memory_space=pltpu.VMEM)
    moved = sum(4 * x.size for x in operands)
    if ids is not None:
        operands, specs = [ids, *operands], [SCALARS, *specs]
    return pl.pallas_call(
        kernel,
        in_specs=specs,
        out_specs=[out_spec] * len(out_shape) if many else out_spec,
        out_shape=out_shape,
        scratch_shapes=list(scratch),
        compiler_params=grant(12),
        name=name,
        cost_estimate=pl.CostEstimate(flops=moved, bytes_accessed=2 * moved, transcendentals=0),
    )(*operands)


def grid_call(kernel, name, ids, grid, in_specs, out_specs, out_shape, operands, scratch=(), aliases=None, flops=0, moved=0, mib=14):
    return pl.pallas_call(
        kernel,
        grid_spec=pltpu.PrefetchScalarGridSpec(
            num_scalar_prefetch=1,
            grid=grid,
            in_specs=in_specs,
            out_specs=out_specs,
            scratch_shapes=list(scratch),
        ),
        out_shape=out_shape,
        input_output_aliases=aliases or {},
        compiler_params=grant(mib),
        name=name,
        cost_estimate=pl.CostEstimate(flops=flops, bytes_accessed=moved, transcendentals=0),
    )(ids, *operands)


def swap(x, axis, size, offset):
    return lax.ppermute(x, axis, [(index, index ^ offset) for index in range(size)])


def scattered(parts, replicas):
    return [parts[0]] + [swap(parts[offset], "rep", replicas, offset) for offset in range(1, replicas)]


def spread(part, axis, size):
    return [part] + [swap(part, axis, size, offset) for offset in range(1, size)]


def local(grads, error, query, momentum, master):
    replicas, tps = lax.axis_size("rep"), lax.axis_size("tp")
    rep, tp = lax.axis_index("rep"), lax.axis_index("tp")
    ids = jnp.stack([rep, tp]).astype(jnp.int32)
    _, matrices, width, cols = grads.shape
    rank = query.shape[1]
    per_tp = matrices // tps
    per_half = 2 * per_tp
    halves = tps // 2
    tp_rows = per_tp * rank
    left_part = tp_rows * width // LANES // replicas
    right_part = tps * tp_rows * cols // LANES // replicas
    own_rows = momentum.shape[0]
    flops = 2 * 3 * per_half * rank * width * cols
    elements = per_half * width * cols

    def matrix_of(half, k, at):
        return (at[1] ^ (2 * half + k // per_tp)) * per_tp + k % per_tp

    term_spec = pl.BlockSpec((1, width, cols), lambda k, at: (k, 0, 0))
    term_shape = pltpu.VMEM((per_half, width, cols), BF16)
    left_specs = [
        pl.BlockSpec((rank, width), lambda k, at, which=which: (jnp.clip(k - which * per_tp, 0, per_tp - 1), 0))
        for which in range(2)
    ]
    left_shapes = [shape(tp_rows, width)] * 2

    def whole_spec(*dims):
        return pl.BlockSpec(dims, lambda k, at: (0,) * len(dims))

    pieces = []
    for offset in range(tps):
        column = (tp ^ offset) * cols
        piece = lax.dynamic_slice_in_dim(master, column, cols, 1)
        pieces.append(piece - (LEARNING_RATE * MOMENTUM_DECAY) * lax.dynamic_slice_in_dim(momentum, column, cols, 1))

    terms, lefts = [None] * halves, [None] * tps
    for half in reversed(range(halves)):
        picked = functools.partial(matrix_of, half)
        high, low, *out = grid_call(
            functools.partial(first_left_kernel, per_tp, picked),
            "first_left",
            ids,
            (per_half,),
            [
                pl.BlockSpec(memory_space=pltpu.HBM),
                pl.BlockSpec(memory_space=pltpu.HBM),
                pl.BlockSpec((1, rank, cols), lambda k, at, picked=picked: (picked(k, at), 0, 0)),
            ],
            [term_spec, term_spec, *left_specs],
            [term_shape, term_shape, *left_shapes],
            (*(pltpu.with_memory_space_constraint(x, pltpu.HBM) for x in (grads, error)), query),
            [
                pltpu.VMEM((per_half, width, cols), BF16),
                pltpu.VMEM((per_half, width, cols), F32),
                pltpu.SemaphoreType.DMA((2, per_half)),
            ],
            mib=26,
            flops=flops,
            moved=10 * elements,
        )
        terms[half] = tuple(pltpu.with_memory_space_constraint(term, pltpu.VMEM) for term in (high, low))
        lefts[2 * half : 2 * half + 2] = out
        ids, _ = lax.optimization_barrier((ids, out[0]))

    for power_pass in range(ROUNDS):
        met = [lefts[0]] + [swap(lefts[offset], "tp", tps, offset) for offset in reversed(range(1, tps))]
        parts = whole_call(
            functools.partial(split_kernel, tps), "left_split", shape(left_part * replicas, LANES), met
        )
        if power_pass == 0:
            parts, pieces = lax.optimization_barrier((parts, pieces))
            base = [pieces[0]]
        parts = parts.reshape(replicas, left_part, LANES)
        parts = lax.all_to_all(parts, "rep", split_axis=0, concat_axis=0, tiled=True)
        parts = whole_call(total_kernel, "left_sum", shape(*parts.shape), [parts])
        parts = lax.all_to_all(parts, "rep", split_axis=0, concat_axis=0, tiled=True)
        basis = whole_call(
            functools.partial(basis_kernel, rank), "basis", shape(tp_rows, width), [parts.reshape(-1, LANES)]
        )
        across = swap(basis, "tp", tps, 2)
        bases = [basis, swap(basis, "tp", tps, 1)]
        before = grid_call(
            functools.partial(right_kernel, per_tp),
            "right_near",
            ids,
            (per_half,),
            [whole_spec(tp_rows, width), whole_spec(tp_rows, width), term_spec, term_spec],
            pl.BlockSpec((rank, cols), lambda k, at: (k, 0)),
            shape(2 * tp_rows, cols),
            (*bases, *terms[0]),
            flops=flops,
            moved=4 * elements,
        )
        before, across = lax.optimization_barrier((before, across))
        bases += [across, swap(across, "tp", tps, 1)]
        parts = grid_call(
            functools.partial(right_kernel, per_tp),
            "right_far",
            ids,
            (per_half,),
            [whole_spec(tp_rows, width), whole_spec(tp_rows, width), term_spec, term_spec, whole_spec(2 * tp_rows, cols)],
            [whole_spec(right_part, LANES)] * replicas,
            [shape(right_part, LANES)] * replicas,
            (*bases[2:], *terms[1], before),
            [pltpu.VMEM((right_part * replicas, LANES), F32), pltpu.VMEM((2 * tp_rows, cols), F32)],
            flops=flops,
            moved=4 * elements,
        )
        met = scattered(parts, replicas)
        arrived = [swap(pieces[offset], "tp", tps, offset) for offset in ((1, 2) if power_pass == 0 else range(3, tps))]
        met, pieces, arrived = lax.optimization_barrier((met, pieces, arrived))
        base += arrived
        part = whole_call(functools.partial(sum_kernel, 1.0 / replicas), "right_sum", shape(right_part, LANES), met)
        rights = spread(part, "rep", replicas)
        if power_pass < ROUNDS - 1:
            for half in reversed(range(halves)):
                lefts[2 * half : 2 * half + 2] = grid_call(
                    functools.partial(left_kernel, per_tp, half),
                    "left",
                    ids,
                    (per_half,),
                    [term_spec, term_spec] + [whole_spec(right_part, LANES)] * replicas,
                    left_specs,
                    left_shapes,
                    (*terms[half], *rights),
                    [pltpu.VMEM((right_part * replicas, LANES), F32), pltpu.VMEM((2 * tp_rows, cols), F32)],
                    flops=flops,
                    moved=10 * elements,
                )

    all_bases = jnp.concatenate(bases, axis=0)
    rep_rows = tps * own_rows
    unit = math.gcd(rep_rows, width)
    right, *block = whole_call(
        functools.partial(late_kernel, unit, per_tp, rank),
        "late_rows",
        [shape(matrices * rank, cols)] + [shape(rep_rows // 2, cols, dtype=BF16)] * 2,
        [all_bases, *rights, *base],
        ids,
        [pltpu.VMEM((right_part * replicas, LANES), F32), pltpu.VMEM((rep_rows, cols), F32)],
    )
    spans = -(-(width - unit + rep_rows) // width)
    first = jnp.minimum(rep * rep_rows // width, matrices - spans)
    near = lax.dynamic_slice_in_dim(right, first * rank, spans * rank, 0)

    def update(slot, ids, before):
        half, start = slot // 2, slot % 2 * per_tp
        return grid_call(
            functools.partial(update_kernel, rank),
            "update",
            ids,
            (per_tp,),
            [
                pl.BlockSpec((tp_rows, width), lambda j, at: (slot, 0)),
                pl.BlockSpec((tp_rows, cols), lambda j, at: (at[1] ^ slot, 0)),
                pl.BlockSpec((1, width, cols), lambda j, at: (start + j, 0, 0)),
                pl.BlockSpec((1, width, cols), lambda j, at: (start + j, 0, 0)),
            ]
            + [pl.BlockSpec(memory_space=pl.ANY)] * len(before),
            pl.BlockSpec((1, 1, width, cols), lambda j, at: (0, (at[1] ^ slot) * per_tp + j, 0, 0)),
            shape(*error.shape),
            (all_bases, right, *terms[half], *before),
            aliases={5: 0} if before else None,
            flops=2 * 3 * rank * error.size // tps,
            moved=8 * error.size // tps,
        )

    def place(pieces, ids, before):
        count = len(pieces)

        def where(k, at):
            at_half, step = pieces[-1][1:]
            for index in range(count - 1):
                at_half = jnp.where(k == index, pieces[index][1], at_half)
                step = jnp.where(k == index, pieces[index][2], step)
            return (owner_of(step, at[0], replicas), at_half, 0, 0)

        return grid_call(
            functools.partial(place_kernel, count),
            "place",
            ids,
            (count,),
            [pl.BlockSpec((rep_rows // 2, cols), lambda k, at: (0, 0))] * count
            + [pl.BlockSpec(memory_space=pl.ANY)] * len(before),
            pl.BlockSpec((1, 1, rep_rows // 2, cols), where),
            shape(replicas, 2, rep_rows // 2, cols, dtype=BF16),
            (*[piece[0] for piece in pieces], *before),
            aliases={1 + count: 0} if before else None,
            moved=4 * count * rep_rows * cols,
        )

    def flat_rows(ids, all_bases, near):
        wide = pl.BlockSpec((own_rows, cols), lambda s, at: (0, at[1] ^ s))
        return grid_call(
            functools.partial(flat_kernel, unit, per_tp, rank, matrices),
            "flat_rows",
            ids,
            (tps,),
            [
                whole_spec(matrices * rank, width),
                pl.BlockSpec((1, spans * rank, cols), lambda s, at: (s, 0, 0)),
                wide,
                wide,
            ],
            [wide, wide],
            [shape(*momentum.shape), shape(*master.shape)],
            (all_bases, near, momentum, master),
            [pltpu.VMEM((rep_rows, cols), F32)],
            flops=2 * 3 * rank * momentum.size * tps,
            moved=16 * momentum.size,
        )

    ring = [(index, (index + 2) % replicas) for index in range(replicas)]
    stages = replicas // 2
    last = 2 * stages - 1
    held, beside = list(block), [None, None]
    pieces = [(block[half], half, 0) for half in range(2)]
    errors, flat, weights = (), (), ()
    jobs = {1: "update", 2: "update", 3: "update", 4: "update", 5: "flat place", 2 * stages - 2: "place", 2 * stages - 1: "place"}
    near = spread(near, "tp", tps)
    updated = 0
    for step in range(2 * stages):
        stage, half = step // 2, step % 2
        if stage > 0:
            arrived = (held[half], beside[half])
            ids, errors, flat, weights, near, arrived = lax.optimization_barrier((ids, errors, flat, weights, near, arrived))
            held[half], beside[half] = arrived
            pieces += [(held[half], half, stage), (beside[half], half, stages + stage - 1)]
        if stage < stages - 1:
            here = held[half]
            held[half] = lax.ppermute(here, "rep", ring)
            beside[half] = swap(here, "rep", replicas, 1)
        elif half == 0:
            beside[half] = swap(held[half], "rep", replicas, 1)
        else:
            beside[half] = lax.ppermute(beside[half], "rep", ring)
        for job in jobs.get(step, "").split():
            if job == "update":
                errors = (update(updated, ids, errors),)
                updated += 1
            elif job == "flat":
                flat = flat_rows(ids, all_bases, jnp.stack(near))
            else:
                weights = (place(pieces, ids, weights),)
                pieces = []
    weights = place([(beside[half], half, last) for half in range(2)], ids, weights).reshape(matrices, width, cols)
    (new_error,) = errors
    new_momentum, new_master = flat
    return (new_error, right.reshape(matrices, rank, cols), new_momentum, new_master, weights)


def plain_orthonormal(factor):
    def gram_of(x):
        return jnp.einsum("krd,ksd->krs", x, x, precision=HIGHEST)

    gram_now = gram_of(factor)
    factor_scale = lax.rsqrt(jnp.trace(gram_now, axis1=1, axis2=2)[:, None, None] + NORM_EPSILON)
    ortho_basis = factor * factor_scale
    gram_now = gram_now * (factor_scale * factor_scale)
    for iteration in range(NS_STEPS):
        if iteration > 0:
            gram_now = gram_of(ortho_basis)
        ortho_basis = 1.5 * ortho_basis - 0.5 * jnp.einsum("krs,ksd->krd", gram_now, ortho_basis, precision=HIGHEST)
    return ortho_basis


def plain_local(grads, error, query, momentum, master):
    corrected = grads[0].astype(F32) + error[0]
    current = query
    replicas = lax.axis_size("rep")
    for _ in range(ROUNDS):
        partial_factor = jnp.einsum("kdf,krf->krd", corrected, current, precision=HIGHEST)
        ortho_basis = plain_orthonormal(lax.psum(partial_factor, ("rep", "tp")))
        partial_query = jnp.einsum("kdf,krd->krf", corrected, ortho_basis, precision=HIGHEST)
        current = lax.psum(partial_query, "rep") / replicas
    approx = jnp.einsum("krd,krf->kdf", ortho_basis, current, precision=HIGHEST)
    new_error = (corrected - approx)[None]
    matrices, width, cols = approx.shape
    block_rows = matrices * width // replicas
    own_block = lax.dynamic_slice_in_dim(
        approx.reshape(matrices * width, cols), lax.axis_index("rep") * block_rows, block_rows, 0
    )
    flat_approx = lax.all_to_all(own_block, "tp", split_axis=0, concat_axis=1, tiled=True)
    new_momentum = MOMENTUM_DECAY * momentum + flat_approx
    new_master = master - LEARNING_RATE * new_momentum
    by_columns = lax.all_to_all(new_master.astype(BF16), "tp", split_axis=1, concat_axis=0, tiled=True)
    weights = lax.all_gather(by_columns, "rep", axis=0, tiled=True).reshape(matrices, width, cols)
    return (new_error, current, new_momentum, new_master, weights)


def divides(mesh, matrices, rank, width, cols):
    replicas, tps = mesh.shape["rep"], mesh.shape["tp"]
    if replicas & (replicas - 1) or tps != 4 or replicas < 8 or matrices % tps or cols % (tps * LANES) or width % LANES:
        return False
    if math.gcd(matrices * width // replicas, width) % LANES:
        return False
    tp_rows = matrices // tps * rank
    tiles = 8 * LANES * replicas
    return tp_rows * width % tiles == 0 and tps * tp_rows * (cols // tps) % tiles == 0


def solution(mesh):
    placed = (
        P("rep", None, None, "tp"),
        P("rep", None, None, "tp"),
        P(None, None, "tp"),
        P(("rep", "tp"), None),
        P(("rep", "tp"), None),
    )

    def step(grads, error, query, momentum, master):
        fits = divides(mesh, grads.shape[1], query.shape[1], grads.shape[2], grads.shape[3])
        return jax.shard_map(
            local if fits else plain_local,
            mesh=mesh,
            in_specs=placed,
            out_specs=(
                P("rep", None, None, "tp"),
                P(None, None, "tp"),
                P(("rep", "tp"), None),
                P(("rep", "tp"), None),
                P(None, None, "tp"),
            ),
            check_vma=False,
        )(grads, error, query, momentum, master)

    return step
```

```python
import functools
import math

import jax
import jax.numpy as jnp
from jax import lax
from jax.experimental import pallas as pl
from jax.experimental.pallas import tpu as pltpu
from jax.sharding import PartitionSpec as P

ROUNDS = 2
NS_STEPS = 5


NORM_EPSILON = 1e-06
MOMENTUM_DECAY = 0.9
LEARNING_RATE = 0.5
HIGHEST = lax.Precision.HIGHEST
LANES = 128
F32, BF16 = jnp.float32, jnp.bfloat16
SCALARS = pl.BlockSpec(memory_space=pltpu.SMEM)


def two_terms(x):
    high = x.astype(BF16)
    return high, (x - high.astype(F32)).astype(BF16)


def dot(a, b, transposed=False):
    dims = (((1,), (1 if transposed else 0,)), ((), ()))
    return lax.dot_general(a, b, dims, preferred_element_type=F32)


def small_by_large(small, high, low, transposed):
    rows = small.shape[0]
    small_high, small_low = two_terms(small)
    both = dot(jnp.concatenate([small_high, small_low], axis=0), high, transposed)
    return both[:rows] + both[rows:] + dot(small_high, low, transposed)


def dot3(a, b):
    a_high, a_low = two_terms(a)
    b_high, b_low = two_terms(b)
    return dot(
        jnp.concatenate([a_high, a_low, a_high], axis=1),
        jnp.concatenate([b_high, b_high, b_low], axis=0),
    )


def stacked(right):
    right_high, right_low = two_terms(right)
    return jnp.concatenate([right_high, right_high, right_low], axis=0)


def lay_lanes(scratch, value):
    rows = value.shape[0]
    for block in range(value.shape[1] // LANES):
        scratch[block * rows : (block + 1) * rows] = value[:, block * LANES : (block + 1) * LANES]


def read_lanes(scratch, rows):
    blocks = scratch.shape[0] // rows
    return jnp.concatenate([scratch[block * rows : (block + 1) * rows] for block in range(blocks)], axis=1)


def part_at(index, rows):
    return pl.ds(pl.multiple_of(index * rows, 8), rows)


def split_parts(scratch, me, part_refs):
    rows = part_refs[0].shape[0]
    for offset, part_ref in enumerate(part_refs):
        part_ref[...] = scratch[part_at(me ^ offset, rows), :]


def join_parts(scratch, me, part_refs):
    rows = part_refs[0].shape[0]
    for offset, part_ref in enumerate(part_refs):
        scratch[part_at(me ^ offset, rows), :] = part_ref[...]


def sum_of(refs):
    values = [ref[...] for ref in refs]
    while len(values) > 1:
        values = [sum(values[at : at + 2][1:], values[at]) for at in range(0, len(values), 2)]
    return values[0]


def put_left(left, step, left_refs, per_tp):
    for which, left_ref in enumerate(left_refs):

        @pl.when(step // per_tp == which)
        def _():
            left_ref[...] = left


def first_left_kernel(per_tp, picked, ids_ref, grads_ref, error_ref, query_ref, high_ref, low_ref, *refs):
    left_refs, (grads_buffer, error_buffer, sems) = refs[:-3], refs[-3:]
    step = pl.program_id(0)

    def copies(k):
        matrix = picked(k, ids_ref)
        return [
            pltpu.make_async_copy(source.at[0, matrix], buffer.at[k], sems.at[which, k])
            for which, (source, buffer) in enumerate(((grads_ref, grads_buffer), (error_ref, error_buffer)))
        ]

    @pl.when(step == 0)
    def _():
        for k in range(grads_buffer.shape[0]):
            for copy in copies(k):
                copy.start()

    for copy in copies(step):
        copy.wait()
    high, low = two_terms(grads_buffer[step].astype(F32) + error_buffer[step])
    high_ref[0] = high
    low_ref[0] = low
    put_left(small_by_large(query_ref[0], high, low, True), step, left_refs, per_tp)


def left_kernel(per_tp, half, ids_ref, high_ref, low_ref, *refs):
    parts, left_refs, (scratch, current) = refs[:-4], refs[-4:-2], refs[-2:]
    step = pl.program_id(0)
    rank = left_refs[0].shape[0]
    rows = current.shape[0]
    lanes = rows * (current.shape[1] // LANES)

    @pl.when(step == 0)
    def _():
        join_parts(scratch, ids_ref[0], parts)
        current[...] = read_lanes(scratch.at[half * lanes : (half + 1) * lanes], rows)

    own = current[part_at(step, rank), :]
    put_left(small_by_large(own, high_ref[0], low_ref[0], True), step, left_refs, per_tp)


def split_kernel(tps, *refs):
    lay_lanes(refs[-1], sum_of(refs[:tps]))


def total_kernel(parts_ref, out_ref):
    summed = sum_of([parts_ref.at[part] for part in range(parts_ref.shape[0])])
    for part in range(parts_ref.shape[0]):
        out_ref[part] = summed


def sum_kernel(scale, *refs):
    summed = sum_of(refs[:-1])
    refs[-1][...] = summed if scale == 1.0 else summed * scale


def mixing(left, rank):
    rows = left.shape[0]
    row_id = lax.broadcasted_iota(jnp.int32, (rows, rows), 0)
    col_id = lax.broadcasted_iota(jnp.int32, (rows, rows), 1)
    same = (row_id // rank) == (col_id // rank)
    eye = (row_id == col_id).astype(F32)
    left_high, left_low = two_terms(left)
    cross = dot(left_high, left_low, True)
    gram = jnp.where(same, dot(left_high, left_high, True) + cross + cross.T, 0.0)
    diagonal = jnp.sum(gram * eye, axis=0, keepdims=True)
    trace = jnp.sum(jnp.where(same, diagonal, 0.0), axis=1, keepdims=True) + NORM_EPSILON
    scale = lax.rsqrt(trace)
    scale = scale * (1.5 - 0.5 * trace * scale * scale)
    gram = gram * (scale * scale)
    step = 1.5 * eye - 0.5 * gram
    mixed = step * scale
    for _ in range(NS_STEPS - 1):
        gram = dot3(dot3(step, gram), step)
        step = 1.5 * eye - 0.5 * gram
        mixed = dot3(step, mixed)
    return mixed


def basis_kernel(rank, left_ref, basis_ref):
    rows = basis_ref.shape[0]
    left = read_lanes(left_ref, rows)
    padded = jnp.concatenate([left, jnp.zeros((-rows % LANES, left.shape[1]), F32)], axis=0)
    basis_ref[...] = dot3(mixing(padded, rank), padded)[:rows]


def right_kernel(per_tp, ids_ref, first_ref, second_ref, high_ref, low_ref, *refs):
    step = pl.program_id(0)
    rank = first_ref.shape[0] // per_tp
    at = part_at(step % per_tp, rank)
    own = jnp.where(step // per_tp == 0, first_ref[at, :], second_ref[at, :])
    product_now = small_by_large(own, high_ref[0], low_ref[0], False)
    if len(refs) == 1:
        refs[0][...] = product_now
        return
    before_ref, part_refs, (scratch, right) = refs[0], refs[1:-2], refs[-2:]
    right[part_at(step, rank), :] = product_now

    @pl.when(step == pl.num_programs(0) - 1)
    def _():
        lanes = scratch.shape[0] // 2
        lay_lanes(scratch.at[:lanes], before_ref[...])
        lay_lanes(scratch.at[lanes:], right[...])
        split_parts(scratch, ids_ref[0], part_refs)


def rows_of_update(basis_ref, right_ref, scratch, first_unit, unit, per_tp, rank, tp, first_matrix):
    per_matrix = basis_ref.shape[1] // unit
    for u in range(scratch.shape[0] // unit):
        at = first_unit + u
        matrix = at // per_matrix
        slot = ((matrix // per_tp) ^ tp) * per_tp + matrix % per_tp
        lanes = pl.ds(pl.multiple_of((at % per_matrix) * unit, LANES), unit)
        factor = basis_ref[part_at(slot, rank), lanes]
        right = right_ref[part_at(matrix - first_matrix, rank), :]
        scratch[u * unit : (u + 1) * unit] = product(factor, right)


def product(factor, right):
    high, low = two_terms(factor.T)
    return dot(jnp.concatenate([high, low, high], axis=1), stacked(right))


def late_kernel(unit, per_tp, rank, ids_ref, basis_ref, *refs):
    query_ref, *weight_refs, lanes, approx = refs[-5:]
    tps = query_ref.shape[0] // (per_tp * rank)
    part_refs, base_refs = refs[: -5 - tps], refs[-5 - tps : -5]
    rows = query_ref.shape[0] // 2
    tp = ids_ref[1]
    join_parts(lanes, ids_ref[0], part_refs)
    for half in range(2):
        per_half = lanes.shape[0] // 2
        value = read_lanes(lanes.at[half * per_half : (half + 1) * per_half], rows)
        for which in range(2):
            owner = tp ^ (2 * half + which)
            query_ref[part_at(owner, rows // 2), :] = value[which * (rows // 2) : (which + 1) * (rows // 2)]
    units = approx.shape[0] // unit
    rows_of_update(basis_ref, query_ref, approx, ids_ref[0] * units, unit, per_tp, rank, tp, 0)
    for offset, base_ref in enumerate(base_refs):
        at = part_at(tp ^ offset, base_ref.shape[0])
        approx[at, :] = base_ref[...] - LEARNING_RATE * approx[at, :]
    for half, weight_ref in enumerate(weight_refs):
        per_half = weight_ref.shape[0]
        weight_ref[...] = approx[half * per_half : (half + 1) * per_half].astype(BF16)


def owner_of(step, rep, replicas):
    half = replicas // 2
    return ((rep ^ (step // half)) + 2 * replicas - 2 * (step % half)) % replicas


def place_kernel(count, ids_ref, *refs):
    for at, part_ref in enumerate(refs[:count]):

        @pl.when(pl.program_id(0) == at)
        def _():
            refs[-1][0, 0] = part_ref[...]


def update_kernel(rank, ids_ref, basis_ref, right_ref, grads_ref, error_ref, *refs):
    at = part_at(pl.program_id(0), rank)
    approx = product(basis_ref[at, :], right_ref[at, :])
    refs[-1][0, 0] = grads_ref[0, 0].astype(F32) + error_ref[0, 0] - approx


def flat_kernel(unit, per_tp, rank, matrices, ids_ref, basis_ref, near_ref, momentum_ref, master_ref, new_momentum_ref, new_master_ref, approx):
    units = approx.shape[0] // unit
    spans = near_ref.shape[1] // rank
    first_unit = ids_ref[0] * units
    first = jnp.minimum(first_unit // (basis_ref.shape[1] // unit), matrices - spans)
    rows_of_update(basis_ref, near_ref.at[0], approx, first_unit, unit, per_tp, rank, ids_ref[1], first)
    own = approx[part_at(ids_ref[1], momentum_ref.shape[0]), :]
    new_momentum = MOMENTUM_DECAY * momentum_ref[...] + own
    new_momentum_ref[...] = new_momentum
    new_master_ref[...] = master_ref[...] - LEARNING_RATE * new_momentum


def shape(*dims, dtype=F32):
    return jax.ShapeDtypeStruct(dims, dtype)


def grant(mib):
    return pltpu.CompilerParams(vmem_limit_bytes=mib * 2**20)


def whole_call(kernel, name, out_shape, operands, ids=None, scratch=()):
    specs = [pl.BlockSpec(memory_space=pltpu.VMEM)] * len(operands)
    many = isinstance(out_shape, (list, tuple))
    out_spec = pl.BlockSpec(memory_space=pltpu.VMEM)
    moved = sum(4 * x.size for x in operands)
    if ids is not None:
        operands, specs = [ids, *operands], [SCALARS, *specs]
    return pl.pallas_call(
        kernel,
        in_specs=specs,
        out_specs=[out_spec] * len(out_shape) if many else out_spec,
        out_shape=out_shape,
        scratch_shapes=list(scratch),
        compiler_params=grant(12),
        name=name,
        cost_estimate=pl.CostEstimate(flops=moved, bytes_accessed=2 * moved, transcendentals=0),
    )(*operands)


def grid_call(kernel, name, ids, grid, in_specs, out_specs, out_shape, operands, scratch=(), aliases=None, flops=0, moved=0, mib=14):
    return pl.pallas_call(
        kernel,
        grid_spec=pltpu.PrefetchScalarGridSpec(
            num_scalar_prefetch=1,
            grid=grid,
            in_specs=in_specs,
            out_specs=out_specs,
            scratch_shapes=list(scratch),
        ),
        out_shape=out_shape,
        input_output_aliases=aliases or {},
        compiler_params=grant(mib),
        name=name,
        cost_estimate=pl.CostEstimate(flops=flops, bytes_accessed=moved, transcendentals=0),
    )(ids, *operands)


def swap(x, axis, size, offset):
    return lax.ppermute(x, axis, [(index, index ^ offset) for index in range(size)])


def scattered(parts, replicas):
    return [parts[0]] + [swap(parts[offset], "rep", replicas, offset) for offset in range(1, replicas)]


def spread(part, axis, size):
    return [part] + [swap(part, axis, size, offset) for offset in range(1, size)]


def local(grads, error, query, momentum, master):
    replicas, tps = lax.axis_size("rep"), lax.axis_size("tp")
    rep, tp = lax.axis_index("rep"), lax.axis_index("tp")
    ids = jnp.stack([rep, tp]).astype(jnp.int32)
    grads, error, query = (pltpu.with_memory_space_constraint(x, pltpu.HBM) for x in (grads, error, query))
    _, matrices, width, cols = grads.shape
    rank = query.shape[1]
    per_tp = matrices // tps
    per_half = 2 * per_tp
    halves = tps // 2
    tp_rows = per_tp * rank
    left_part = tp_rows * width // LANES // replicas
    right_part = tps * tp_rows * cols // LANES // replicas
    own_rows = momentum.shape[0]
    flops = 2 * 3 * per_half * rank * width * cols
    elements = per_half * width * cols

    def matrix_of(half, k, at):
        return (at[1] ^ (2 * half + k // per_tp)) * per_tp + k % per_tp

    term_spec = pl.BlockSpec((1, width, cols), lambda k, at: (k, 0, 0))
    term_shape = pltpu.VMEM((per_half, width, cols), BF16)
    left_specs = [
        pl.BlockSpec((rank, width), lambda k, at, which=which: (jnp.clip(k - which * per_tp, 0, per_tp - 1), 0))
        for which in range(2)
    ]
    left_shapes = [shape(tp_rows, width)] * 2

    def whole_spec(*dims):
        return pl.BlockSpec(dims, lambda k, at: (0,) * len(dims))

    pieces = []
    for offset in range(tps):
        column = (tp ^ offset) * cols
        piece = lax.dynamic_slice_in_dim(master, column, cols, 1)
        pieces.append(piece - (LEARNING_RATE * MOMENTUM_DECAY) * lax.dynamic_slice_in_dim(momentum, column, cols, 1))

    terms, lefts = [None] * halves, [None] * tps
    for half in reversed(range(halves)):
        picked = functools.partial(matrix_of, half)
        high, low, *out = grid_call(
            functools.partial(first_left_kernel, per_tp, picked),
            "first_left",
            ids,
            (per_half,),
            [
                pl.BlockSpec(memory_space=pltpu.HBM),
                pl.BlockSpec(memory_space=pltpu.HBM),
                pl.BlockSpec((1, rank, cols), lambda k, at, picked=picked: (picked(k, at), 0, 0)),
            ],
            [term_spec, term_spec, *left_specs],
            [term_shape, term_shape, *left_shapes],
            (grads, error, query),
            [
                pltpu.VMEM((per_half, width, cols), BF16),
                pltpu.VMEM((per_half, width, cols), F32),
                pltpu.SemaphoreType.DMA((2, per_half)),
            ],
            mib=26,
            flops=flops,
            moved=10 * elements,
        )
        terms[half] = tuple(pltpu.with_memory_space_constraint(term, pltpu.VMEM) for term in (high, low))
        lefts[2 * half : 2 * half + 2] = out
        ids, _ = lax.optimization_barrier((ids, out[0]))

    for power_pass in range(ROUNDS):
        met = [lefts[0]] + [swap(lefts[offset], "tp", tps, offset) for offset in reversed(range(1, tps))]
        parts = whole_call(
            functools.partial(split_kernel, tps), "left_split", shape(left_part * replicas, LANES), met
        )
        if power_pass == 0:
            parts, pieces = lax.optimization_barrier((parts, pieces))
            base = [pieces[0]]
        parts = parts.reshape(replicas, left_part, LANES)
        parts = lax.all_to_all(parts, "rep", split_axis=0, concat_axis=0, tiled=True)
        parts = whole_call(total_kernel, "left_sum", shape(*parts.shape), [parts])
        parts = lax.all_to_all(parts, "rep", split_axis=0, concat_axis=0, tiled=True)
        basis = whole_call(
            functools.partial(basis_kernel, rank), "basis", shape(tp_rows, width), [parts.reshape(-1, LANES)]
        )
        across = swap(basis, "tp", tps, 2)
        bases = [basis, swap(basis, "tp", tps, 1)]
        before = grid_call(
            functools.partial(right_kernel, per_tp),
            "right_near",
            ids,
            (per_half,),
            [whole_spec(tp_rows, width), whole_spec(tp_rows, width), term_spec, term_spec],
            pl.BlockSpec((rank, cols), lambda k, at: (k, 0)),
            shape(2 * tp_rows, cols),
            (*bases, *terms[0]),
            flops=flops,
            moved=4 * elements,
        )
        before, across = lax.optimization_barrier((before, across))
        bases += [across, swap(across, "tp", tps, 1)]
        parts = grid_call(
            functools.partial(right_kernel, per_tp),
            "right_far",
            ids,
            (per_half,),
            [whole_spec(tp_rows, width), whole_spec(tp_rows, width), term_spec, term_spec, whole_spec(2 * tp_rows, cols)],
            [whole_spec(right_part, LANES)] * replicas,
            [shape(right_part, LANES)] * replicas,
            (*bases[2:], *terms[1], before),
            [pltpu.VMEM((right_part * replicas, LANES), F32), pltpu.VMEM((2 * tp_rows, cols), F32)],
            flops=flops,
            moved=4 * elements,
        )
        met = scattered(parts, replicas)
        arrived = [swap(pieces[offset], "tp", tps, offset) for offset in ((1, 2) if power_pass == 0 else range(3, tps))]
        met, pieces, arrived = lax.optimization_barrier((met, pieces, arrived))
        base += arrived
        part = whole_call(functools.partial(sum_kernel, 1.0 / replicas), "right_sum", shape(right_part, LANES), met)
        rights = spread(part, "rep", replicas)
        if power_pass < ROUNDS - 1:
            for half in reversed(range(halves)):
                lefts[2 * half : 2 * half + 2] = grid_call(
                    functools.partial(left_kernel, per_tp, half),
                    "left",
                    ids,
                    (per_half,),
                    [term_spec, term_spec] + [whole_spec(right_part, LANES)] * replicas,
                    left_specs,
                    left_shapes,
                    (*terms[half], *rights),
                    [pltpu.VMEM((right_part * replicas, LANES), F32), pltpu.VMEM((2 * tp_rows, cols), F32)],
                    flops=flops,
                    moved=10 * elements,
                )

    all_bases = jnp.concatenate(bases, axis=0)
    rep_rows = tps * own_rows
    unit = math.gcd(rep_rows, width)
    right, *block = whole_call(
        functools.partial(late_kernel, unit, per_tp, rank),
        "late_rows",
        [shape(matrices * rank, cols)] + [shape(rep_rows // 2, cols, dtype=BF16)] * 2,
        [all_bases, *rights, *base],
        ids,
        [pltpu.VMEM((right_part * replicas, LANES), F32), pltpu.VMEM((rep_rows, cols), F32)],
    )
    spans = -(-(width - unit + rep_rows) // width)
    first = jnp.minimum(rep * rep_rows // width, matrices - spans)
    near = lax.dynamic_slice_in_dim(right, first * rank, spans * rank, 0)

    def update(slot, ids, before):
        own = pl.BlockSpec((1, 1, width, cols), lambda j, at: (0, (at[1] ^ slot) * per_tp + j, 0, 0))
        return grid_call(
            functools.partial(update_kernel, rank),
            "update",
            ids,
            (per_tp,),
            [
                pl.BlockSpec((tp_rows, width), lambda j, at: (slot, 0)),
                pl.BlockSpec((tp_rows, cols), lambda j, at: (at[1] ^ slot, 0)),
                own,
                own,
            ]
            + [pl.BlockSpec(memory_space=pl.ANY)] * len(before),
            own,
            shape(*error.shape),
            (all_bases, right, grads, error, *before),
            aliases={5: 0} if before else None,
            flops=2 * 3 * rank * error.size // tps,
            moved=8 * error.size // tps,
        )

    def place(pieces, ids, before):
        count = len(pieces)

        def where(k, at):
            at_half, step = pieces[-1][1:]
            for index in range(count - 1):
                at_half = jnp.where(k == index, pieces[index][1], at_half)
                step = jnp.where(k == index, pieces[index][2], step)
            return (owner_of(step, at[0], replicas), at_half, 0, 0)

        return grid_call(
            functools.partial(place_kernel, count),
            "place",
            ids,
            (count,),
            [pl.BlockSpec((rep_rows // 2, cols), lambda k, at: (0, 0))] * count
            + [pl.BlockSpec(memory_space=pl.ANY)] * len(before),
            pl.BlockSpec((1, 1, rep_rows // 2, cols), where),
            shape(replicas, 2, rep_rows // 2, cols, dtype=BF16),
            (*[piece[0] for piece in pieces], *before),
            aliases={1 + count: 0} if before else None,
            moved=4 * count * rep_rows * cols,
        )

    def flat_rows(ids, all_bases, near):
        wide = pl.BlockSpec((own_rows, cols), lambda s, at: (0, at[1] ^ s))
        return grid_call(
            functools.partial(flat_kernel, unit, per_tp, rank, matrices),
            "flat_rows",
            ids,
            (tps,),
            [
                whole_spec(matrices * rank, width),
                pl.BlockSpec((1, spans * rank, cols), lambda s, at: (s, 0, 0)),
                wide,
                wide,
            ],
            [wide, wide],
            [shape(*momentum.shape), shape(*master.shape)],
            (all_bases, near, momentum, master),
            [pltpu.VMEM((rep_rows, cols), F32)],
            flops=2 * 3 * rank * momentum.size * tps,
            moved=16 * momentum.size,
        )

    ring = [(index, (index + 2) % replicas) for index in range(replicas)]
    stages = replicas // 2
    last = 2 * stages - 1
    held, beside = list(block), [None, None]
    pieces = [(block[half], half, 0) for half in range(2)]
    errors, flat, weights = (), (), ()
    jobs = {1: "update", 2: "update", 3: "update", 4: "update", 5: "flat place", 2 * stages - 2: "place", 2 * stages - 1: "place"}
    near = spread(near, "tp", tps)
    updated = 0
    for step in range(2 * stages):
        stage, half = step // 2, step % 2
        if stage > 0:
            arrived = (held[half], beside[half])
            ids, errors, flat, weights, near, arrived = lax.optimization_barrier((ids, errors, flat, weights, near, arrived))
            held[half], beside[half] = arrived
            pieces += [(held[half], half, stage), (beside[half], half, stages + stage - 1)]
        if stage < stages - 1:
            here = held[half]
            held[half] = lax.ppermute(here, "rep", ring)
            beside[half] = swap(here, "rep", replicas, 1)
        elif half == 0:
            beside[half] = swap(held[half], "rep", replicas, 1)
        else:
            beside[half] = lax.ppermute(beside[half], "rep", ring)
        for job in jobs.get(step, "").split():
            if job == "update":
                errors = (update(updated, ids, errors),)
                updated += 1
            elif job == "flat":
                flat = flat_rows(ids, all_bases, jnp.stack(near))
            else:
                weights = (place(pieces, ids, weights),)
                pieces = []
    weights = place([(beside[half], half, last) for half in range(2)], ids, weights).reshape(matrices, width, cols)
    (new_error,) = errors
    new_momentum, new_master = flat
    return (new_error, right.reshape(matrices, rank, cols), new_momentum, new_master, weights)


def plain_orthonormal(factor):
    def gram_of(x):
        return jnp.einsum("krd,ksd->krs", x, x, precision=HIGHEST)

    gram_now = gram_of(factor)
    factor_scale = lax.rsqrt(jnp.trace(gram_now, axis1=1, axis2=2)[:, None, None] + NORM_EPSILON)
    ortho_basis = factor * factor_scale
    gram_now = gram_now * (factor_scale * factor_scale)
    for iteration in range(NS_STEPS):
        if iteration > 0:
            gram_now = gram_of(ortho_basis)
        ortho_basis = 1.5 * ortho_basis - 0.5 * jnp.einsum("krs,ksd->krd", gram_now, ortho_basis, precision=HIGHEST)
    return ortho_basis


def plain_local(grads, error, query, momentum, master):
    corrected = grads[0].astype(F32) + error[0]
    current = query
    replicas = lax.axis_size("rep")
    for _ in range(ROUNDS):
        partial_factor = jnp.einsum("kdf,krf->krd", corrected, current, precision=HIGHEST)
        ortho_basis = plain_orthonormal(lax.psum(partial_factor, ("rep", "tp")))
        partial_query = jnp.einsum("kdf,krd->krf", corrected, ortho_basis, precision=HIGHEST)
        current = lax.psum(partial_query, "rep") / replicas
    approx = jnp.einsum("krd,krf->kdf", ortho_basis, current, precision=HIGHEST)
    new_error = (corrected - approx)[None]
    matrices, width, cols = approx.shape
    block_rows = matrices * width // replicas
    own_block = lax.dynamic_slice_in_dim(
        approx.reshape(matrices * width, cols), lax.axis_index("rep") * block_rows, block_rows, 0
    )
    flat_approx = lax.all_to_all(own_block, "tp", split_axis=0, concat_axis=1, tiled=True)
    new_momentum = MOMENTUM_DECAY * momentum + flat_approx
    new_master = master - LEARNING_RATE * new_momentum
    by_columns = lax.all_to_all(new_master.astype(BF16), "tp", split_axis=1, concat_axis=0, tiled=True)
    weights = lax.all_gather(by_columns, "rep", axis=0, tiled=True).reshape(matrices, width, cols)
    return (new_error, current, new_momentum, new_master, weights)


def divides(mesh, matrices, rank, width, cols):
    replicas, tps = mesh.shape["rep"], mesh.shape["tp"]
    if replicas & (replicas - 1) or tps != 4 or replicas < 8 or matrices % tps or cols % (tps * LANES) or width % LANES:
        return False
    if math.gcd(matrices * width // replicas, width) % LANES:
        return False
    tp_rows = matrices // tps * rank
    tiles = 8 * LANES * replicas
    return tp_rows * width % tiles == 0 and tps * tp_rows * (cols // tps) % tiles == 0


def solution(mesh):
    placed = (
        P("rep", None, None, "tp"),
        P("rep", None, None, "tp"),
        P(None, None, "tp"),
        P(("rep", "tp"), None),
        P(("rep", "tp"), None),
    )

    def step(grads, error, query, momentum, master):
        fits = divides(mesh, grads.shape[1], query.shape[1], grads.shape[2], grads.shape[3])
        return jax.shard_map(
            local if fits else plain_local,
            mesh=mesh,
            in_specs=placed,
            out_specs=(
                P("rep", None, None, "tp"),
                P(None, None, "tp"),
                P(("rep", "tp"), None),
                P(("rep", "tp"), None),
                P(None, None, "tp"),
            ),
            check_vma=False,
        )(grads, error, query, momentum, master)

    return step
```

```python
import functools
import math

import jax
import jax.numpy as jnp
from jax import lax
from jax.experimental import pallas as pl
from jax.experimental.pallas import tpu as pltpu
from jax.sharding import PartitionSpec as P

ROUNDS = 2
NS_STEPS = 5


NORM_EPSILON = 1e-06
MOMENTUM_DECAY = 0.9
LEARNING_RATE = 0.5
HIGHEST = lax.Precision.HIGHEST
LANES = 128
F32, BF16 = jnp.float32, jnp.bfloat16
SCALARS = pl.BlockSpec(memory_space=pltpu.SMEM)


def two_terms(x):
    high = x.astype(BF16)
    return high, (x - high.astype(F32)).astype(BF16)


def dot(a, b, transposed=False):
    dims = (((1,), (1 if transposed else 0,)), ((), ()))
    return lax.dot_general(a, b, dims, preferred_element_type=F32)


def small_by_large(small, high, low, transposed):
    rows = small.shape[0]
    small_high, small_low = two_terms(small)
    both = dot(jnp.concatenate([small_high, small_low], axis=0), high, transposed)
    return both[:rows] + both[rows:] + dot(small_high, low, transposed)


def dot3(a, b):
    a_high, a_low = two_terms(a)
    b_high, b_low = two_terms(b)
    return dot(
        jnp.concatenate([a_high, a_low, a_high], axis=1),
        jnp.concatenate([b_high, b_high, b_low], axis=0),
    )


def stacked(right):
    right_high, right_low = two_terms(right)
    return jnp.concatenate([right_high, right_high, right_low], axis=0)


def lay_lanes(scratch, value):
    rows = value.shape[0]
    for block in range(value.shape[1] // LANES):
        scratch[block * rows : (block + 1) * rows] = value[:, block * LANES : (block + 1) * LANES]


def read_lanes(scratch, rows):
    blocks = scratch.shape[0] // rows
    return jnp.concatenate([scratch[block * rows : (block + 1) * rows] for block in range(blocks)], axis=1)


def part_at(index, rows):
    return pl.ds(pl.multiple_of(index * rows, 8), rows)


def split_parts(scratch, me, part_refs):
    rows = part_refs[0].shape[0]
    for offset, part_ref in enumerate(part_refs):
        part_ref[...] = scratch[part_at(me ^ offset, rows), :]


def join_parts(scratch, me, part_refs):
    rows = part_refs[0].shape[0]
    for offset, part_ref in enumerate(part_refs):
        scratch[part_at(me ^ offset, rows), :] = part_ref[...]


def sum_of(refs):
    values = [ref[...] for ref in refs]
    while len(values) > 1:
        values = [sum(values[at : at + 2][1:], values[at]) for at in range(0, len(values), 2)]
    return values[0]


def put_left(left, step, left_refs, per_tp):
    for which, left_ref in enumerate(left_refs):

        @pl.when(step // per_tp == which)
        def _():
            left_ref[...] = left


def first_left_kernel(per_tp, picked, ids_ref, grads_ref, error_ref, query_ref, high_ref, low_ref, *refs):
    left_refs, (grads_buffer, error_buffer, sems) = refs[:-3], refs[-3:]
    step = pl.program_id(0)

    def copies(k):
        matrix = picked(k, ids_ref)
        return [
            pltpu.make_async_copy(source.at[0, matrix], buffer.at[k], sems.at[which, k])
            for which, (source, buffer) in enumerate(((grads_ref, grads_buffer), (error_ref, error_buffer)))
        ]

    @pl.when(step == 0)
    def _():
        for k in range(grads_buffer.shape[0]):
            for copy in copies(k):
                copy.start()

    for copy in copies(step):
        copy.wait()
    high, low = two_terms(grads_buffer[step].astype(F32) + error_buffer[step])
    high_ref[0] = high
    low_ref[0] = low
    put_left(small_by_large(query_ref[0], high, low, True), step, left_refs, per_tp)


def left_kernel(per_tp, half, ids_ref, high_ref, low_ref, *refs):
    parts, left_refs, (scratch, current) = refs[:-4], refs[-4:-2], refs[-2:]
    step = pl.program_id(0)
    rank = left_refs[0].shape[0]
    rows = current.shape[0]
    lanes = rows * (current.shape[1] // LANES)

    @pl.when(step == 0)
    def _():
        join_parts(scratch, ids_ref[0], parts)
        current[...] = read_lanes(scratch.at[half * lanes : (half + 1) * lanes], rows)

    own = current[part_at(step, rank), :]
    put_left(small_by_large(own, high_ref[0], low_ref[0], True), step, left_refs, per_tp)


def split_kernel(tps, *refs):
    lay_lanes(refs[-1], sum_of(refs[:tps]))


def total_kernel(parts_ref, out_ref):
    summed = sum_of([parts_ref.at[part] for part in range(parts_ref.shape[0])])
    for part in range(parts_ref.shape[0]):
        out_ref[part] = summed


def sum_kernel(scale, *refs):
    summed = sum_of(refs[:-1])
    refs[-1][...] = summed if scale == 1.0 else summed * scale


def mixing(left, rank):
    rows = left.shape[0]
    row_id = lax.broadcasted_iota(jnp.int32, (rows, rows), 0)
    col_id = lax.broadcasted_iota(jnp.int32, (rows, rows), 1)
    same = (row_id // rank) == (col_id // rank)
    eye = (row_id == col_id).astype(F32)
    left_high, left_low = two_terms(left)
    cross = dot(left_high, left_low, True)
    gram = jnp.where(same, dot(left_high, left_high, True) + cross + cross.T, 0.0)
    diagonal = jnp.sum(gram * eye, axis=0, keepdims=True)
    trace = jnp.sum(jnp.where(same, diagonal, 0.0), axis=1, keepdims=True) + NORM_EPSILON
    scale = lax.rsqrt(trace)
    scale = scale * (1.5 - 0.5 * trace * scale * scale)
    gram = gram * (scale * scale)
    step = 1.5 * eye - 0.5 * gram
    mixed = step * scale
    for _ in range(NS_STEPS - 1):
        gram = dot3(dot3(step, gram), step)
        step = 1.5 * eye - 0.5 * gram
        mixed = dot3(step, mixed)
    return mixed


def basis_kernel(rank, left_ref, basis_ref):
    rows = basis_ref.shape[0]
    left = read_lanes(left_ref, rows)
    padded = jnp.concatenate([left, jnp.zeros((-rows % LANES, left.shape[1]), F32)], axis=0)
    basis_ref[...] = dot3(mixing(padded, rank), padded)[:rows]


def right_kernel(per_tp, ids_ref, first_ref, second_ref, high_ref, low_ref, *refs):
    step = pl.program_id(0)
    rank = first_ref.shape[0] // per_tp
    at = part_at(step % per_tp, rank)
    own = jnp.where(step // per_tp == 0, first_ref[at, :], second_ref[at, :])
    product_now = small_by_large(own, high_ref[0], low_ref[0], False)
    if len(refs) == 1:
        refs[0][...] = product_now
        return
    before_ref, part_refs, (scratch, right) = refs[0], refs[1:-2], refs[-2:]
    right[part_at(step, rank), :] = product_now

    @pl.when(step == pl.num_programs(0) - 1)
    def _():
        lanes = scratch.shape[0] // 2
        lay_lanes(scratch.at[:lanes], before_ref[...])
        lay_lanes(scratch.at[lanes:], right[...])
        split_parts(scratch, ids_ref[0], part_refs)


def rows_of_update(basis_ref, right_ref, scratch, first_unit, unit, per_tp, rank, tp, first_matrix):
    per_matrix = basis_ref.shape[1] // unit
    for u in range(scratch.shape[0] // unit):
        at = first_unit + u
        matrix = at // per_matrix
        slot = ((matrix // per_tp) ^ tp) * per_tp + matrix % per_tp
        lanes = pl.ds(pl.multiple_of((at % per_matrix) * unit, LANES), unit)
        factor = basis_ref[part_at(slot, rank), lanes]
        right = right_ref[part_at(matrix - first_matrix, rank), :]
        scratch[u * unit : (u + 1) * unit] = product(factor, right)


def product(factor, right):
    high, low = two_terms(factor.T)
    return dot(jnp.concatenate([high, low, high], axis=1), stacked(right))


def late_kernel(unit, per_tp, rank, ids_ref, basis_ref, *refs):
    query_ref, *weight_refs, lanes, approx = refs[-5:]
    tps = query_ref.shape[0] // (per_tp * rank)
    part_refs, base_refs = refs[: -5 - tps], refs[-5 - tps : -5]
    rows = query_ref.shape[0] // 2
    tp = ids_ref[1]
    join_parts(lanes, ids_ref[0], part_refs)
    for half in range(2):
        per_half = lanes.shape[0] // 2
        value = read_lanes(lanes.at[half * per_half : (half + 1) * per_half], rows)
        for which in range(2):
            owner = tp ^ (2 * half + which)
            query_ref[part_at(owner, rows // 2), :] = value[which * (rows // 2) : (which + 1) * (rows // 2)]
    units = approx.shape[0] // unit
    rows_of_update(basis_ref, query_ref, approx, ids_ref[0] * units, unit, per_tp, rank, tp, 0)
    for offset, base_ref in enumerate(base_refs):
        at = part_at(tp ^ offset, base_ref.shape[0])
        approx[at, :] = base_ref[...] - LEARNING_RATE * approx[at, :]
    for half, weight_ref in enumerate(weight_refs):
        per_half = weight_ref.shape[0]
        weight_ref[...] = approx[half * per_half : (half + 1) * per_half].astype(BF16)


def owner_of(step, rep, replicas):
    half = replicas // 2
    return ((rep ^ (step // half)) + 2 * replicas - 2 * (step % half)) % replicas


def place_kernel(count, ids_ref, *refs):
    for at, part_ref in enumerate(refs[:count]):

        @pl.when(pl.program_id(0) == at)
        def _():
            refs[-1][0, 0] = part_ref[...]


def update_kernel(rank, ids_ref, basis_ref, right_ref, high_ref, low_ref, *refs):
    at = part_at(pl.program_id(0), rank)
    approx = product(basis_ref[at, :], right_ref[at, :])
    refs[-1][0, 0] = high_ref[0].astype(F32) + low_ref[0].astype(F32) - approx


def flat_kernel(unit, per_tp, rank, matrices, ids_ref, basis_ref, near_ref, momentum_ref, master_ref, new_momentum_ref, new_master_ref, approx):
    units = approx.shape[0] // unit
    spans = near_ref.shape[1] // rank
    first_unit = ids_ref[0] * units
    first = jnp.minimum(first_unit // (basis_ref.shape[1] // unit), matrices - spans)
    rows_of_update(basis_ref, near_ref.at[0], approx, first_unit, unit, per_tp, rank, ids_ref[1], first)
    own = approx[part_at(ids_ref[1], momentum_ref.shape[0]), :]
    new_momentum = MOMENTUM_DECAY * momentum_ref[...] + own
    new_momentum_ref[...] = new_momentum
    new_master_ref[...] = master_ref[...] - LEARNING_RATE * new_momentum


def shape(*dims, dtype=F32):
    return jax.ShapeDtypeStruct(dims, dtype)


def grant(mib):
    return pltpu.CompilerParams(vmem_limit_bytes=mib * 2**20)


def whole_call(kernel, name, out_shape, operands, ids=None, scratch=()):
    specs = [pl.BlockSpec(memory_space=pltpu.VMEM)] * len(operands)
    many = isinstance(out_shape, (list, tuple))
    out_spec = pl.BlockSpec(memory_space=pltpu.VMEM)
    moved = sum(4 * x.size for x in operands)
    if ids is not None:
        operands, specs = [ids, *operands], [SCALARS, *specs]
    return pl.pallas_call(
        kernel,
        in_specs=specs,
        out_specs=[out_spec] * len(out_shape) if many else out_spec,
        out_shape=out_shape,
        scratch_shapes=list(scratch),
        compiler_params=grant(12),
        name=name,
        cost_estimate=pl.CostEstimate(flops=moved, bytes_accessed=2 * moved, transcendentals=0),
    )(*operands)


def grid_call(kernel, name, ids, grid, in_specs, out_specs, out_shape, operands, scratch=(), aliases=None, flops=0, moved=0, mib=14):
    return pl.pallas_call(
        kernel,
        grid_spec=pltpu.PrefetchScalarGridSpec(
            num_scalar_prefetch=1,
            grid=grid,
            in_specs=in_specs,
            out_specs=out_specs,
            scratch_shapes=list(scratch),
        ),
        out_shape=out_shape,
        input_output_aliases=aliases or {},
        compiler_params=grant(mib),
        name=name,
        cost_estimate=pl.CostEstimate(flops=flops, bytes_accessed=moved, transcendentals=0),
    )(ids, *operands)


def swap(x, axis, size, offset):
    return lax.ppermute(x, axis, [(index, index ^ offset) for index in range(size)])


def scattered(parts, replicas):
    return [parts[0]] + [swap(parts[offset], "rep", replicas, offset) for offset in range(1, replicas)]


def spread(part, axis, size):
    return [part] + [swap(part, axis, size, offset) for offset in range(1, size)]


def local(grads, error, query, momentum, master):
    replicas, tps = lax.axis_size("rep"), lax.axis_size("tp")
    rep, tp = lax.axis_index("rep"), lax.axis_index("tp")
    ids = jnp.stack([rep, tp]).astype(jnp.int32)
    _, matrices, width, cols = grads.shape
    rank = query.shape[1]
    per_tp = matrices // tps
    per_half = 2 * per_tp
    halves = tps // 2
    tp_rows = per_tp * rank
    left_part = tp_rows * width // LANES // replicas
    right_part = tps * tp_rows * cols // LANES // replicas
    own_rows = momentum.shape[0]
    flops = 2 * 3 * per_half * rank * width * cols
    elements = per_half * width * cols

    def matrix_of(half, k, at):
        return (at[1] ^ (2 * half + k // per_tp)) * per_tp + k % per_tp

    term_spec = pl.BlockSpec((1, width, cols), lambda k, at: (k, 0, 0))
    term_shape = pltpu.VMEM((per_half, width, cols), BF16)
    left_specs = [
        pl.BlockSpec((rank, width), lambda k, at, which=which: (jnp.clip(k - which * per_tp, 0, per_tp - 1), 0))
        for which in range(2)
    ]
    left_shapes = [shape(tp_rows, width)] * 2

    def whole_spec(*dims):
        return pl.BlockSpec(dims, lambda k, at: (0,) * len(dims))

    pieces = []
    for offset in range(tps):
        column = (tp ^ offset) * cols
        piece = lax.dynamic_slice_in_dim(master, column, cols, 1)
        pieces.append(piece - (LEARNING_RATE * MOMENTUM_DECAY) * lax.dynamic_slice_in_dim(momentum, column, cols, 1))

    terms, lefts = [None] * halves, [None] * tps
    for half in reversed(range(halves)):
        picked = functools.partial(matrix_of, half)
        high, low, *out = grid_call(
            functools.partial(first_left_kernel, per_tp, picked),
            "first_left",
            ids,
            (per_half,),
            [
                pl.BlockSpec(memory_space=pltpu.HBM),
                pl.BlockSpec(memory_space=pltpu.HBM),
                pl.BlockSpec((1, rank, cols), lambda k, at, picked=picked: (picked(k, at), 0, 0)),
            ],
            [term_spec, term_spec, *left_specs],
            [term_shape, term_shape, *left_shapes],
            (*(pltpu.with_memory_space_constraint(x, pltpu.HBM) for x in (grads, error)), query),
            [
                pltpu.VMEM((per_half, width, cols), BF16),
                pltpu.VMEM((per_half, width, cols), F32),
                pltpu.SemaphoreType.DMA((2, per_half)),
            ],
            mib=26,
            flops=flops,
            moved=10 * elements,
        )
        terms[half] = tuple(pltpu.with_memory_space_constraint(term, pltpu.VMEM) for term in (high, low))
        lefts[2 * half : 2 * half + 2] = out
        ids, _ = lax.optimization_barrier((ids, out[0]))

    for power_pass in range(ROUNDS):
        met = [lefts[0]] + [swap(lefts[offset], "tp", tps, offset) for offset in reversed(range(1, tps))]
        parts = whole_call(
            functools.partial(split_kernel, tps), "left_split", shape(left_part * replicas, LANES), met
        )
        if power_pass == 0:
            parts, pieces = lax.optimization_barrier((parts, pieces))
            base = [pieces[0]]
        parts = parts.reshape(replicas, left_part, LANES)
        parts = lax.all_to_all(parts, "rep", split_axis=0, concat_axis=0, tiled=True)
        parts = whole_call(total_kernel, "left_sum", shape(*parts.shape), [parts])
        parts = lax.all_to_all(parts, "rep", split_axis=0, concat_axis=0, tiled=True)
        basis = whole_call(
            functools.partial(basis_kernel, rank), "basis", shape(tp_rows, width), [parts.reshape(-1, LANES)]
        )
        across = swap(basis, "tp", tps, 2)
        bases = [basis, swap(basis, "tp", tps, 1)]
        before = grid_call(
            functools.partial(right_kernel, per_tp),
            "right_near",
            ids,
            (per_half,),
            [whole_spec(tp_rows, width), whole_spec(tp_rows, width), term_spec, term_spec],
            pl.BlockSpec((rank, cols), lambda k, at: (k, 0)),
            shape(2 * tp_rows, cols),
            (*bases, *terms[0]),
            flops=flops,
            moved=4 * elements,
        )
        before, across = lax.optimization_barrier((before, across))
        bases += [across, swap(across, "tp", tps, 1)]
        parts = grid_call(
            functools.partial(right_kernel, per_tp),
            "right_far",
            ids,
            (per_half,),
            [whole_spec(tp_rows, width), whole_spec(tp_rows, width), term_spec, term_spec, whole_spec(2 * tp_rows, cols)],
            [whole_spec(right_part, LANES)] * replicas,
            [shape(right_part, LANES)] * replicas,
            (*bases[2:], *terms[1], before),
            [pltpu.VMEM((right_part * replicas, LANES), F32), pltpu.VMEM((2 * tp_rows, cols), F32)],
            flops=flops,
            moved=4 * elements,
        )
        met = scattered(parts, replicas)
        arrived = [swap(pieces[offset], "tp", tps, offset) for offset in ((1, 2) if power_pass == 0 else range(3, tps))]
        met, pieces, arrived = lax.optimization_barrier((met, pieces, arrived))
        base += arrived
        part = whole_call(functools.partial(sum_kernel, 1.0 / replicas), "right_sum", shape(right_part, LANES), met)
        rights = spread(part, "rep", replicas)
        if power_pass < ROUNDS - 1:
            for half in reversed(range(halves)):
                lefts[2 * half : 2 * half + 2] = grid_call(
                    functools.partial(left_kernel, per_tp, half),
                    "left",
                    ids,
                    (per_half,),
                    [term_spec, term_spec] + [whole_spec(right_part, LANES)] * replicas,
                    left_specs,
                    left_shapes,
                    (*terms[half], *rights),
                    [pltpu.VMEM((right_part * replicas, LANES), F32), pltpu.VMEM((2 * tp_rows, cols), F32)],
                    flops=flops,
                    moved=10 * elements,
                )

    all_bases = jnp.concatenate(bases, axis=0)
    rep_rows = tps * own_rows
    unit = math.gcd(rep_rows, width)
    right, *block = whole_call(
        functools.partial(late_kernel, unit, per_tp, rank),
        "late_rows",
        [shape(matrices * rank, cols)] + [shape(rep_rows // 2, cols, dtype=BF16)] * 2,
        [all_bases, *rights, *base],
        ids,
        [pltpu.VMEM((right_part * replicas, LANES), F32), pltpu.VMEM((rep_rows, cols), F32)],
    )
    spans = -(-(width - unit + rep_rows) // width)
    first = jnp.minimum(rep * rep_rows // width, matrices - spans)
    near = lax.dynamic_slice_in_dim(right, first * rank, spans * rank, 0)

    def update(slot, ids, before):
        half, start = slot // 2, slot % 2 * per_tp
        return grid_call(
            functools.partial(update_kernel, rank),
            "update",
            ids,
            (per_tp,),
            [
                pl.BlockSpec((tp_rows, width), lambda j, at: (slot, 0)),
                pl.BlockSpec((tp_rows, cols), lambda j, at: (at[1] ^ slot, 0)),
                pl.BlockSpec((1, width, cols), lambda j, at: (start + j, 0, 0)),
                pl.BlockSpec((1, width, cols), lambda j, at: (start + j, 0, 0)),
            ]
            + [pl.BlockSpec(memory_space=pl.ANY)] * len(before),
            pl.BlockSpec((1, 1, width, cols), lambda j, at: (0, (at[1] ^ slot) * per_tp + j, 0, 0)),
            shape(*error.shape),
            (all_bases, right, *terms[half], *before),
            aliases={5: 0} if before else None,
            flops=2 * 3 * rank * error.size // tps,
            moved=8 * error.size // tps,
        )

    def place(pieces, ids, before):
        count = len(pieces)

        def where(k, at):
            at_half, step = pieces[-1][1:]
            for index in range(count - 1):
                at_half = jnp.where(k == index, pieces[index][1], at_half)
                step = jnp.where(k == index, pieces[index][2], step)
            return (owner_of(step, at[0], replicas), at_half, 0, 0)

        return grid_call(
            functools.partial(place_kernel, count),
            "place",
            ids,
            (count,),
            [pl.BlockSpec((rep_rows // 2, cols), lambda k, at: (0, 0))] * count
            + [pl.BlockSpec(memory_space=pl.ANY)] * len(before),
            pl.BlockSpec((1, 1, rep_rows // 2, cols), where),
            shape(replicas, 2, rep_rows // 2, cols, dtype=BF16),
            (*[piece[0] for piece in pieces], *before),
            aliases={1 + count: 0} if before else None,
            moved=4 * count * rep_rows * cols,
        )

    def flat_rows(ids, all_bases, near):
        wide = pl.BlockSpec((own_rows, cols), lambda s, at: (0, at[1] ^ s))
        return grid_call(
            functools.partial(flat_kernel, unit, per_tp, rank, matrices),
            "flat_rows",
            ids,
            (tps,),
            [
                whole_spec(matrices * rank, width),
                pl.BlockSpec((1, spans * rank, cols), lambda s, at: (s, 0, 0)),
                wide,
                wide,
            ],
            [wide, wide],
            [shape(*momentum.shape), shape(*master.shape)],
            (all_bases, near, momentum, master),
            [pltpu.VMEM((rep_rows, cols), F32)],
            flops=2 * 3 * rank * momentum.size * tps,
            moved=16 * momentum.size,
        )

    ring = [(index, (index + 2) % replicas) for index in range(replicas)]
    stages = replicas // 2
    last = 2 * stages - 1
    held, beside = list(block), [None, None]
    pieces = [(block[half], half, 0) for half in range(2)]
    errors, flat, weights = (), (), ()
    jobs = {2: "update", 3: "update update", 4: "update", 5: "flat place", 2 * stages - 2: "place", 2 * stages - 1: "place"}
    near = spread(near, "tp", tps)
    updated = 0
    for step in range(2 * stages):
        stage, half = step // 2, step % 2
        if stage > 0:
            arrived = (held[half], beside[half])
            ids, errors, flat, weights, near, arrived = lax.optimization_barrier((ids, errors, flat, weights, near, arrived))
            held[half], beside[half] = arrived
            pieces += [(held[half], half, stage), (beside[half], half, stages + stage - 1)]
        if stage < stages - 1:
            here = held[half]
            held[half] = lax.ppermute(here, "rep", ring)
            beside[half] = swap(here, "rep", replicas, 1)
        elif half == 0:
            beside[half] = swap(held[half], "rep", replicas, 1)
        else:
            beside[half] = lax.ppermute(beside[half], "rep", ring)
        for job in jobs.get(step, "").split():
            if job == "update":
                errors = (update(updated, ids, errors),)
                updated += 1
            elif job == "flat":
                flat = flat_rows(ids, all_bases, jnp.stack(near))
            else:
                weights = (place(pieces, ids, weights),)
                pieces = []
    weights = place([(beside[half], half, last) for half in range(2)], ids, weights).reshape(matrices, width, cols)
    (new_error,) = errors
    new_momentum, new_master = flat
    return (new_error, right.reshape(matrices, rank, cols), new_momentum, new_master, weights)


def plain_orthonormal(factor):
    def gram_of(x):
        return jnp.einsum("krd,ksd->krs", x, x, precision=HIGHEST)

    gram_now = gram_of(factor)
    factor_scale = lax.rsqrt(jnp.trace(gram_now, axis1=1, axis2=2)[:, None, None] + NORM_EPSILON)
    ortho_basis = factor * factor_scale
    gram_now = gram_now * (factor_scale * factor_scale)
    for iteration in range(NS_STEPS):
        if iteration > 0:
            gram_now = gram_of(ortho_basis)
        ortho_basis = 1.5 * ortho_basis - 0.5 * jnp.einsum("krs,ksd->krd", gram_now, ortho_basis, precision=HIGHEST)
    return ortho_basis


def plain_local(grads, error, query, momentum, master):
    corrected = grads[0].astype(F32) + error[0]
    current = query
    replicas = lax.axis_size("rep")
    for _ in range(ROUNDS):
        partial_factor = jnp.einsum("kdf,krf->krd", corrected, current, precision=HIGHEST)
        ortho_basis = plain_orthonormal(lax.psum(partial_factor, ("rep", "tp")))
        partial_query = jnp.einsum("kdf,krd->krf", corrected, ortho_basis, precision=HIGHEST)
        current = lax.psum(partial_query, "rep") / replicas
    approx = jnp.einsum("krd,krf->kdf", ortho_basis, current, precision=HIGHEST)
    new_error = (corrected - approx)[None]
    matrices, width, cols = approx.shape
    block_rows = matrices * width // replicas
    own_block = lax.dynamic_slice_in_dim(
        approx.reshape(matrices * width, cols), lax.axis_index("rep") * block_rows, block_rows, 0
    )
    flat_approx = lax.all_to_all(own_block, "tp", split_axis=0, concat_axis=1, tiled=True)
    new_momentum = MOMENTUM_DECAY * momentum + flat_approx
    new_master = master - LEARNING_RATE * new_momentum
    by_columns = lax.all_to_all(new_master.astype(BF16), "tp", split_axis=1, concat_axis=0, tiled=True)
    weights = lax.all_gather(by_columns, "rep", axis=0, tiled=True).reshape(matrices, width, cols)
    return (new_error, current, new_momentum, new_master, weights)


def divides(mesh, matrices, rank, width, cols):
    replicas, tps = mesh.shape["rep"], mesh.shape["tp"]
    if replicas & (replicas - 1) or tps != 4 or replicas < 8 or matrices % tps or cols % (tps * LANES) or width % LANES:
        return False
    if math.gcd(matrices * width // replicas, width) % LANES:
        return False
    tp_rows = matrices // tps * rank
    tiles = 8 * LANES * replicas
    return tp_rows * width % tiles == 0 and tps * tp_rows * (cols // tps) % tiles == 0


def solution(mesh):
    placed = (
        P("rep", None, None, "tp"),
        P("rep", None, None, "tp"),
        P(None, None, "tp"),
        P(("rep", "tp"), None),
        P(("rep", "tp"), None),
    )

    def step(grads, error, query, momentum, master):
        fits = divides(mesh, grads.shape[1], query.shape[1], grads.shape[2], grads.shape[3])
        return jax.shard_map(
            local if fits else plain_local,
            mesh=mesh,
            in_specs=placed,
            out_specs=(
                P("rep", None, None, "tp"),
                P(None, None, "tp"),
                P(("rep", "tp"), None),
                P(("rep", "tp"), None),
                P(None, None, "tp"),
            ),
            check_vma=False,
        )(grads, error, query, momentum, master)

    return step
```
